32 devices in a mesh: section: 2 (over core), dp: 4 (over y, x), tensor: 4 (over z).
Axes of the slice: x: 2, y: 2, z: 4, core: 2. Of those that a mesh axis runs over, the one named last changes fastest.
Arguments:
- layer_input_activations: bfloat16 [4, 128, 2048], P(None, ('dp', 'tensor')), may hold values from -6 to 6
- cotangent: bfloat16 [4, 128, 2048], P(None, ('dp', 'tensor')), may hold values from -0.59765625 to 0.59765625
- domain_ids: int32 [4, 4], P(None, 'dp'), may hold values from 0 to 3
- norm_gain: float32 [2, 2048], P('section'), may hold values from 0.5 to 1.5
- w_gate: bfloat16 [2, 2048, 7168], P('section', None, 'tensor'), may hold values from -0.125 to 0.125
- w_up: bfloat16 [2, 2048, 7168], P('section', None, 'tensor'), may hold values from -0.125 to 0.125
- w_down: bfloat16 [2, 7168, 2048], P('section', 'tensor'), may hold values from -0.0625 to 0.0625
Outputs:
- domain_grads: bfloat16 [2, 4, 7168, 2048], P('section', None, 'tensor', 'dp')
- level_norms: float32 [4, 3], replicated
The draws below stay inside these ranges and needn't reach their ends.
All inputs are finite; a program needn't handle non-finite values.
Results may differ from the reference program's by a relative error of at most 0.01.
Values may be sent and summed in bfloat16 or wider, within the bound.
No kernel may reach another device: no remote copies, remote signals or barrier semaphores. Data moves between devices by JAX's collectives and lax.ppermute only.
A program may use at most 256 MiB of HBM per device.

```python
import jax
import jax.numpy as jnp
from jax import lax

D = 2048
FF = 7168
TOK_MB = 32
MICRO = 4
DOMAINS = 4
SECTIONS = 2
ROWS = 128
LEVELS = 3
N_DP = 4


def touch_ends(result, own_key, low, largest):
    longest = result.shape.index(max(result.shape))
    spots = []
    for shift in (0, 1):
        where = [jax.random.randint(jax.random.fold_in(own_key, axis), (), 0, length) for axis, length in enumerate(result.shape)]
        where[longest] = (where[longest] + shift) % result.shape[longest]
        spots.append(tuple(where))
    return result.at[spots[0]].set(low).at[spots[1]].set(largest)


def block_levels(rng, shape, pieces, smallest, high):
    def one(dim, blocks):
        draws = jax.random.uniform(jax.random.fold_in(jax.random.fold_in(rng, 6), dim), (blocks,), jnp.float32, smallest / len(pieces), high / len(pieces))
        return jnp.repeat(jnp.exp(draws), shape[dim] // blocks).reshape((-1,) + (1,) * (len(shape) - dim - 1))

    factor_of = one(*pieces[0])
    for cut in pieces[1:]:
        factor_of = factor_of * one(*cut)
    return factor_of


def normal_values(own_key, extent, deviation, limit, shards=(), dtype=jnp.bfloat16):
    values = jax.random.normal(own_key, extent, jnp.float32) * deviation
    if len(shards) > 0:
        values = block_levels(own_key, extent, shards, -0.22, 0.18) * values
    return jnp.clip(values, min=-limit, max=limit).astype(dtype)


def setup_inputs(seed: int = 0) -> dict:
    keys = jax.random.split(jax.random.key(seed), 8)
    return {
        "layer_input_activations": normal_values(keys[0], (MICRO, ROWS, D), 1.0, 6.0, ((1, 16),)),
        "cotangent": normal_values(keys[1], (MICRO, ROWS, D), 0.1, 0.59765625, ((1, 16),)),
        "domain_ids": touch_ends(jax.random.randint(keys[2], (MICRO, N_DP), 0, DOMAINS), jax.random.fold_in(keys[2], 1), 0, DOMAINS - 1).astype(jnp.int32),
        "norm_gain": jnp.clip(1.0 + 0.1 * jax.random.normal(keys[3], (SECTIONS, D), jnp.float32), 0.5, 1.5),
        "w_gate": normal_values(keys[4], (SECTIONS, D, FF), D ** -0.5, 0.125, ((0, 2), (2, 4))),
        "w_up": normal_values(keys[5], (SECTIONS, D, FF), D ** -0.5, 0.125, ((0, 2), (2, 4))),
        "w_down": normal_values(keys[6], (SECTIONS, FF, D), FF ** -0.5, 0.0625, ((0, 2), (1, 4))),
    }


def rms_norm(values, gain):
    widened = values.astype(jnp.float32)
    scale_inv = lax.rsqrt(lax.optimization_barrier(jnp.mean(widened * widened, axis=-1, keepdims=True)) + 1e-05)
    return widened * scale_inv * gain

def layer_parts(rows, gain, w_gate_s, w_up_s):
    normed = rms_norm(rows, gain).astype(jnp.bfloat16)
    gate = jnp.dot(normed, w_gate_s, preferred_element_type=jnp.float32)
    up_vals = jnp.dot(normed, w_up_s, preferred_element_type=jnp.float32)
    hidden = (jax.nn.silu(gate) * up_vals).astype(jnp.bfloat16)
    return (gate, up_vals, hidden)

def reference(layer_input_activations, cotangent, domain_ids, norm_gain, w_gate, w_up, w_down):
    current = layer_input_activations.reshape(MICRO * ROWS, D)
    saved_inputs = []
    for segment_num in range(SECTIONS):
        saved_inputs.append(current)
        gate, up_vals, hidden = layer_parts(current, norm_gain[segment_num], w_gate[segment_num], w_up[segment_num])
        mixed = jnp.dot(hidden, w_down[segment_num], preferred_element_type=jnp.float32)
        current = (current.astype(jnp.float32) + mixed).astype(jnp.bfloat16)
    onehot = (domain_ids[:, :, None] == jnp.arange(DOMAINS)[None, None, :]).astype(jnp.float32)
    upstream = cotangent.reshape(MICRO * ROWS, D)
    grads = [None] * SECTIONS
    squared_entries = [jnp.zeros((DOMAINS,), jnp.float32) for level in range(LEVELS)]
    for segment_num in reversed(range(SECTIONS)):
        rows_in = saved_inputs[segment_num]
        gain = norm_gain[segment_num]
        gate, up_vals, hidden = layer_parts(rows_in, gain, w_gate[segment_num], w_up[segment_num])
        hidden_rep = hidden.reshape(MICRO, N_DP, TOK_MB, FF)
        upstream_rep = upstream.reshape(MICRO, N_DP, TOK_MB, D)
        per_rep = []
        for replica in range(N_DP):
            product = jnp.einsum('mtf,mtc->mfc', hidden_rep[:, replica].astype(jnp.float32), upstream_rep[:, replica].astype(jnp.float32), precision=lax.Precision.HIGHEST)
            per_rep.append(jnp.einsum('me,mfc->efc', onehot[:, replica], product, precision=lax.Precision.HIGHEST).astype(jnp.bfloat16))
        blocks = jnp.stack(per_rep)
        squared_entries[0] = squared_entries[0] + lax.optimization_barrier(jnp.sum(jnp.square(blocks.astype(jnp.float32)), axis=(0, 2, 3)))
        for level in range(1, LEVELS):
            widened = blocks.astype(jnp.float32)
            blocks = (widened[0::2] + widened[1::2]).astype(jnp.bfloat16)
            squared_entries[level] = squared_entries[level] + lax.optimization_barrier(jnp.sum(jnp.square(blocks.astype(jnp.float32)), axis=(0, 2, 3)))
        grads[segment_num] = blocks[0]
        d_hidden = jnp.dot(upstream, w_down[segment_num].T, preferred_element_type=jnp.float32)
        sig = jax.nn.sigmoid(gate)
        d_gate = (d_hidden * up_vals * (sig * (1.0 + gate * (1.0 - sig)))).astype(jnp.bfloat16)
        d_up = (d_hidden * gate * sig).astype(jnp.bfloat16)
        d_normed = jnp.dot(d_gate, w_gate[segment_num].T, preferred_element_type=jnp.float32)
        d_normed = d_normed + jnp.dot(d_up, w_up[segment_num].T, preferred_element_type=jnp.float32)
        unused, pull = jax.vjp(lambda values: rms_norm(values, gain), rows_in.astype(jnp.float32))
        upstream = (upstream.astype(jnp.float32) + pull(d_normed)[0]).astype(jnp.bfloat16)
    entries = SECTIONS * FF * D
    columns = [squared_entries[level] / float((N_DP >> level) * entries) for level in range(LEVELS)]
    return (jnp.stack(grads), jnp.stack(columns, axis=1))
```

```python
import functools

import jax
import jax.numpy as jnp
from jax import lax
from jax.experimental import pallas as pl
from jax.experimental.pallas import tpu as pltpu
from jax.sharding import PartitionSpec as P

DOMAINS = 4
EPS = 1e-05
CONTRACT_LAST = (((1,), (1,)), ((), ()))
CONTRACT_FIRST = (((0,), (0,)), ((), ()))


def swap(block, axis, offset):
    size = lax.axis_size(axis)
    return lax.ppermute(block, axis, [(i, i ^ offset) for i in range(size)])


def across(block, source, offset):
    size = lax.axis_size("tensor")
    route = [
        (source * size + i, (1 - source) * size + (i ^ offset)) for i in range(size)
    ]
    return lax.ppermute(block, ("section", "tensor"), route)


def gather_relative(block, axis):
    return [block] + [swap(block, axis, k) for k in range(1, lax.axis_size(axis))]


def gradient_kernel(ids_ref, hidden_ref, y_ref, out_ref, masked):
    piece = y_ref.shape[1]

    @pl.when(pl.program_id(0) == 0)
    def _():
        for e in range(DOMAINS):
            keep = ids_ref[...] == e
            masked[:, e * piece : (e + 1) * piece] = jnp.where(
                keep, y_ref[...].astype(jnp.float32), 0.0
            ).astype(jnp.bfloat16)

    product = lax.dot_general(
        hidden_ref[...], masked[...], CONTRACT_FIRST, preferred_element_type=jnp.float32
    )
    for e in range(DOMAINS):
        out_ref[e] = product[:, e * piece : (e + 1) * piece].astype(jnp.bfloat16)


def domain_gradients(row_ids, hidden, y):
    rows, units = hidden.shape
    piece = y.shape[1]
    tile = 256
    return pl.pallas_call(
        gradient_kernel,
        grid=(units // tile,),
        in_specs=[
            pl.BlockSpec((rows, 1), lambda i: (0, 0)),
            pl.BlockSpec((rows, tile), lambda i: (0, i)),
            pl.BlockSpec((rows, piece), lambda i: (0, 0)),
        ],
        out_specs=pl.BlockSpec((DOMAINS, tile, piece), lambda i: (0, i, 0)),
        out_shape=jax.ShapeDtypeStruct((DOMAINS, units, piece), jnp.bfloat16),
        scratch_shapes=[pltpu.VMEM((rows, DOMAINS * piece), jnp.bfloat16)],
        compiler_params=pltpu.CompilerParams(vmem_limit_bytes=32 * 2**20),
        cost_estimate=pl.CostEstimate(
            flops=2 * rows * units * DOMAINS * piece,
            bytes_accessed=2 * (rows * units + rows * piece + DOMAINS * units * piece),
            transcendentals=0,
        ),
    )(row_ids, hidden, y)


def shards(layer_input_activations, cotangent, domain_ids, norm_gain, w_gate, w_up, w_down):
    segment = lax.axis_index("section")
    dp_index = lax.axis_index("dp")
    segments = lax.axis_size("section")
    tensor_size = lax.axis_size("tensor")
    dp_size = lax.axis_size("dp")
    assert segments == 2
    micro, local_rows, width = layer_input_activations.shape
    gain = norm_gain[0][None, :]
    gate_w, up_w, down_w = w_gate[0], w_up[0], w_down[0]
    units = down_w.shape[0]
    block = micro * local_rows
    tok_rows = block * tensor_size
    first = segment == 0

    def reorder(value, offset):
        parts = value.reshape(tensor_size, block, width)
        return jnp.concatenate([parts[k ^ offset] for k in range(tensor_size)], axis=0)

    own_rows = jnp.where(first, layer_input_activations, cotangent).reshape(block, width)
    rows_in = jnp.concatenate(gather_relative(own_rows, "tensor"), axis=0)
    ids_all = gather_relative(domain_ids, "dp")
    rows_other = swap(rows_in, "section", 1)

    def layer_parts(rows):
        widened = rows.astype(jnp.float32)
        scale = lax.rsqrt(jnp.mean(widened * widened, axis=-1, keepdims=True) + EPS)
        normed = (widened * scale * gain).astype(jnp.bfloat16)
        gate = jnp.dot(normed, gate_w, preferred_element_type=jnp.float32)
        up = jnp.dot(normed, up_w, preferred_element_type=jnp.float32)
        return widened, scale, gate, up

    _, _, gate0, up0 = layer_parts(rows_in)
    hidden0 = (jax.nn.silu(gate0) * up0).astype(jnp.bfloat16)
    mixed = jnp.dot(hidden0, down_w, preferred_element_type=jnp.float32).astype(jnp.bfloat16)
    cot_rows, mixed = lax.optimization_barrier((rows_in, mixed))
    d_hidden = lax.dot_general(cot_rows, down_w, CONTRACT_LAST, preferred_element_type=jnp.float32)

    total = rows_other.astype(jnp.float32)
    for k in range(tensor_size):
        total = total + reorder(across(mixed, 0, k), k).astype(jnp.float32)
    x1 = total.astype(jnp.bfloat16)

    widened, scale, gate, up = layer_parts(x1)
    sig = jax.nn.sigmoid(gate)
    hidden1 = (gate * sig * up).astype(jnp.bfloat16)
    hidden = jnp.where(first, hidden0, hidden1)
    hidden_all = jnp.concatenate(gather_relative(hidden, "dp"), axis=0)
    d_gate = (d_hidden * up * (sig * (1.0 + gate * (1.0 - sig)))).astype(jnp.bfloat16)
    d_up = (d_hidden * gate * sig).astype(jnp.bfloat16)
    d_normed = lax.dot_general(d_gate, gate_w, CONTRACT_LAST, preferred_element_type=jnp.float32)
    d_normed = d_normed + lax.dot_general(
        d_up, up_w, CONTRACT_LAST, preferred_element_type=jnp.float32
    )
    pulled = d_normed * gain
    along = jnp.sum(pulled * widened, axis=-1, keepdims=True) / width
    term = (pulled * scale - widened * (scale * scale * scale * along)).astype(jnp.bfloat16)

    total = rows_other.astype(jnp.float32)
    for k in range(tensor_size):
        total = total + reorder(across(term, 1, k), k).astype(jnp.float32)
    dy = jnp.where(first, total.astype(jnp.bfloat16), rows_in)

    piece = width // dp_size
    columns = []
    for k in range(dp_size):
        part = lax.dynamic_slice_in_dim(dy, (dp_index ^ k) * piece, piece, axis=1)
        columns.append(part if k == 0 else swap(part, "dp", k))
    y = jnp.concatenate(columns, axis=0)

    one_row_block = [
        jnp.broadcast_to(ids[None, :, :], (tensor_size, micro, local_rows)).reshape(tok_rows, 1)
        for ids in ids_all
    ]
    row_ids = jnp.concatenate(one_row_block, axis=0)
    grads = domain_gradients(row_ids, hidden_all, y)

    gram_hidden = lax.dot_general(
        hidden_all, hidden_all, CONTRACT_LAST, preferred_element_type=jnp.float32
    )
    gram_y = lax.dot_general(y, y, CONTRACT_LAST, preferred_element_type=jnp.float32)
    pairs = jnp.where(row_ids == row_ids.T, gram_hidden * gram_y, 0.0)
    replica = jnp.arange(tok_rows * dp_size) // tok_rows
    onehot = (row_ids == jnp.arange(DOMAINS)[None, :]).astype(jnp.float32)
    levels = dp_size.bit_length()
    sums = []
    for level in range(levels):
        group = replica >> level
        of_row = jnp.sum(jnp.where(group[:, None] == group[None, :], pairs, 0.0), axis=1)
        sums.append(jnp.sum(onehot * of_row[:, None], axis=0))
    norms = jnp.stack(sums, axis=1)
    for axis in ("tensor", "dp", "section"):
        for bit in range(lax.axis_size(axis).bit_length() - 1):
            norms = norms + swap(norms, axis, 2**bit)
    entries = segments * units * tensor_size * width
    counts = [float((dp_size >> level) * entries) for level in range(levels)]
    return grads[None], norms / jnp.array(counts, jnp.float32)[None, :]


def solution(mesh):
    return jax.shard_map(
        shards,
        mesh=mesh,
        in_specs=(
            P(None, ("dp", "tensor"), None),
            P(None, ("dp", "tensor"), None),
            P(None, "dp"),
            P("section", None),
            P("section", None, "tensor"),
            P("section", None, "tensor"),
            P("section", "tensor", None),
        ),
        out_specs=(P("section", None, "tensor", "dp"), P()),
        check_vma=False,
    )
```

```python
import jax
import jax.numpy as jnp
from jax import lax
from jax.experimental import pallas as pl
from jax.experimental.pallas import tpu as pltpu
from jax.sharding import PartitionSpec as P

DOMAINS = 4
TILE = 256
EPS = 1e-05
CONTRACT_LAST = (((1,), (1,)), ((), ()))
CONTRACT_FIRST = (((0,), (0,)), ((), ()))


def swap(block, axis, offset):
    size = lax.axis_size(axis)
    return lax.ppermute(block, axis, [(i, i ^ offset) for i in range(size)])


def swap_in(block, section, axis, offset):
    size = lax.axis_size(axis)
    route = [(section * size + i, section * size + (i ^ offset)) for i in range(size)]
    return lax.ppermute(block, ("section", axis), route)


def across(block, source, offset):
    size = lax.axis_size("tensor")
    route = [
        (source * size + i, (1 - source) * size + (i ^ offset)) for i in range(size)
    ]
    return lax.ppermute(block, ("section", "tensor"), route)


def bits(axis):
    return lax.axis_size(axis).bit_length() - 1


def gather_rows(rows, section=None):
    size = lax.axis_size("tensor")
    if section is None:
        others = [swap(rows, "tensor", k) for k in range(1, size)]
    else:
        others = [swap_in(rows, section, "tensor", k) for k in range(1, size)]
    return jnp.concatenate([rows] + others, axis=0)


def scatter_sum(start, terms, source, block):
    total = start.astype(jnp.float32)
    for k in range(lax.axis_size("tensor")):
        arrived = across(terms[k * block : (k + 1) * block], source, k)
        total = total + arrived.astype(jnp.float32)
    return total.astype(jnp.bfloat16)


def load_kernel(*refs):
    count = (len(refs) - 1) // 2
    copies = [
        pltpu.make_async_copy(refs[i].at[0], refs[count + i], refs[-1].at[i])
        for i in range(count)
    ]
    for copy in copies:
        copy.start()
    for copy in copies:
        copy.wait()


def load_weights(*weights):
    total = sum(w.size * 2 for w in weights)
    return pl.pallas_call(
        load_kernel,
        in_specs=[pl.BlockSpec(memory_space=pltpu.HBM)] * len(weights),
        out_specs=[pl.BlockSpec(memory_space=pltpu.VMEM)] * len(weights),
        out_shape=[pltpu.VMEM(w.shape[1:], w.dtype) for w in weights],
        scratch_shapes=[pltpu.SemaphoreType.DMA((len(weights),))],
        compiler_params=pltpu.CompilerParams(vmem_limit_bytes=total + 2**20),
        cost_estimate=pl.CostEstimate(flops=0, bytes_accessed=total, transcendentals=0),
    )(*weights)


def gradient_kernel(ids_ref, hidden_ref, y_ref, *rest):
    out_ref, masked = rest[-2:]
    piece = y_ref.shape[1]

    @pl.when(pl.program_id(0) == 0)
    def _():
        for e in range(DOMAINS):
            keep = ids_ref[...] == e
            masked[:, e * piece : (e + 1) * piece] = jnp.where(
                keep, y_ref[...].astype(jnp.float32), 0.0
            ).astype(jnp.bfloat16)

    product = lax.dot_general(
        hidden_ref[...], masked[...], CONTRACT_FIRST, preferred_element_type=jnp.float32
    )
    for e in range(DOMAINS):
        out_ref[e] = product[:, e * piece : (e + 1) * piece].astype(jnp.bfloat16)


def domain_gradients(row_ids, hidden, y, begin, count, grads=None):
    rows, units = hidden.shape
    piece = y.shape[1]
    in_specs = [
        pl.BlockSpec((rows, 1), lambda i: (0, 0)),
        pl.BlockSpec((rows, TILE), lambda i: (0, begin + i)),
        pl.BlockSpec((rows, piece), lambda i: (0, 0)),
    ]
    operands = [row_ids, hidden, y]
    if grads is not None:
        in_specs.append(pl.BlockSpec(memory_space=pl.ANY))
        operands.append(grads)
    return pl.pallas_call(
        gradient_kernel,
        grid=(count,),
        in_specs=in_specs,
        out_specs=pl.BlockSpec((DOMAINS, TILE, piece), lambda i: (0, begin + i, 0)),
        out_shape=jax.ShapeDtypeStruct((DOMAINS, units, piece), jnp.bfloat16),
        scratch_shapes=[pltpu.VMEM((rows, DOMAINS * piece), jnp.bfloat16)],
        input_output_aliases={} if grads is None else {3: 0},
        compiler_params=pltpu.CompilerParams(vmem_limit_bytes=24 * 2**20),
        cost_estimate=pl.CostEstimate(
            flops=2 * rows * count * TILE * DOMAINS * piece,
            bytes_accessed=2 * count * TILE * (rows + DOMAINS * piece),
            transcendentals=0,
        ),
    )(*operands)


def shards(layer_input_activations, cotangent, domain_ids, norm_gain, w_gate, w_up, w_down):
    segment = lax.axis_index("section")
    dp_index = lax.axis_index("dp")
    segments = lax.axis_size("section")
    tensor_size = lax.axis_size("tensor")
    dp_size = lax.axis_size("dp")
    assert segments == 2
    micro, local_rows, width = layer_input_activations.shape
    gain = norm_gain[0][None, :]
    gate_w, up_w, down_w = load_weights(w_gate, w_up, w_down)
    units = down_w.shape[0]
    block = micro * local_rows
    tok_rows = block * tensor_size
    first = segment == 0

    x_own = layer_input_activations.reshape(block, width)
    cot_own = cotangent.reshape(block, width)
    rows_in = gather_rows(jnp.where(first, x_own, cot_own))

    def layer_parts(rows):
        widened = rows.astype(jnp.float32)
        scale = lax.rsqrt(jnp.mean(widened * widened, axis=-1, keepdims=True) + EPS)
        normed = (widened * scale * gain).astype(jnp.bfloat16)
        gate = jnp.dot(normed, gate_w, preferred_element_type=jnp.float32)
        up = jnp.dot(normed, up_w, preferred_element_type=jnp.float32)
        return widened, scale, gate, up

    id_rows = -(-micro // 16) * 16
    id_block = jnp.broadcast_to(
        jnp.pad(domain_ids.astype(jnp.bfloat16), ((0, id_rows - micro), (0, 0))), (id_rows, units)
    )

    def gather_hidden(hidden, section):
        gathered = jnp.concatenate([hidden, id_block], axis=0)[None]
        for bit in range(bits("dp")):
            other = swap_in(gathered, section, "dp", 2**bit)
            gathered = jnp.concatenate([gathered, other], axis=0)
        return gathered

    _, _, gate0, up0 = layer_parts(rows_in)
    hidden0 = (jax.nn.silu(gate0) * up0).astype(jnp.bfloat16)
    mixed = jnp.dot(hidden0, down_w, preferred_element_type=jnp.float32).astype(jnp.bfloat16)
    cot_rows, mixed = lax.optimization_barrier((rows_in, mixed))
    d_hidden = lax.dot_general(cot_rows, down_w, CONTRACT_LAST, preferred_element_type=jnp.float32)
    x1 = gather_rows(scatter_sum(x_own, mixed, 0, block), 1)
    gathered0 = gather_hidden(hidden0, 0)

    widened, scale, gate, up = layer_parts(x1)
    sig = jax.nn.sigmoid(gate)
    hidden1 = (gate * sig * up).astype(jnp.bfloat16)
    d_gate = (d_hidden * up * (sig * (1.0 + gate * (1.0 - sig)))).astype(jnp.bfloat16)
    d_up = (d_hidden * gate * sig).astype(jnp.bfloat16)
    d_normed = lax.dot_general(d_gate, gate_w, CONTRACT_LAST, preferred_element_type=jnp.float32)
    d_normed = d_normed + lax.dot_general(
        d_up, up_w, CONTRACT_LAST, preferred_element_type=jnp.float32
    )
    pulled = d_normed * gain
    along = jnp.sum(pulled * widened, axis=-1, keepdims=True) / width
    term = (pulled * scale - widened * (scale * scale * scale * along)).astype(jnp.bfloat16)
    hidden1, term = lax.optimization_barrier((hidden1, term))
    dy_own = scatter_sum(cot_own, term, 1, block)
    dy_own = jnp.where(first, dy_own, cot_own)

    piece = width // dp_size
    columns = []
    for k in range(dp_size):
        part = lax.dynamic_slice_in_dim(dy_own, (dp_index ^ k) * piece, piece, axis=1)
        columns.append(part if k == 0 else swap(part, "dp", k))
    y = gather_rows(jnp.concatenate(columns, axis=0))

    gathered = jnp.where(first, gathered0, gather_hidden(hidden1, 1))
    hidden_all = gathered[:, :tok_rows].reshape(dp_size, tensor_size, block, units)
    hidden_all = jnp.swapaxes(hidden_all, 0, 1).reshape(dp_size * tok_rows, units)
    ids_all = gathered[:, tok_rows : tok_rows + micro, 0].astype(jnp.int32)
    row_ids = jnp.broadcast_to(
        ids_all[None, :, :, None], (tensor_size, dp_size, micro, local_rows)
    ).reshape(dp_size * tok_rows, 1)
    gram_hidden = lax.dot_general(
        hidden_all, hidden_all, CONTRACT_LAST, preferred_element_type=jnp.float32
    )
    gram_y = lax.dot_general(y, y, CONTRACT_LAST, preferred_element_type=jnp.float32)
    pairs = jnp.where(row_ids == row_ids.T, gram_hidden * gram_y, 0.0)
    replica = jnp.arange(tok_rows * dp_size) // block % dp_size
    onehot = (row_ids == jnp.arange(DOMAINS)[None, :]).astype(jnp.float32)
    levels = dp_size.bit_length()
    sums = []
    for level in range(levels):
        group = replica >> level
        of_row = jnp.sum(jnp.where(group[:, None] == group[None, :], pairs, 0.0), axis=1)
        sums.append(jnp.sum(onehot * of_row[:, None], axis=0))
    norms = jnp.stack(sums, axis=1)
    rounds = [(axis, bit) for axis in ("tensor", "dp", "section") for bit in range(bits(axis))]
    tiles = units // TILE
    parts = min(len(rounds) - 1, tiles)
    grads = None
    begin = 0
    for part, (axis, bit) in enumerate(rounds):
        other = swap(norms, axis, 2**bit)
        if part < parts:
            end = tiles * (part + 1) // parts
            grads = domain_gradients(row_ids, hidden_all, y, begin, end - begin, grads)
            begin = end
        norms = norms + other
        row_ids, norms = lax.optimization_barrier((row_ids, norms))
    entries = segments * units * tensor_size * width
    counts = [float((dp_size >> level) * entries) for level in range(levels)]
    return grads[None], norms / jnp.array(counts, jnp.float32)[None, :]


def solution(mesh):
    return jax.shard_map(
        shards,
        mesh=mesh,
        in_specs=(
            P(None, ("dp", "tensor"), None),
            P(None, ("dp", "tensor"), None),
            P(None, "dp"),
            P("section", None),
            P("section", None, "tensor"),
            P("section", None, "tensor"),
            P("section", "tensor", None),
        ),
        out_specs=(P("section", None, "tensor", "dp"), P()),
        check_vma=False,
    )
```

```python
import jax
import jax.numpy as jnp
from jax import lax
from jax.experimental import pallas as pl
from jax.experimental.pallas import tpu as pltpu
from jax.sharding import PartitionSpec as P

DOMAINS = 4
TILE = 256
EPS = 1e-05
CONTRACT_LAST = (((1,), (1,)), ((), ()))
CONTRACT_FIRST = (((0,), (0,)), ((), ()))


def swap(block, axis, offset):
    size = lax.axis_size(axis)
    return lax.ppermute(block, axis, [(i, i ^ offset) for i in range(size)])


def swap_in(block, section, axis, offset):
    size = lax.axis_size(axis)
    route = [(section * size + i, section * size + (i ^ offset)) for i in range(size)]
    return lax.ppermute(block, ("section", axis), route)


def across(block, source, offset):
    size = lax.axis_size("tensor")
    route = [
        (source * size + i, (1 - source) * size + (i ^ offset)) for i in range(size)
    ]
    return lax.ppermute(block, ("section", "tensor"), route)


def bits(axis):
    return lax.axis_size(axis).bit_length() - 1


def gather_rows(rows, section=None):
    size = lax.axis_size("tensor")
    if section is None:
        others = [swap(rows, "tensor", k) for k in range(1, size)]
    else:
        others = [swap_in(rows, section, "tensor", k) for k in range(1, size)]
    return jnp.concatenate([rows] + others, axis=0)


def scatter_sum(start, terms, source, block):
    total = start.astype(jnp.float32)
    for k in range(lax.axis_size("tensor")):
        arrived = across(terms[k * block : (k + 1) * block], source, k)
        total = total + arrived.astype(jnp.float32)
    return total.astype(jnp.bfloat16)


def load_kernel(*refs):
    count = (len(refs) - 1) // 2
    copies = [
        pltpu.make_async_copy(refs[i].at[0], refs[count + i], refs[-1].at[i])
        for i in range(count)
    ]
    for copy in copies:
        copy.start()
    for copy in copies:
        copy.wait()


def load_weights(*weights):
    total = sum(w.size * 2 for w in weights)
    weights = [pltpu.with_memory_space_constraint(w, pltpu.HBM) for w in weights]
    return pl.pallas_call(
        load_kernel,
        in_specs=[pl.BlockSpec(memory_space=pltpu.HBM)] * len(weights),
        out_specs=[pl.BlockSpec(memory_space=pltpu.VMEM)] * len(weights),
        out_shape=[pltpu.VMEM(w.shape[1:], w.dtype) for w in weights],
        scratch_shapes=[pltpu.SemaphoreType.DMA((len(weights),))],
        compiler_params=pltpu.CompilerParams(vmem_limit_bytes=total + 2**20),
        cost_estimate=pl.CostEstimate(flops=0, bytes_accessed=total, transcendentals=0),
    )(*weights)


def gradient_kernel(ids_ref, hidden_ref, y_ref, *rest):
    out_ref, masked = rest[-2:]
    piece = y_ref.shape[1]

    @pl.when(pl.program_id(0) == 0)
    def _():
        for e in range(DOMAINS):
            keep = ids_ref[...] == e
            masked[:, e * piece : (e + 1) * piece] = jnp.where(
                keep, y_ref[...].astype(jnp.float32), 0.0
            ).astype(jnp.bfloat16)

    product = lax.dot_general(
        hidden_ref[...], masked[...], CONTRACT_FIRST, preferred_element_type=jnp.float32
    )
    for e in range(DOMAINS):
        out_ref[e] = product[:, e * piece : (e + 1) * piece].astype(jnp.bfloat16)


def domain_gradients(row_ids, hidden, y, begin, count, grads=None):
    rows, units = hidden.shape
    piece = y.shape[1]
    in_specs = [
        pl.BlockSpec((rows, 1), lambda i: (0, 0)),
        pl.BlockSpec((rows, TILE), lambda i: (0, begin + i)),
        pl.BlockSpec((rows, piece), lambda i: (0, 0)),
    ]
    operands = [row_ids, hidden, y]
    if grads is not None:
        in_specs.append(pl.BlockSpec(memory_space=pl.ANY))
        operands.append(grads)
    return pl.pallas_call(
        gradient_kernel,
        grid=(count,),
        in_specs=in_specs,
        out_specs=pl.BlockSpec((DOMAINS, TILE, piece), lambda i: (0, begin + i, 0)),
        out_shape=jax.ShapeDtypeStruct((DOMAINS, units, piece), jnp.bfloat16),
        scratch_shapes=[pltpu.VMEM((rows, DOMAINS * piece), jnp.bfloat16)],
        input_output_aliases={} if grads is None else {3: 0},
        compiler_params=pltpu.CompilerParams(vmem_limit_bytes=24 * 2**20),
        cost_estimate=pl.CostEstimate(
            flops=2 * rows * count * TILE * DOMAINS * piece,
            bytes_accessed=2 * count * TILE * (rows + DOMAINS * piece),
            transcendentals=0,
        ),
    )(*operands)


def shards(layer_input_activations, cotangent, domain_ids, norm_gain, w_gate, w_up, w_down):
    segment = lax.axis_index("section")
    dp_index = lax.axis_index("dp")
    segments = lax.axis_size("section")
    tensor_size = lax.axis_size("tensor")
    dp_size = lax.axis_size("dp")
    assert segments == 2
    micro, local_rows, width = layer_input_activations.shape
    gain = norm_gain[0][None, :]
    gate_w, up_w, down_w = load_weights(w_gate, w_up, w_down)
    units = down_w.shape[0]
    block = micro * local_rows
    tok_rows = block * tensor_size
    first = segment == 0

    x_own = layer_input_activations.reshape(block, width)
    cot_own = cotangent.reshape(block, width)
    rows_in = gather_rows(jnp.where(first, x_own, cot_own))

    def layer_parts(rows):
        widened = rows.astype(jnp.float32)
        scale = lax.rsqrt(jnp.mean(widened * widened, axis=-1, keepdims=True) + EPS)
        normed = (widened * scale * gain).astype(jnp.bfloat16)
        gate = jnp.dot(normed, gate_w, preferred_element_type=jnp.float32)
        up = jnp.dot(normed, up_w, preferred_element_type=jnp.float32)
        return widened, scale, gate, up

    def gather_hidden(gathered, section, begin, end):
        for bit in range(begin, end):
            other = swap_in(gathered, section, "dp", 2**bit)
            gathered = jnp.concatenate([gathered, other], axis=0)
        return gathered

    _, _, gate0, up0 = layer_parts(rows_in)
    hidden0 = (jax.nn.silu(gate0) * up0).astype(jnp.bfloat16)
    mixed = jnp.dot(hidden0, down_w, preferred_element_type=jnp.float32).astype(jnp.bfloat16)
    cot_rows, hidden0, mixed = lax.optimization_barrier((rows_in, hidden0, mixed))
    d_hidden = lax.dot_general(cot_rows, down_w, CONTRACT_LAST, preferred_element_type=jnp.float32)
    some0 = gather_hidden(hidden0, 0, 0, 1)
    x1_own = scatter_sum(x_own, mixed, 0, block)
    x1_own, d_hidden, some0 = lax.optimization_barrier((x1_own, d_hidden, some0))
    x1 = gather_rows(x1_own, 1)
    all0 = gather_hidden(some0, 0, 1, bits("dp"))

    widened, scale, gate, up = layer_parts(x1)
    sig = jax.nn.sigmoid(gate)
    hidden1 = (gate * sig * up).astype(jnp.bfloat16)
    d_gate = (d_hidden * up * (sig * (1.0 + gate * (1.0 - sig)))).astype(jnp.bfloat16)
    d_up = (d_hidden * gate * sig).astype(jnp.bfloat16)
    d_normed = lax.dot_general(d_gate, gate_w, CONTRACT_LAST, preferred_element_type=jnp.float32)
    d_normed = d_normed + lax.dot_general(
        d_up, up_w, CONTRACT_LAST, preferred_element_type=jnp.float32
    )
    pulled = d_normed * gain
    along = jnp.sum(pulled * widened, axis=-1, keepdims=True) / width
    term = (pulled * scale - widened * (scale * scale * scale * along)).astype(jnp.bfloat16)
    term, all0 = lax.optimization_barrier((term, all0))
    dy_own = scatter_sum(cot_own, term, 1, block)
    dy_own = jnp.where(first, dy_own, cot_own)
    dy_own, hidden1 = lax.optimization_barrier((dy_own, hidden1))

    piece = width // dp_size
    id_rows = -(-micro // 16) * 16
    id_block = jnp.broadcast_to(
        jnp.pad(domain_ids.astype(jnp.bfloat16), ((0, id_rows - micro), (0, 0))), (id_rows, piece)
    )
    messages = []
    for k in range(dp_size):
        part = lax.dynamic_slice_in_dim(dy_own, (dp_index ^ k) * piece, piece, axis=1)
        part = jnp.concatenate([part, id_block], axis=0)
        messages.append(part if k == 0 else swap(part, "dp", k))
    all1 = gather_hidden(hidden1, 1, 0, bits("dp"))
    hidden_all = jnp.where(first, all0, all1)
    gram_hidden = lax.dot_general(
        hidden_all, hidden_all, CONTRACT_LAST, preferred_element_type=jnp.float32
    )
    columns = jnp.concatenate([message[:block] for message in messages], axis=0)
    columns, hidden_all, gram_hidden = lax.optimization_barrier(
        (columns, hidden_all, gram_hidden)
    )
    y = gather_rows(columns).reshape(tensor_size, dp_size, block, piece)
    y = jnp.swapaxes(y, 0, 1).reshape(dp_size * tok_rows, piece)
    ids_all = jnp.stack([message[block : block + micro, 0] for message in messages])
    row_ids = jnp.broadcast_to(
        ids_all.astype(jnp.int32)[:, None, :, None], (dp_size, tensor_size, micro, local_rows)
    ).reshape(dp_size * tok_rows, 1)

    gram_y = lax.dot_general(y, y, CONTRACT_LAST, preferred_element_type=jnp.float32)
    pairs = jnp.where(row_ids == row_ids.T, gram_hidden * gram_y, 0.0)
    replica = jnp.arange(tok_rows * dp_size) // tok_rows
    onehot = (row_ids == jnp.arange(DOMAINS)[None, :]).astype(jnp.float32)
    levels = dp_size.bit_length()
    sums = []
    for level in range(levels):
        group = replica >> level
        of_row = jnp.sum(jnp.where(group[:, None] == group[None, :], pairs, 0.0), axis=1)
        sums.append(jnp.sum(onehot * of_row[:, None], axis=0))
    norms = jnp.stack(sums, axis=1)
    rounds = [(axis, bit) for axis in ("tensor", "dp", "section") for bit in range(bits(axis))]
    tiles = units // TILE
    parts = min(3, tiles)
    grads = None
    begin = 0
    for part, (axis, bit) in enumerate(rounds):
        other = swap(norms, axis, 2**bit)
        if part < parts:
            end = tiles * (part + 1) // parts
            grads = domain_gradients(row_ids, hidden_all, y, begin, end - begin, grads)
            begin = end
        norms = norms + other
        row_ids, norms = lax.optimization_barrier((row_ids, norms))
    entries = segments * units * tensor_size * width
    counts = [float((dp_size >> level) * entries) for level in range(levels)]
    return grads[None], norms / jnp.array(counts, jnp.float32)[None, :]


def solution(mesh):
    return jax.shard_map(
        shards,
        mesh=mesh,
        in_specs=(
            P(None, ("dp", "tensor"), None),
            P(None, ("dp", "tensor"), None),
            P(None, "dp"),
            P("section", None),
            P("section", None, "tensor"),
            P("section", None, "tensor"),
            P("section", "tensor", None),
        ),
        out_specs=(P("section", None, "tensor", "dp"), P()),
        check_vma=False,
    )
```

```python
import functools

import jax
import jax.numpy as jnp
from jax import lax
from jax.experimental import pallas as pl
from jax.experimental.pallas import tpu as pltpu
from jax.sharding import PartitionSpec as P

DOMAINS = 4
TILE = 256
EPS = 1e-05
CONTRACT_LAST = (((1,), (1,)), ((), ()))
CONTRACT_FIRST = (((0,), (0,)), ((), ()))


def swap(block, axis, offset):
    size = lax.axis_size(axis)
    return lax.ppermute(block, axis, [(i, i ^ offset) for i in range(size)])


def swap_in(block, section, axis, offset):
    size = lax.axis_size(axis)
    route = [(section * size + i, section * size + (i ^ offset)) for i in range(size)]
    return lax.ppermute(block, ("section", axis), route)


def across(block, source, offset):
    size = lax.axis_size("tensor")
    route = [
        (source * size + i, (1 - source) * size + (i ^ offset)) for i in range(size)
    ]
    return lax.ppermute(block, ("section", "tensor"), route)


def bits(axis):
    return lax.axis_size(axis).bit_length() - 1


def gather_in(rows, section, axis):
    size = lax.axis_size(axis)
    return [rows] + [swap_in(rows, section, axis, k) for k in range(1, size)]


def scatter_sum(start, terms, source, block):
    total = start.astype(jnp.float32)
    for k in range(lax.axis_size("tensor")):
        arrived = across(terms[k * block : (k + 1) * block], source, k)
        total = total + arrived.astype(jnp.float32)
    return total.astype(jnp.bfloat16)


def load_kernel(*refs):
    count = (len(refs) - 1) // 2
    copies = [
        pltpu.make_async_copy(refs[i].at[0], refs[count + i], refs[-1].at[i])
        for i in range(count)
    ]
    for copy in copies:
        copy.start()
    for copy in copies:
        copy.wait()


def load_weights(*weights):
    total = sum(w.size * 2 for w in weights)
    weights = [pltpu.with_memory_space_constraint(w, pltpu.HBM) for w in weights]
    return pl.pallas_call(
        load_kernel,
        in_specs=[pl.BlockSpec(memory_space=pltpu.HBM)] * len(weights),
        out_specs=[pl.BlockSpec(memory_space=pltpu.VMEM)] * len(weights),
        out_shape=[pltpu.VMEM(w.shape[1:], w.dtype) for w in weights],
        scratch_shapes=[pltpu.SemaphoreType.DMA((len(weights),))],
        compiler_params=pltpu.CompilerParams(vmem_limit_bytes=total + 2**20),
        cost_estimate=pl.CostEstimate(flops=0, bytes_accessed=total, transcendentals=0),
    )(*weights)


def gradient_kernel(ids_ref, hidden_ref, y_ref, *rest):
    out_ref, masked = rest[-2:]
    piece = y_ref.shape[1]

    @pl.when(pl.program_id(0) == 0)
    def _():
        for e in range(DOMAINS):
            keep = ids_ref[...] == e
            masked[:, e * piece : (e + 1) * piece] = jnp.where(
                keep, y_ref[...].astype(jnp.float32), 0.0
            ).astype(jnp.bfloat16)

    product = lax.dot_general(
        hidden_ref[...], masked[...], CONTRACT_FIRST, preferred_element_type=jnp.float32
    )
    for e in range(DOMAINS):
        out_ref[e] = product[:, e * piece : (e + 1) * piece].astype(jnp.bfloat16)


def domain_gradients(row_ids, hidden, y, begin, count, grads=None):
    rows, units = hidden.shape
    piece = y.shape[1]
    in_specs = [
        pl.BlockSpec((rows, 1), lambda i: (0, 0)),
        pl.BlockSpec((rows, TILE), lambda i: (0, begin + i)),
        pl.BlockSpec((rows, piece), lambda i: (0, 0)),
    ]
    operands = [row_ids, hidden, y]
    if grads is not None:
        in_specs.append(pl.BlockSpec(memory_space=pl.ANY))
        operands.append(grads)
    return pl.pallas_call(
        gradient_kernel,
        grid=(count,),
        in_specs=in_specs,
        out_specs=pl.BlockSpec((DOMAINS, TILE, piece), lambda i: (0, begin + i, 0)),
        out_shape=jax.ShapeDtypeStruct((DOMAINS, units, piece), jnp.bfloat16),
        scratch_shapes=[pltpu.VMEM((rows, DOMAINS * piece), jnp.bfloat16)],
        input_output_aliases={} if grads is None else {3: 0},
        compiler_params=pltpu.CompilerParams(vmem_limit_bytes=24 * 2**20),
        cost_estimate=pl.CostEstimate(
            flops=2 * rows * count * TILE * DOMAINS * piece,
            bytes_accessed=2 * count * TILE * (rows + DOMAINS * piece),
            transcendentals=0,
        ),
    )(*operands)


def assemble_kernel(count, flag_ref, *refs):
    pieces = refs[: 2 * count]
    hidden_ref, gram_ref, sems = refs[2 * count :]
    rows = pieces[0].shape[0]
    for section in range(2):

        @pl.when(flag_ref[0] == section)
        def _(section=section):
            copies = [
                pltpu.make_async_copy(
                    pieces[section * count + k],
                    hidden_ref.at[pl.ds(k * rows, rows)],
                    sems.at[k],
                )
                for k in range(count)
            ]
            for copy in copies:
                copy.start()
            for copy in copies:
                copy.wait()

    total = rows * count
    step = min(total, 512)
    for begin in range(0, total, step):
        gram_ref[begin : begin + step, :] = lax.dot_general(
            hidden_ref[begin : begin + step, :],
            hidden_ref[...],
            CONTRACT_LAST,
            preferred_element_type=jnp.float32,
        )


def assemble(segment, pieces0, pieces1):
    count = len(pieces0)
    rows, units = pieces0[0].shape
    total = rows * count
    pieces = [pltpu.with_memory_space_constraint(p, pltpu.HBM) for p in pieces0 + pieces1]
    return pl.pallas_call(
        functools.partial(assemble_kernel, count),
        in_specs=[pl.BlockSpec(memory_space=pltpu.SMEM)]
        + [pl.BlockSpec(memory_space=pl.ANY)] * (2 * count),
        out_specs=[pl.BlockSpec(memory_space=pltpu.VMEM)] * 2,
        out_shape=[
            jax.ShapeDtypeStruct((total, units), jnp.bfloat16),
            jax.ShapeDtypeStruct((total, total), jnp.float32),
        ],
        scratch_shapes=[pltpu.SemaphoreType.DMA((count,))],
        compiler_params=pltpu.CompilerParams(
            vmem_limit_bytes=2 * total * units + 4 * total * total + 4 * 2**20
        ),
        cost_estimate=pl.CostEstimate(
            flops=2 * total * total * units,
            bytes_accessed=4 * total * units + 4 * total * total,
            transcendentals=0,
        ),
    )(segment.reshape(1), *pieces)


def norms_kernel(replicas, levels, ids_ref, ids_row_ref, gram_ref, *refs):
    *parts, y_ref, norms_ref, acc = refs
    block = parts[0].shape[0] // replicas
    tok_rows = block * len(parts)
    for t, part in enumerate(parts):
        for k in range(replicas):
            y_ref[k * tok_rows + t * block : k * tok_rows + (t + 1) * block, :] = part[
                k * block : (k + 1) * block, :
            ]
    acc[...] = jnp.zeros_like(acc)
    lane = lax.broadcasted_iota(jnp.int32, (1, acc.shape[1]), 1)
    for k in range(replicas):
        columns = slice(k * tok_rows, (k + 1) * tok_rows)
        gram_y = lax.dot_general(
            y_ref[...], y_ref[columns, :], CONTRACT_LAST, preferred_element_type=jnp.float32
        )
        pairs = jnp.where(ids_ref[...] == ids_row_ref[:, columns], gram_ref[:, columns] * gram_y, 0.0)
        of_row = jnp.sum(pairs, axis=1, keepdims=True)
        for level in range(levels):
            begin = (k >> level << level) * tok_rows
            end = begin + (tok_rows << level)
            acc[begin:end, :] += jnp.where(lane == level, of_row[begin:end], 0.0)
    for e in range(DOMAINS):
        norms_ref[e : e + 1, :] = jnp.sum(
            jnp.where(ids_ref[...] == e, acc[...], 0.0), axis=0, keepdims=True
        )
    norms_ref[DOMAINS:, :] = jnp.zeros_like(norms_ref[DOMAINS:, :])


def norm_sums(row_ids, gram_hidden, parts, replicas, levels):
    total = gram_hidden.shape[0]
    piece = parts[0].shape[1]
    return pl.pallas_call(
        functools.partial(norms_kernel, replicas, levels),
        in_specs=[pl.BlockSpec(memory_space=pltpu.VMEM)] * (3 + len(parts)),
        out_specs=[pl.BlockSpec(memory_space=pltpu.VMEM)] * 2,
        out_shape=[
            jax.ShapeDtypeStruct((total, piece), jnp.bfloat16),
            jax.ShapeDtypeStruct((8, 128), jnp.float32),
        ],
        scratch_shapes=[pltpu.VMEM((total, 128), jnp.float32)],
        compiler_params=pltpu.CompilerParams(
            vmem_limit_bytes=8 * total * piece + 4 * total * total + 1024 * total * 4 + 8 * 2**20
        ),
        cost_estimate=pl.CostEstimate(
            flops=2 * total * total * piece + 4 * total * total,
            bytes_accessed=4 * total * piece + 4 * total * total,
            transcendentals=0,
        ),
    )(row_ids, row_ids.reshape(1, total), gram_hidden, *parts)


def shards(layer_input_activations, cotangent, domain_ids, norm_gain, w_gate, w_up, w_down):
    segment = lax.axis_index("section")
    dp_index = lax.axis_index("dp")
    segments = lax.axis_size("section")
    tensor_size = lax.axis_size("tensor")
    dp_size = lax.axis_size("dp")
    assert segments == 2
    micro, local_rows, width = layer_input_activations.shape
    gain = norm_gain[0][None, :]
    gate_w, up_w = load_weights(w_gate, w_up)
    down_w = w_down[0]
    units = down_w.shape[0]
    block = micro * local_rows
    tok_rows = block * tensor_size
    first = segment == 0

    x_own = layer_input_activations.reshape(block, width)
    cot_own = cotangent.reshape(block, width)
    x0 = jnp.concatenate(gather_in(x_own, 0, "tensor"), axis=0)
    cot_late, gate_w, up_w = lax.optimization_barrier((cot_own, gate_w, up_w))
    cot_rows = jnp.concatenate(gather_in(cot_late, 1, "tensor"), axis=0)

    def layer_parts(rows):
        widened = rows.astype(jnp.float32)
        scale = lax.rsqrt(jnp.mean(widened * widened, axis=-1, keepdims=True) + EPS)
        normed = (widened * scale * gain).astype(jnp.bfloat16)
        gate = jnp.dot(normed, gate_w, preferred_element_type=jnp.float32)
        up = jnp.dot(normed, up_w, preferred_element_type=jnp.float32)
        return widened, scale, gate, up

    _, _, gate0, up0 = layer_parts(x0)
    hidden0 = (jax.nn.silu(gate0) * up0).astype(jnp.bfloat16)
    mixed = jnp.dot(hidden0, down_w, preferred_element_type=jnp.float32).astype(jnp.bfloat16)
    cot_rows, hidden0, mixed = lax.optimization_barrier((cot_rows, hidden0, mixed))
    d_hidden = lax.dot_general(cot_rows, down_w, CONTRACT_LAST, preferred_element_type=jnp.float32)
    x1_own = scatter_sum(x_own, mixed, 0, block)
    x1_own, d_hidden = lax.optimization_barrier((x1_own, d_hidden))
    x1 = jnp.concatenate(gather_in(x1_own, 1, "tensor"), axis=0)
    x1, hidden0 = lax.optimization_barrier((x1, hidden0))
    pieces0 = gather_in(hidden0, 0, "dp")

    widened, scale, gate, up = layer_parts(x1)
    sig = jax.nn.sigmoid(gate)
    hidden1 = (gate * sig * up).astype(jnp.bfloat16)
    d_gate = (d_hidden * up * (sig * (1.0 + gate * (1.0 - sig)))).astype(jnp.bfloat16)
    d_up = (d_hidden * gate * sig).astype(jnp.bfloat16)
    d_gate, d_up = lax.optimization_barrier((d_gate, d_up))
    d_normed = lax.dot_general(d_gate, gate_w, CONTRACT_LAST, preferred_element_type=jnp.float32)
    d_normed = d_normed + lax.dot_general(
        d_up, up_w, CONTRACT_LAST, preferred_element_type=jnp.float32
    )
    pulled = d_normed * gain
    along = jnp.sum(pulled * widened, axis=-1, keepdims=True) / width
    term = (pulled * scale - widened * (scale * scale * scale * along)).astype(jnp.bfloat16)
    term, pieces0 = lax.optimization_barrier((term, pieces0))
    dy_own = scatter_sum(cot_own, term, 1, block)
    dy_own = jnp.where(first, dy_own, cot_own)
    dy_own, hidden1 = lax.optimization_barrier((dy_own, hidden1))

    piece = width // dp_size
    id_rows = -(-micro // 16) * 16
    id_block = jnp.broadcast_to(
        jnp.pad(domain_ids.astype(jnp.bfloat16), ((0, id_rows - micro), (0, 0))), (id_rows, piece)
    )
    messages = []
    for k in range(dp_size):
        part = lax.dynamic_slice_in_dim(dy_own, (dp_index ^ k) * piece, piece, axis=1)
        part = jnp.concatenate([part, id_block], axis=0)
        messages.append(part if k == 0 else swap(part, "dp", k))
    pieces1 = gather_in(hidden1, 1, "dp")
    columns = jnp.concatenate([message[:block] for message in messages], axis=0)
    columns, pieces1 = lax.optimization_barrier((columns, pieces1))
    parts_y = [columns] + [swap(columns, "tensor", k) for k in range(1, tensor_size)]
    hidden_all, gram_hidden = assemble(segment, pieces0, pieces1)
    ids_all = jnp.stack([message[block : block + micro, 0] for message in messages])
    row_ids = jnp.broadcast_to(
        ids_all.astype(jnp.int32)[:, None, :, None], (dp_size, tensor_size, micro, local_rows)
    ).reshape(dp_size * tok_rows, 1)
    levels = dp_size.bit_length()
    y, norms = norm_sums(row_ids, gram_hidden, parts_y, dp_size, levels)
    rounds = [(axis, bit) for axis in ("tensor", "dp", "section") for bit in range(bits(axis))]
    tiles = units // TILE
    parts = min(3, tiles)
    grads = None
    begin = 0
    for part, (axis, bit) in enumerate(rounds):
        other = swap(norms, axis, 2**bit)
        if part < parts:
            end = tiles * (part + 1) // parts
            grads = domain_gradients(row_ids, hidden_all, y, begin, end - begin, grads)
            begin = end
        norms = norms + other
        row_ids, norms = lax.optimization_barrier((row_ids, norms))
    entries = segments * units * tensor_size * width
    counts = [float((dp_size >> level) * entries) for level in range(levels)]
    return grads[None], norms[:DOMAINS, :levels] / jnp.array(counts, jnp.float32)[None, :]


def solution(mesh):
    return jax.shard_map(
        shards,
        mesh=mesh,
        in_specs=(
            P(None, ("dp", "tensor"), None),
            P(None, ("dp", "tensor"), None),
            P(None, "dp"),
            P("section", None),
            P("section", None, "tensor"),
            P("section", None, "tensor"),
            P("section", "tensor", None),
        ),
        out_specs=(P("section", None, "tensor", "dp"), P()),
        check_vma=False,
    )
```

```python
import functools

import jax
import jax.numpy as jnp
from jax import lax
from jax.experimental import pallas as pl
from jax.experimental.pallas import tpu as pltpu
from jax.sharding import PartitionSpec as P

DOMAINS = 4
TILE = 256
EPS = 1e-05
CONTRACT_LAST = (((1,), (1,)), ((), ()))
CONTRACT_FIRST = (((0,), (0,)), ((), ()))


def swap(block, axis, offset):
    size = lax.axis_size(axis)
    return lax.ppermute(block, axis, [(i, i ^ offset) for i in range(size)])


def swap_in(block, section, axis, offset):
    size = lax.axis_size(axis)
    route = [(section * size + i, section * size + (i ^ offset)) for i in range(size)]
    return lax.ppermute(block, ("section", axis), route)


def across(block, source, offset):
    size = lax.axis_size("tensor")
    route = [
        (source * size + i, (1 - source) * size + (i ^ offset)) for i in range(size)
    ]
    return lax.ppermute(block, ("section", "tensor"), route)


def bits(axis):
    return lax.axis_size(axis).bit_length() - 1


def gather_in(rows, section, axis):
    size = lax.axis_size(axis)
    return [rows] + [swap_in(rows, section, axis, k) for k in range(1, size)]


def gather(rows, axis):
    return [rows] + [swap(rows, axis, k) for k in range(1, lax.axis_size(axis))]


def scatter_sum(start, terms, source, block):
    total = start.astype(jnp.float32)
    for k in range(lax.axis_size("tensor")):
        arrived = across(terms[k * block : (k + 1) * block], source, k)
        total = total + arrived.astype(jnp.float32)
    return total.astype(jnp.bfloat16)


def load_kernel(*refs):
    count = (len(refs) - 1) // 2
    copies = [
        pltpu.make_async_copy(refs[i].at[0], refs[count + i], refs[-1].at[i])
        for i in range(count)
    ]
    for copy in copies:
        copy.start()
    for copy in copies:
        copy.wait()


def load_weights(*weights):
    total = sum(w.size * 2 for w in weights)
    weights = [pltpu.with_memory_space_constraint(w, pltpu.HBM) for w in weights]
    return pl.pallas_call(
        load_kernel,
        in_specs=[pl.BlockSpec(memory_space=pltpu.HBM)] * len(weights),
        out_specs=[pl.BlockSpec(memory_space=pltpu.VMEM)] * len(weights),
        out_shape=[pltpu.VMEM(w.shape[1:], w.dtype) for w in weights],
        scratch_shapes=[pltpu.SemaphoreType.DMA((len(weights),))],
        compiler_params=pltpu.CompilerParams(vmem_limit_bytes=total + 2**20),
        cost_estimate=pl.CostEstimate(flops=0, bytes_accessed=total, transcendentals=0),
    )(*weights)


def gradient_kernel(ids_ref, hidden_ref, y_ref, *rest):
    out_ref, masked = rest[-2:]
    piece = y_ref.shape[1]

    @pl.when(pl.program_id(0) == 0)
    def _():
        for e in range(DOMAINS):
            keep = ids_ref[...] == e
            masked[:, e * piece : (e + 1) * piece] = jnp.where(
                keep, y_ref[...].astype(jnp.float32), 0.0
            ).astype(jnp.bfloat16)

    product = lax.dot_general(
        hidden_ref[...], masked[...], CONTRACT_FIRST, preferred_element_type=jnp.float32
    )
    for e in range(DOMAINS):
        out_ref[e] = product[:, e * piece : (e + 1) * piece].astype(jnp.bfloat16)


def domain_gradients(row_ids, hidden, y, begin, count, grads=None):
    rows, units = hidden.shape
    piece = y.shape[1]
    in_specs = [
        pl.BlockSpec((rows, 1), lambda i: (0, 0)),
        pl.BlockSpec((rows, TILE), lambda i: (0, begin + i)),
        pl.BlockSpec((rows, piece), lambda i: (0, 0)),
    ]
    operands = [row_ids, hidden, y]
    if grads is not None:
        in_specs.append(pl.BlockSpec(memory_space=pl.ANY))
        operands.append(grads)
    return pl.pallas_call(
        gradient_kernel,
        grid=(count,),
        in_specs=in_specs,
        out_specs=pl.BlockSpec((DOMAINS, TILE, piece), lambda i: (0, begin + i, 0)),
        out_shape=jax.ShapeDtypeStruct((DOMAINS, units, piece), jnp.bfloat16),
        scratch_shapes=[pltpu.VMEM((rows, DOMAINS * piece), jnp.bfloat16)],
        input_output_aliases={} if grads is None else {3: 0},
        compiler_params=pltpu.CompilerParams(vmem_limit_bytes=24 * 2**20),
        cost_estimate=pl.CostEstimate(
            flops=2 * rows * count * TILE * DOMAINS * piece,
            bytes_accessed=2 * count * TILE * (rows + DOMAINS * piece),
            transcendentals=0,
        ),
    )(*operands)


def assemble_kernel(count, flag_ref, *refs):
    pieces = refs[: 2 * count]
    hidden_ref, gram_ref, sems = refs[2 * count :]
    rows = pieces[0].shape[0]
    for section in range(2):

        @pl.when(flag_ref[0] == section)
        def _(section=section):
            copies = [
                pltpu.make_async_copy(
                    pieces[section * count + k],
                    hidden_ref.at[pl.ds(k * rows, rows)],
                    sems.at[k],
                )
                for k in range(count)
            ]
            for copy in copies:
                copy.start()
            for copy in copies:
                copy.wait()

    total = rows * count
    step = min(total, 512)
    for begin in range(0, total, step):
        gram_ref[begin : begin + step, :] = lax.dot_general(
            hidden_ref[begin : begin + step, :],
            hidden_ref[...],
            CONTRACT_LAST,
            preferred_element_type=jnp.float32,
        )


def assemble(segment, pieces0, pieces1):
    count = len(pieces0)
    rows, units = pieces0[0].shape
    total = rows * count
    pieces = [pltpu.with_memory_space_constraint(p, pltpu.HBM) for p in pieces0 + pieces1]
    return pl.pallas_call(
        functools.partial(assemble_kernel, count),
        in_specs=[pl.BlockSpec(memory_space=pltpu.SMEM)]
        + [pl.BlockSpec(memory_space=pl.ANY)] * (2 * count),
        out_specs=[pl.BlockSpec(memory_space=pltpu.VMEM)] * 2,
        out_shape=[
            jax.ShapeDtypeStruct((total, units), jnp.bfloat16),
            jax.ShapeDtypeStruct((total, total), jnp.float32),
        ],
        scratch_shapes=[pltpu.SemaphoreType.DMA((count,))],
        compiler_params=pltpu.CompilerParams(
            vmem_limit_bytes=2 * total * units + 4 * total * total + 4 * 2**20
        ),
        cost_estimate=pl.CostEstimate(
            flops=2 * total * total * units,
            bytes_accessed=4 * total * units + 4 * total * total,
            transcendentals=0,
        ),
    )(segment.reshape(1), *pieces)


def norms_kernel(replicas, levels, ids_ref, ids_row_ref, gram_ref, *refs):
    *parts, y_ref, norms_ref, acc = refs
    block = parts[0].shape[0] // replicas
    tok_rows = block * len(parts)
    for t, part in enumerate(parts):
        for k in range(replicas):
            y_ref[k * tok_rows + t * block : k * tok_rows + (t + 1) * block, :] = part[
                k * block : (k + 1) * block, :
            ]
    acc[...] = jnp.zeros_like(acc)
    lane = lax.broadcasted_iota(jnp.int32, (1, acc.shape[1]), 1)
    for k in range(replicas):
        columns = slice(k * tok_rows, (k + 1) * tok_rows)
        gram_y = lax.dot_general(
            y_ref[...], y_ref[columns, :], CONTRACT_LAST, preferred_element_type=jnp.float32
        )
        pairs = jnp.where(ids_ref[...] == ids_row_ref[:, columns], gram_ref[:, columns] * gram_y, 0.0)
        of_row = jnp.sum(pairs, axis=1, keepdims=True)
        for level in range(levels):
            begin = (k >> level << level) * tok_rows
            end = begin + (tok_rows << level)
            acc[begin:end, :] += jnp.where(lane == level, of_row[begin:end], 0.0)
    for e in range(DOMAINS):
        norms_ref[e : e + 1, :] = jnp.sum(
            jnp.where(ids_ref[...] == e, acc[...], 0.0), axis=0, keepdims=True
        )
    norms_ref[DOMAINS:, :] = jnp.zeros_like(norms_ref[DOMAINS:, :])


def norm_sums(row_ids, gram_hidden, parts, replicas, levels):
    total = gram_hidden.shape[0]
    piece = parts[0].shape[1]
    return pl.pallas_call(
        functools.partial(norms_kernel, replicas, levels),
        in_specs=[pl.BlockSpec(memory_space=pltpu.VMEM)] * (3 + len(parts)),
        out_specs=[pl.BlockSpec(memory_space=pltpu.VMEM)] * 2,
        out_shape=[
            jax.ShapeDtypeStruct((total, piece), jnp.bfloat16),
            jax.ShapeDtypeStruct((8, 128), jnp.float32),
        ],
        scratch_shapes=[pltpu.VMEM((total, 128), jnp.float32)],
        compiler_params=pltpu.CompilerParams(
            vmem_limit_bytes=8 * total * piece + 4 * total * total + 1024 * total * 4 + 8 * 2**20
        ),
        cost_estimate=pl.CostEstimate(
            flops=2 * total * total * piece + 4 * total * total,
            bytes_accessed=4 * total * piece + 4 * total * total,
            transcendentals=0,
        ),
    )(row_ids, row_ids.reshape(1, total), gram_hidden, *parts)


def shards(layer_input_activations, cotangent, domain_ids, norm_gain, w_gate, w_up, w_down):
    segment = lax.axis_index("section")
    dp_index = lax.axis_index("dp")
    segments = lax.axis_size("section")
    tensor_size = lax.axis_size("tensor")
    dp_size = lax.axis_size("dp")
    assert segments == 2
    micro, local_rows, width = layer_input_activations.shape
    gain = norm_gain[0][None, :]
    gate_w, up_w, down_w = load_weights(w_gate, w_up, w_down)
    units = down_w.shape[0]
    block = micro * local_rows
    tok_rows = block * tensor_size
    first = segment == 0

    x_own = layer_input_activations.reshape(block, width)
    cot_own = cotangent.reshape(block, width)
    rows_in = jnp.concatenate(gather(jnp.where(first, x_own, cot_own), "tensor"), axis=0)

    def layer_parts(rows):
        widened = rows.astype(jnp.float32)
        scale = lax.rsqrt(jnp.mean(widened * widened, axis=-1, keepdims=True) + EPS)
        normed = (widened * scale * gain).astype(jnp.bfloat16)
        gate = jnp.dot(normed, gate_w, preferred_element_type=jnp.float32)
        up = jnp.dot(normed, up_w, preferred_element_type=jnp.float32)
        return widened, scale, gate, up

    _, _, gate0, up0 = layer_parts(rows_in)
    hidden0 = (jax.nn.silu(gate0) * up0).astype(jnp.bfloat16)
    mixed = jnp.dot(hidden0, down_w, preferred_element_type=jnp.float32).astype(jnp.bfloat16)
    cot_rows, hidden0, mixed = lax.optimization_barrier((rows_in, hidden0, mixed))
    d_hidden = lax.dot_general(cot_rows, down_w, CONTRACT_LAST, preferred_element_type=jnp.float32)
    x1_own = scatter_sum(x_own, mixed, 0, block)
    x1_own, d_hidden = lax.optimization_barrier((x1_own, d_hidden))
    x1 = jnp.concatenate(gather_in(x1_own, 1, "tensor"), axis=0)
    x1, hidden0 = lax.optimization_barrier((x1, hidden0))
    pieces0 = gather_in(hidden0, 0, "dp")

    widened, scale, gate, up = layer_parts(x1)
    sig = jax.nn.sigmoid(gate)
    hidden1 = (gate * sig * up).astype(jnp.bfloat16)
    d_gate = (d_hidden * up * (sig * (1.0 + gate * (1.0 - sig)))).astype(jnp.bfloat16)
    d_up = (d_hidden * gate * sig).astype(jnp.bfloat16)
    d_gate, d_up = lax.optimization_barrier((d_gate, d_up))
    d_normed = lax.dot_general(d_gate, gate_w, CONTRACT_LAST, preferred_element_type=jnp.float32)
    d_normed = d_normed + lax.dot_general(
        d_up, up_w, CONTRACT_LAST, preferred_element_type=jnp.float32
    )
    pulled = d_normed * gain
    along = jnp.sum(pulled * widened, axis=-1, keepdims=True) / width
    term = (pulled * scale - widened * (scale * scale * scale * along)).astype(jnp.bfloat16)
    term, pieces0 = lax.optimization_barrier((term, pieces0))
    dy_own = scatter_sum(cot_own, term, 1, block)
    dy_own = jnp.where(first, dy_own, cot_own)
    dy_own, hidden1 = lax.optimization_barrier((dy_own, hidden1))

    piece = width // dp_size
    id_rows = -(-micro // 16) * 16
    id_block = jnp.broadcast_to(
        jnp.pad(domain_ids.astype(jnp.bfloat16), ((0, id_rows - micro), (0, 0))), (id_rows, piece)
    )
    messages = []
    for k in range(dp_size):
        part = lax.dynamic_slice_in_dim(dy_own, (dp_index ^ k) * piece, piece, axis=1)
        part = jnp.concatenate([part, id_block], axis=0)
        messages.append(part if k == 0 else swap(part, "dp", k))
    pieces1 = gather_in(hidden1, 1, "dp")
    columns = jnp.concatenate([message[:block] for message in messages], axis=0)
    columns, pieces1 = lax.optimization_barrier((columns, pieces1))
    parts_y = gather(columns, "tensor")
    hidden_all, gram_hidden = assemble(segment, pieces0, pieces1)
    ids_all = jnp.stack([message[block : block + micro, 0] for message in messages])
    row_ids = jnp.broadcast_to(
        ids_all.astype(jnp.int32)[:, None, :, None], (dp_size, tensor_size, micro, local_rows)
    ).reshape(dp_size * tok_rows, 1)
    levels = dp_size.bit_length()
    y, norms = norm_sums(row_ids, gram_hidden, parts_y, dp_size, levels)
    rounds = [
        (axis, bit, min(2, bits(axis) - bit))
        for axis in ("tensor", "dp", "section")
        for bit in range(0, bits(axis), 2)
    ]
    tiles = units // TILE
    parts = min(len(rounds), tiles)
    grads = None
    begin = 0
    for part, (axis, bit, count) in enumerate(rounds):
        others = [swap(norms, axis, k << bit) for k in range(1, 1 << count)]
        if part < parts:
            end = tiles * (part + 1) // parts
            grads = domain_gradients(row_ids, hidden_all, y, begin, end - begin, grads)
            begin = end
        norms = norms + others[0]
        if count == 2:
            norms = norms + (others[1] + others[2])
        row_ids, norms = lax.optimization_barrier((row_ids, norms))
    entries = segments * units * tensor_size * width
    counts = [float((dp_size >> level) * entries) for level in range(levels)]
    return grads[None], norms[:DOMAINS, :levels] / jnp.array(counts, jnp.float32)[None, :]


def solution(mesh):
    return jax.shard_map(
        shards,
        mesh=mesh,
        in_specs=(
            P(None, ("dp", "tensor"), None),
            P(None, ("dp", "tensor"), None),
            P(None, "dp"),
            P("section", None),
            P("section", None, "tensor"),
            P("section", None, "tensor"),
            P("section", "tensor", None),
        ),
        out_specs=(P("section", None, "tensor", "dp"), P()),
        check_vma=False,
    )
```

```python
import functools

import jax
import jax.numpy as jnp
from jax import lax
from jax.experimental import pallas as pl
from jax.experimental.pallas import tpu as pltpu
from jax.sharding import PartitionSpec as P

DOMAINS = 4
TILE = 256
EPS = 1e-05
CONTRACT_LAST = (((1,), (1,)), ((), ()))
CONTRACT_FIRST = (((0,), (0,)), ((), ()))


def swap(block, axis, offset):
    size = lax.axis_size(axis)
    return lax.ppermute(block, axis, [(i, i ^ offset) for i in range(size)])


def swap_in(block, section, axis, offset):
    size = lax.axis_size(axis)
    route = [(section * size + i, section * size + (i ^ offset)) for i in range(size)]
    return lax.ppermute(block, ("section", axis), route)


def across(block, source, offset):
    size = lax.axis_size("tensor")
    route = [
        (source * size + i, (1 - source) * size + (i ^ offset)) for i in range(size)
    ]
    return lax.ppermute(block, ("section", "tensor"), route)


def bits(axis):
    return lax.axis_size(axis).bit_length() - 1


def gather_in(rows, section, axis):
    size = lax.axis_size(axis)
    return [rows] + [swap_in(rows, section, axis, k) for k in range(1, size)]


def gather(rows, axis):
    return [rows] + [swap(rows, axis, k) for k in range(1, lax.axis_size(axis))]


def scatter_sum(start, terms, source, block, rows):
    arrived = [
        across(terms[k * block : (k + 1) * block], source, k)
        for k in range(lax.axis_size("tensor"))
    ]
    others = []
    for k in range(1, lax.axis_size("dp")):
        near = 1 if k == 1 and source == 0 else 0
        if k == 1 and source == 1:
            late = None
            others.append(late)
            continue
        late, arrived[near] = lax.optimization_barrier((rows, arrived[near]))
        others.append(swap_in(late, source, "dp", k))
    total = start.astype(jnp.float32)
    for value in arrived:
        total = total + value.astype(jnp.float32)
    total = total.astype(jnp.bfloat16)
    if others[0] is None:
        late, total = lax.optimization_barrier((rows, total))
        others[0] = swap_in(late, source, "dp", 1)
    return total, [rows] + others


def load_kernel(*refs):
    count = (len(refs) - 1) // 2
    copies = [
        pltpu.make_async_copy(refs[i].at[0], refs[count + i], refs[-1].at[i])
        for i in range(count)
    ]
    for copy in copies:
        copy.start()
    for copy in copies:
        copy.wait()


def load_weights(*weights):
    total = sum(w.size * 2 for w in weights)
    weights = [pltpu.with_memory_space_constraint(w, pltpu.HBM) for w in weights]
    return pl.pallas_call(
        load_kernel,
        in_specs=[pl.BlockSpec(memory_space=pltpu.HBM)] * len(weights),
        out_specs=[pl.BlockSpec(memory_space=pltpu.VMEM)] * len(weights),
        out_shape=[pltpu.VMEM(w.shape[1:], w.dtype) for w in weights],
        scratch_shapes=[pltpu.SemaphoreType.DMA((len(weights),))],
        compiler_params=pltpu.CompilerParams(vmem_limit_bytes=total + 2**20),
        cost_estimate=pl.CostEstimate(flops=0, bytes_accessed=total, transcendentals=0),
    )(*weights)


def gradient_kernel(ids_ref, hidden_ref, y_ref, *rest):
    out_ref, masked = rest[-2:]
    piece = y_ref.shape[1]

    @pl.when(pl.program_id(0) == 0)
    def _():
        for e in range(DOMAINS):
            keep = ids_ref[...] == e
            masked[:, e * piece : (e + 1) * piece] = jnp.where(
                keep, y_ref[...].astype(jnp.float32), 0.0
            ).astype(jnp.bfloat16)

    product = lax.dot_general(
        hidden_ref[...], masked[...], CONTRACT_FIRST, preferred_element_type=jnp.float32
    )
    for e in range(DOMAINS):
        out_ref[e] = product[:, e * piece : (e + 1) * piece].astype(jnp.bfloat16)


def domain_gradients(row_ids, hidden, y, begin, count, grads=None):
    rows, units = hidden.shape
    piece = y.shape[1]
    in_specs = [
        pl.BlockSpec((rows, 1), lambda i: (0, 0)),
        pl.BlockSpec((rows, TILE), lambda i: (0, begin + i)),
        pl.BlockSpec((rows, piece), lambda i: (0, 0)),
    ]
    operands = [row_ids, hidden, y]
    if grads is not None:
        in_specs.append(pl.BlockSpec(memory_space=pl.ANY))
        operands.append(grads)
    return pl.pallas_call(
        gradient_kernel,
        grid=(count,),
        in_specs=in_specs,
        out_specs=pl.BlockSpec((DOMAINS, TILE, piece), lambda i: (0, begin + i, 0)),
        out_shape=jax.ShapeDtypeStruct((DOMAINS, units, piece), jnp.bfloat16),
        scratch_shapes=[pltpu.VMEM((rows, DOMAINS * piece), jnp.bfloat16)],
        input_output_aliases={} if grads is None else {3: 0},
        compiler_params=pltpu.CompilerParams(vmem_limit_bytes=24 * 2**20),
        cost_estimate=pl.CostEstimate(
            flops=2 * rows * count * TILE * DOMAINS * piece,
            bytes_accessed=2 * count * TILE * (rows + DOMAINS * piece),
            transcendentals=0,
        ),
    )(*operands)


def assemble_kernel(count, flag_ref, *refs):
    pieces = refs[: 2 * count]
    hidden_ref, gram_ref, sems = refs[2 * count :]
    rows = pieces[0].shape[0]
    for section in range(2):

        @pl.when(flag_ref[0] == section)
        def _(section=section):
            copies = [
                pltpu.make_async_copy(
                    pieces[section * count + k],
                    hidden_ref.at[pl.ds(k * rows, rows)],
                    sems.at[k],
                )
                for k in range(count)
            ]
            for copy in copies:
                copy.start()
            for copy in copies:
                copy.wait()

    total = rows * count
    step = min(total, 512)
    for begin in range(0, total, step):
        gram_ref[begin : begin + step, :] = lax.dot_general(
            hidden_ref[begin : begin + step, :],
            hidden_ref[...],
            CONTRACT_LAST,
            preferred_element_type=jnp.float32,
        )


def assemble(segment, pieces0, pieces1):
    count = len(pieces0)
    rows, units = pieces0[0].shape
    total = rows * count
    pieces = [pltpu.with_memory_space_constraint(p, pltpu.HBM) for p in pieces0 + pieces1]
    return pl.pallas_call(
        functools.partial(assemble_kernel, count),
        in_specs=[pl.BlockSpec(memory_space=pltpu.SMEM)]
        + [pl.BlockSpec(memory_space=pl.ANY)] * (2 * count),
        out_specs=[pl.BlockSpec(memory_space=pltpu.VMEM)] * 2,
        out_shape=[
            jax.ShapeDtypeStruct((total, units), jnp.bfloat16),
            jax.ShapeDtypeStruct((total, total), jnp.float32),
        ],
        scratch_shapes=[pltpu.SemaphoreType.DMA((count,))],
        compiler_params=pltpu.CompilerParams(
            vmem_limit_bytes=2 * total * units + 4 * total * total + 4 * 2**20
        ),
        cost_estimate=pl.CostEstimate(
            flops=2 * total * total * units,
            bytes_accessed=4 * total * units + 4 * total * total,
            transcendentals=0,
        ),
    )(segment.reshape(1), *pieces)


def norms_kernel(replicas, levels, ids_ref, ids_row_ref, gram_ref, *refs):
    *parts, y_ref, norms_ref, acc = refs
    block = parts[0].shape[0] // replicas
    tok_rows = block * len(parts)
    for t, part in enumerate(parts):
        for k in range(replicas):
            y_ref[k * tok_rows + t * block : k * tok_rows + (t + 1) * block, :] = part[
                k * block : (k + 1) * block, :
            ]
    acc[...] = jnp.zeros_like(acc)
    lane = lax.broadcasted_iota(jnp.int32, (1, acc.shape[1]), 1)
    for k in range(replicas):
        columns = slice(k * tok_rows, (k + 1) * tok_rows)
        gram_y = lax.dot_general(
            y_ref[...], y_ref[columns, :], CONTRACT_LAST, preferred_element_type=jnp.float32
        )
        pairs = jnp.where(ids_ref[...] == ids_row_ref[:, columns], gram_ref[:, columns] * gram_y, 0.0)
        of_row = jnp.sum(pairs, axis=1, keepdims=True)
        for level in range(levels):
            begin = (k >> level << level) * tok_rows
            end = begin + (tok_rows << level)
            acc[begin:end, :] += jnp.where(lane == level, of_row[begin:end], 0.0)
    for e in range(DOMAINS):
        norms_ref[e : e + 1, :] = jnp.sum(
            jnp.where(ids_ref[...] == e, acc[...], 0.0), axis=0, keepdims=True
        )
    norms_ref[DOMAINS:, :] = jnp.zeros_like(norms_ref[DOMAINS:, :])


def norm_sums(row_ids, gram_hidden, parts, replicas, levels):
    total = gram_hidden.shape[0]
    piece = parts[0].shape[1]
    return pl.pallas_call(
        functools.partial(norms_kernel, replicas, levels),
        in_specs=[pl.BlockSpec(memory_space=pltpu.VMEM)] * (3 + len(parts)),
        out_specs=[pl.BlockSpec(memory_space=pltpu.VMEM)] * 2,
        out_shape=[
            jax.ShapeDtypeStruct((total, piece), jnp.bfloat16),
            jax.ShapeDtypeStruct((8, 128), jnp.float32),
        ],
        scratch_shapes=[pltpu.VMEM((total, 128), jnp.float32)],
        compiler_params=pltpu.CompilerParams(
            vmem_limit_bytes=8 * total * piece + 4 * total * total + 1024 * total * 4 + 8 * 2**20
        ),
        cost_estimate=pl.CostEstimate(
            flops=2 * total * total * piece + 4 * total * total,
            bytes_accessed=4 * total * piece + 4 * total * total,
            transcendentals=0,
        ),
    )(row_ids, row_ids.reshape(1, total), gram_hidden, *parts)


def shards(layer_input_activations, cotangent, domain_ids, norm_gain, w_gate, w_up, w_down):
    segment = lax.axis_index("section")
    dp_index = lax.axis_index("dp")
    segments = lax.axis_size("section")
    tensor_size = lax.axis_size("tensor")
    dp_size = lax.axis_size("dp")
    assert segments == 2
    micro, local_rows, width = layer_input_activations.shape
    gain = norm_gain[0][None, :]
    gate_w, up_w, down_w = load_weights(w_gate, w_up, w_down)
    units = down_w.shape[0]
    block = micro * local_rows
    tok_rows = block * tensor_size
    first = segment == 0

    x_own = layer_input_activations.reshape(block, width)
    cot_own = cotangent.reshape(block, width)
    rows_in = jnp.concatenate(gather(jnp.where(first, x_own, cot_own), "tensor"), axis=0)

    def layer_parts(rows):
        widened = rows.astype(jnp.float32)
        scale = lax.rsqrt(jnp.mean(widened * widened, axis=-1, keepdims=True) + EPS)
        normed = (widened * scale * gain).astype(jnp.bfloat16)
        gate = jnp.dot(normed, gate_w, preferred_element_type=jnp.float32)
        up = jnp.dot(normed, up_w, preferred_element_type=jnp.float32)
        return widened, scale, gate, up

    _, _, gate0, up0 = layer_parts(rows_in)
    hidden0 = (jax.nn.silu(gate0) * up0).astype(jnp.bfloat16)
    mixed = jnp.dot(hidden0, down_w, preferred_element_type=jnp.float32).astype(jnp.bfloat16)
    cot_rows, hidden0, mixed = lax.optimization_barrier((rows_in, hidden0, mixed))
    d_hidden = lax.dot_general(cot_rows, down_w, CONTRACT_LAST, preferred_element_type=jnp.float32)
    x1_own, pieces0 = scatter_sum(x_own, mixed, 0, block, hidden0)
    x1_own, d_hidden = lax.optimization_barrier((x1_own, d_hidden))
    x1 = jnp.concatenate(gather_in(x1_own, 1, "tensor"), axis=0)

    widened, scale, gate, up = layer_parts(x1)
    sig = jax.nn.sigmoid(gate)
    hidden1 = (gate * sig * up).astype(jnp.bfloat16)
    d_gate = (d_hidden * up * (sig * (1.0 + gate * (1.0 - sig)))).astype(jnp.bfloat16)
    d_up = (d_hidden * gate * sig).astype(jnp.bfloat16)
    d_gate, d_up = lax.optimization_barrier((d_gate, d_up))
    d_normed = lax.dot_general(d_gate, gate_w, CONTRACT_LAST, preferred_element_type=jnp.float32)
    d_normed = d_normed + lax.dot_general(
        d_up, up_w, CONTRACT_LAST, preferred_element_type=jnp.float32
    )
    pulled = d_normed * gain
    along = jnp.sum(pulled * widened, axis=-1, keepdims=True) / width
    term = (pulled * scale - widened * (scale * scale * scale * along)).astype(jnp.bfloat16)
    term, pieces0 = lax.optimization_barrier((term, pieces0))
    dy_own, pieces1 = scatter_sum(cot_own, term, 1, block, hidden1)
    dy_own = jnp.where(first, dy_own, cot_own)

    piece = width // dp_size
    id_rows = -(-micro // 16) * 16
    id_block = jnp.broadcast_to(
        jnp.pad(domain_ids.astype(jnp.bfloat16), ((0, id_rows - micro), (0, 0))), (id_rows, piece)
    )
    messages = []
    for k in range(dp_size):
        part = lax.dynamic_slice_in_dim(dy_own, (dp_index ^ k) * piece, piece, axis=1)
        part = jnp.concatenate([part, id_block], axis=0)
        messages.append(part if k == 0 else swap(part, "dp", k))
    columns = jnp.concatenate([message[:block] for message in messages], axis=0)
    columns, pieces1[1] = lax.optimization_barrier((columns, pieces1[1]))
    parts_y = gather(columns, "tensor")
    hidden_all, gram_hidden = assemble(segment, pieces0, pieces1)
    ids_all = jnp.stack([message[block : block + micro, 0] for message in messages])
    row_ids = jnp.broadcast_to(
        ids_all.astype(jnp.int32)[:, None, :, None], (dp_size, tensor_size, micro, local_rows)
    ).reshape(dp_size * tok_rows, 1)
    levels = dp_size.bit_length()
    y, norms = norm_sums(row_ids, gram_hidden, parts_y, dp_size, levels)
    rounds = [
        (axis, bit, min(2, bits(axis) - bit))
        for axis in ("tensor", "dp", "section")
        for bit in range(0, bits(axis), 2)
    ]
    tiles = units // TILE
    parts = min(len(rounds), tiles)
    grads = None
    begin = 0
    for part, (axis, bit, count) in enumerate(rounds):
        others = [swap(norms, axis, k << bit) for k in range(1, 1 << count)]
        if part < parts:
            end = tiles * (part + 1) // parts
            grads = domain_gradients(row_ids, hidden_all, y, begin, end - begin, grads)
            begin = end
        norms = norms + others[0]
        if count == 2:
            norms = norms + (others[1] + others[2])
        row_ids, norms = lax.optimization_barrier((row_ids, norms))
    entries = segments * units * tensor_size * width
    counts = [float((dp_size >> level) * entries) for level in range(levels)]
    return grads[None], norms[:DOMAINS, :levels] / jnp.array(counts, jnp.float32)[None, :]


def solution(mesh):
    return jax.shard_map(
        shards,
        mesh=mesh,
        in_specs=(
            P(None, ("dp", "tensor"), None),
            P(None, ("dp", "tensor"), None),
            P(None, "dp"),
            P("section", None),
            P("section", None, "tensor"),
            P("section", None, "tensor"),
            P("section", "tensor", None),
        ),
        out_specs=(P("section", None, "tensor", "dp"), P()),
        check_vma=False,
    )
```

```python
import functools

import jax
import jax.numpy as jnp
from jax import lax
from jax.experimental import pallas as pl
from jax.experimental.pallas import tpu as pltpu
from jax.sharding import PartitionSpec as P

DOMAINS = 4
TILE = 256
EPS = 1e-05
CONTRACT_LAST = (((1,), (1,)), ((), ()))
CONTRACT_FIRST = (((0,), (0,)), ((), ()))


def swap(block, axis, offset):
    size = lax.axis_size(axis)
    return lax.ppermute(block, axis, [(i, i ^ offset) for i in range(size)])


def swap_in(block, section, axis, offset):
    size = lax.axis_size(axis)
    route = [(section * size + i, section * size + (i ^ offset)) for i in range(size)]
    return lax.ppermute(block, ("section", axis), route)


def across(block, source, offset):
    size = lax.axis_size("tensor")
    route = [
        (source * size + i, (1 - source) * size + (i ^ offset)) for i in range(size)
    ]
    return lax.ppermute(block, ("section", "tensor"), route)


def bits(axis):
    return lax.axis_size(axis).bit_length() - 1


def gather_in(rows, section, axis):
    size = lax.axis_size(axis)
    return [rows] + [swap_in(rows, section, axis, k) for k in range(1, size)]


def gather(rows, axis):
    return [rows] + [swap(rows, axis, k) for k in range(1, lax.axis_size(axis))]


def scatter_sum(start, terms, source, block, rows):
    arrived = [
        across(terms[k * block : (k + 1) * block], source, k)
        for k in range(lax.axis_size("tensor"))
    ]
    others = []
    if source == 1:
        for k in range(2, lax.axis_size("dp")):
            early, arrived[0] = lax.optimization_barrier((rows, arrived[0]))
            others.append(swap_in(early, source, "dp", k))
    total = start.astype(jnp.float32)
    for value in arrived:
        total = total + value.astype(jnp.float32)
    total = total.astype(jnp.bfloat16)
    late, total = lax.optimization_barrier((rows, total))
    if source == 0:
        return total, gather_in(late, source, "dp")
    return total, [rows, swap_in(late, source, "dp", 1)] + others


def load_kernel(gate_in, up_in, down_in, gate, up, down, gate_t, sems):
    width = gate.shape[0]
    pieces = [(begin, min(256, width - begin)) for begin in range(0, width, 256)]
    copies = []
    for number, (begin, count) in enumerate(pieces):
        rows = pl.ds(begin, count)
        copies.append(pltpu.make_async_copy(gate_in.at[0, rows], gate.at[rows], sems.at[2 + number]))
    rest = [
        pltpu.make_async_copy(up_in.at[0], up, sems.at[0]),
        pltpu.make_async_copy(down_in.at[0], down, sems.at[1]),
    ]
    for copy in copies + rest:
        copy.start()
    for copy, (begin, count) in zip(copies, pieces):
        copy.wait()
        gate_t[:, begin : begin + count] = gate[begin : begin + count, :].T
    for copy in rest:
        copy.wait()


def load_weights(w_gate, w_up, w_down):
    _, width, units = w_gate.shape
    weights = [pltpu.with_memory_space_constraint(w, pltpu.HBM) for w in (w_gate, w_up, w_down)]
    shapes = [(width, units), (width, units), (units, width), (units, width)]
    return pl.pallas_call(
        load_kernel,
        in_specs=[pl.BlockSpec(memory_space=pltpu.HBM)] * 3,
        out_specs=[pl.BlockSpec(memory_space=pltpu.VMEM)] * 4,
        out_shape=[pltpu.VMEM(shape, jnp.bfloat16) for shape in shapes],
        scratch_shapes=[pltpu.SemaphoreType.DMA((2 + -(-width // 256),))],
        compiler_params=pltpu.CompilerParams(vmem_limit_bytes=4 * 2**20),
        cost_estimate=pl.CostEstimate(
            flops=0, bytes_accessed=6 * width * units, transcendentals=0
        ),
    )(*weights)


def hidden_grad_kernel(flag_ref, rows_ref, down_ref, out_ref):
    units = down_ref.shape[0]

    @pl.when(flag_ref[0] == 1)
    def _():
        for begin in range(0, units, TILE):
            out_ref[:, begin : begin + TILE] = lax.dot_general(
                rows_ref[...],
                down_ref[begin : begin + TILE, :],
                CONTRACT_LAST,
                preferred_element_type=jnp.float32,
            )

    @pl.when(flag_ref[0] == 0)
    def _():
        out_ref[...] = jnp.zeros_like(out_ref)


def hidden_grad(segment, rows, down_w):
    units, width = down_w.shape
    return pl.pallas_call(
        hidden_grad_kernel,
        in_specs=[pl.BlockSpec(memory_space=pltpu.SMEM)]
        + [pl.BlockSpec(memory_space=pltpu.VMEM)] * 2,
        out_specs=pl.BlockSpec(memory_space=pltpu.VMEM),
        out_shape=jax.ShapeDtypeStruct((rows.shape[0], units), jnp.float32),
        compiler_params=pltpu.CompilerParams(vmem_limit_bytes=16 * 2**20),
        cost_estimate=pl.CostEstimate(
            flops=2 * rows.shape[0] * units * width,
            bytes_accessed=2 * units * width,
            transcendentals=0,
        ),
    )(segment.reshape(1), rows, down_w)


def gradient_kernel(hidden_ref, masked_ref, *rest):
    out_ref = rest[-1]
    piece = out_ref.shape[2]
    product = lax.dot_general(
        hidden_ref[...], masked_ref[...], CONTRACT_FIRST, preferred_element_type=jnp.float32
    )
    for e in range(DOMAINS):
        out_ref[e] = product[:, e * piece : (e + 1) * piece].astype(jnp.bfloat16)


def domain_gradients(hidden, masked, begin, count, grads=None):
    rows, units = hidden.shape
    columns = masked.shape[1]
    piece = columns // DOMAINS
    in_specs = [
        pl.BlockSpec((rows, TILE), lambda i: (0, begin + i)),
        pl.BlockSpec(memory_space=pltpu.VMEM),
    ]
    operands = [hidden, masked]
    if grads is not None:
        in_specs.append(pl.BlockSpec(memory_space=pl.ANY))
        operands.append(grads)
    return pl.pallas_call(
        gradient_kernel,
        grid=(count,),
        in_specs=in_specs,
        out_specs=pl.BlockSpec((DOMAINS, TILE, piece), lambda i: (0, begin + i, 0)),
        out_shape=jax.ShapeDtypeStruct((DOMAINS, units, piece), jnp.bfloat16),
        input_output_aliases={} if grads is None else {2: 0},
        compiler_params=pltpu.CompilerParams(vmem_limit_bytes=16 * 2**20),
        cost_estimate=pl.CostEstimate(
            flops=2 * rows * count * TILE * columns,
            bytes_accessed=2 * count * TILE * (rows + columns),
            transcendentals=0,
        ),
    )(*operands)


def assemble_kernel(count, flag_ref, *refs):
    pieces = refs[: 2 * count]
    hidden_ref, gram_ref, sems = refs[2 * count :]
    rows = pieces[0].shape[0]
    for section in range(2):

        @pl.when(flag_ref[0] == section)
        def _(section=section):
            copies = [
                pltpu.make_async_copy(
                    pieces[section * count + k],
                    hidden_ref.at[pl.ds(k * rows, rows)],
                    sems.at[k],
                )
                for k in range(count)
            ]
            for copy in copies:
                copy.start()
            for copy in copies:
                copy.wait()

    total = rows * count
    step = min(total, 512)
    for begin in range(0, total, step):
        gram_ref[begin : begin + step, :] = lax.dot_general(
            hidden_ref[begin : begin + step, :],
            hidden_ref[...],
            CONTRACT_LAST,
            preferred_element_type=jnp.float32,
        )


def assemble(segment, pieces0, pieces1):
    count = len(pieces0)
    rows, units = pieces0[0].shape
    total = rows * count
    pieces = [pltpu.with_memory_space_constraint(p, pltpu.HBM) for p in pieces0 + pieces1]
    return pl.pallas_call(
        functools.partial(assemble_kernel, count),
        in_specs=[pl.BlockSpec(memory_space=pltpu.SMEM)]
        + [pl.BlockSpec(memory_space=pl.ANY)] * (2 * count),
        out_specs=[pl.BlockSpec(memory_space=pltpu.VMEM)] * 2,
        out_shape=[
            jax.ShapeDtypeStruct((total, units), jnp.bfloat16),
            jax.ShapeDtypeStruct((total, total), jnp.float32),
        ],
        scratch_shapes=[pltpu.SemaphoreType.DMA((count,))],
        compiler_params=pltpu.CompilerParams(
            vmem_limit_bytes=2 * total * units + 4 * total * total + 4 * 2**20
        ),
        cost_estimate=pl.CostEstimate(
            flops=2 * total * total * units,
            bytes_accessed=4 * total * units + 4 * total * total,
            transcendentals=0,
        ),
    )(segment.reshape(1), *pieces)


def norms_kernel(replicas, levels, ids_ref, ids_row_ref, gram_ref, *refs):
    *parts, masked_ref, norms_ref, y_ref, acc = refs
    piece = y_ref.shape[1]
    block = parts[0].shape[0] // replicas
    tok_rows = block * len(parts)
    for t, part in enumerate(parts):
        for k in range(replicas):
            y_ref[k * tok_rows + t * block : k * tok_rows + (t + 1) * block, :] = part[
                k * block : (k + 1) * block, :
            ]
    for e in range(DOMAINS):
        masked_ref[:, e * piece : (e + 1) * piece] = jnp.where(
            ids_ref[...] == e, y_ref[...].astype(jnp.float32), 0.0
        ).astype(jnp.bfloat16)
    acc[...] = jnp.zeros_like(acc)
    lane = lax.broadcasted_iota(jnp.int32, (1, acc.shape[1]), 1)
    for k in range(replicas):
        columns = slice(k * tok_rows, (k + 1) * tok_rows)
        gram_y = lax.dot_general(
            y_ref[...], y_ref[columns, :], CONTRACT_LAST, preferred_element_type=jnp.float32
        )
        pairs = jnp.where(ids_ref[...] == ids_row_ref[:, columns], gram_ref[:, columns] * gram_y, 0.0)
        of_row = jnp.sum(pairs, axis=1, keepdims=True)
        for level in range(levels):
            begin = (k >> level << level) * tok_rows
            end = begin + (tok_rows << level)
            acc[begin:end, :] += jnp.where(lane == level, of_row[begin:end], 0.0)
    for e in range(DOMAINS):
        norms_ref[e : e + 1, :] = jnp.sum(
            jnp.where(ids_ref[...] == e, acc[...], 0.0), axis=0, keepdims=True
        )
    norms_ref[DOMAINS:, :] = jnp.zeros_like(norms_ref[DOMAINS:, :])


def norm_sums(row_ids, gram_hidden, parts, replicas, levels):
    total = gram_hidden.shape[0]
    piece = parts[0].shape[1]
    return pl.pallas_call(
        functools.partial(norms_kernel, replicas, levels),
        in_specs=[pl.BlockSpec(memory_space=pltpu.VMEM)] * (3 + len(parts)),
        out_specs=[pl.BlockSpec(memory_space=pltpu.VMEM)] * 2,
        out_shape=[
            pltpu.VMEM((total, DOMAINS * piece), jnp.bfloat16),
            jax.ShapeDtypeStruct((8, 128), jnp.float32),
        ],
        scratch_shapes=[
            pltpu.VMEM((total, piece), jnp.bfloat16),
            pltpu.VMEM((total, 128), jnp.float32),
        ],
        compiler_params=pltpu.CompilerParams(
            vmem_limit_bytes=8 * total * piece + 4 * total * total + 1024 * total * 4 + 8 * 2**20
        ),
        cost_estimate=pl.CostEstimate(
            flops=2 * total * total * piece + 4 * total * total,
            bytes_accessed=4 * total * piece + 4 * total * total,
            transcendentals=0,
        ),
    )(row_ids, row_ids.reshape(1, total), gram_hidden, *parts)


def shards(layer_input_activations, cotangent, domain_ids, norm_gain, w_gate, w_up, w_down):
    segment = lax.axis_index("section")
    dp_index = lax.axis_index("dp")
    segments = lax.axis_size("section")
    tensor_size = lax.axis_size("tensor")
    dp_size = lax.axis_size("dp")
    assert segments == 2
    micro, local_rows, width = layer_input_activations.shape
    gain = norm_gain[0][None, :]
    gate_w, up_w, down_w, gate_t = load_weights(w_gate, w_up, w_down)
    units = down_w.shape[0]
    block = micro * local_rows
    tok_rows = block * tensor_size
    first = segment == 0

    x_own = layer_input_activations.reshape(block, width)
    cot_own = cotangent.reshape(block, width)
    rows_in = jnp.concatenate(gather(jnp.where(first, x_own, cot_own), "tensor"), axis=0)

    def layer_parts(rows):
        widened = rows.astype(jnp.float32)
        scale = lax.rsqrt(jnp.mean(widened * widened, axis=-1, keepdims=True) + EPS)
        normed = (widened * scale * gain).astype(jnp.bfloat16)
        gate = jnp.dot(normed, gate_w, preferred_element_type=jnp.float32)
        up = jnp.dot(normed, up_w, preferred_element_type=jnp.float32)
        return widened, scale, gate, up

    _, _, gate0, up0 = layer_parts(rows_in)
    hidden0 = (jax.nn.silu(gate0) * up0).astype(jnp.bfloat16)
    mixed = jnp.dot(hidden0, down_w, preferred_element_type=jnp.float32).astype(jnp.bfloat16)
    cot_rows, hidden0, mixed = lax.optimization_barrier((rows_in, hidden0, mixed))
    d_hidden = hidden_grad(segment, cot_rows, down_w)
    x1_own, pieces0 = scatter_sum(x_own, mixed, 0, block, hidden0)
    x1_own, d_hidden = lax.optimization_barrier((x1_own, d_hidden))
    x1 = jnp.concatenate(gather_in(x1_own, 1, "tensor"), axis=0)

    widened, scale, gate, up = layer_parts(x1)
    sig = jax.nn.sigmoid(gate)
    hidden1 = (gate * sig * up).astype(jnp.bfloat16)
    d_gate = (d_hidden * up * (sig * (1.0 + gate * (1.0 - sig)))).astype(jnp.bfloat16)
    d_up = (d_hidden * gate * sig).astype(jnp.bfloat16)
    d_gate, d_up = lax.optimization_barrier((d_gate, d_up))
    d_normed = jnp.dot(d_gate, gate_t, preferred_element_type=jnp.float32)
    d_normed = d_normed + lax.dot_general(
        d_up, up_w, CONTRACT_LAST, preferred_element_type=jnp.float32
    )
    pulled = d_normed * gain
    along = jnp.sum(pulled * widened, axis=-1, keepdims=True) / width
    term = (pulled * scale - widened * (scale * scale * scale * along)).astype(jnp.bfloat16)
    term, pieces0 = lax.optimization_barrier((term, pieces0))
    dy_own, pieces1 = scatter_sum(cot_own, term, 1, block, hidden1)
    dy_own = jnp.where(first, dy_own, cot_own)

    piece = width // dp_size
    id_rows = -(-micro // 16) * 16
    id_block = jnp.broadcast_to(
        jnp.pad(domain_ids.astype(jnp.bfloat16), ((0, id_rows - micro), (0, 0))), (id_rows, piece)
    )
    messages = []
    for k in range(dp_size):
        part = lax.dynamic_slice_in_dim(dy_own, (dp_index ^ k) * piece, piece, axis=1)
        part = jnp.concatenate([part, id_block], axis=0)
        messages.append(part if k == 0 else swap(part, "dp", k))
    columns = jnp.concatenate([message[:block] for message in messages], axis=0)
    columns, pieces1[1] = lax.optimization_barrier((columns, pieces1[1]))
    parts_y = gather(columns, "tensor")
    hidden_all, gram_hidden = assemble(segment, pieces0, pieces1)
    ids_all = jnp.stack([message[block : block + micro, 0] for message in messages])
    row_ids = jnp.broadcast_to(
        ids_all.astype(jnp.int32)[:, None, :, None], (dp_size, tensor_size, micro, local_rows)
    ).reshape(dp_size * tok_rows, 1)
    levels = dp_size.bit_length()
    masked, norms = norm_sums(row_ids, gram_hidden, parts_y, dp_size, levels)
    rounds = [
        (axis, bit, min(2, bits(axis) - bit))
        for axis in ("tensor", "dp", "section")
        for bit in range(0, bits(axis), 2)
    ]
    tiles = units // TILE
    parts = min(len(rounds), tiles)
    grads = None
    begin = 0
    for part, (axis, bit, count) in enumerate(rounds):
        others = [swap(norms, axis, k << bit) for k in range(1, 1 << count)]
        if part < parts:
            end = tiles * (part + 1) // parts
            grads = domain_gradients(hidden_all, masked, begin, end - begin, grads)
            begin = end
        norms = norms + others[0]
        if count == 2:
            norms = norms + (others[1] + others[2])
        masked, norms = lax.optimization_barrier((masked, norms))
    entries = segments * units * tensor_size * width
    counts = [float((dp_size >> level) * entries) for level in range(levels)]
    return grads[None], norms[:DOMAINS, :levels] / jnp.array(counts, jnp.float32)[None, :]


def solution(mesh):
    return jax.shard_map(
        shards,
        mesh=mesh,
        in_specs=(
            P(None, ("dp", "tensor"), None),
            P(None, ("dp", "tensor"), None),
            P(None, "dp"),
            P("section", None),
            P("section", None, "tensor"),
            P("section", None, "tensor"),
            P("section", "tensor", None),
        ),
        out_specs=(P("section", None, "tensor", "dp"), P()),
        check_vma=False,
    )
```

```python
import functools

import jax
import jax.numpy as jnp
from jax import lax
from jax.experimental import pallas as pl
from jax.experimental.pallas import tpu as pltpu
from jax.sharding import PartitionSpec as P

DOMAINS = 4
TILE = 256
EPS = 1e-05
CONTRACT_LAST = (((1,), (1,)), ((), ()))
CONTRACT_FIRST = (((0,), (0,)), ((), ()))


def swap(block, axis, offset):
    size = lax.axis_size(axis)
    return lax.ppermute(block, axis, [(i, i ^ offset) for i in range(size)])


def swap_in(block, section, axis, offset):
    size = lax.axis_size(axis)
    route = [(section * size + i, section * size + (i ^ offset)) for i in range(size)]
    return lax.ppermute(block, ("section", axis), route)


def across(block, source, offset):
    size = lax.axis_size("tensor")
    route = [
        (source * size + i, (1 - source) * size + (i ^ offset)) for i in range(size)
    ]
    return lax.ppermute(block, ("section", "tensor"), route)


def bits(axis):
    return lax.axis_size(axis).bit_length() - 1


def gather_in(rows, section, axis):
    size = lax.axis_size(axis)
    return [rows] + [swap_in(rows, section, axis, k) for k in range(1, size)]


def gather(rows, axis):
    return [rows] + [swap(rows, axis, k) for k in range(1, lax.axis_size(axis))]


def scatter_sum(start, terms, source, block, rows):
    arrived = [
        across(terms[k * block : (k + 1) * block], source, k)
        for k in range(lax.axis_size("tensor"))
    ]
    others = []
    if source == 1:
        for k in range(2, lax.axis_size("dp")):
            early, arrived[0] = lax.optimization_barrier((rows, arrived[0]))
            others.append(swap_in(early, source, "dp", k))
    total = start.astype(jnp.float32)
    for value in arrived:
        total = total + value.astype(jnp.float32)
    total = total.astype(jnp.bfloat16)
    late, total = lax.optimization_barrier((rows, total))
    if source == 0:
        return total, gather_in(late, source, "dp")
    return total, [rows, swap_in(late, source, "dp", 1)] + others


def load_kernel(gate_in, up_in, down_in, gate, up, down, gate_t, sems):
    width = gate.shape[0]
    pieces = [(begin, min(256, width - begin)) for begin in range(0, width, 256)]
    copies = []
    for number, (begin, count) in enumerate(pieces):
        rows = pl.ds(begin, count)
        copies.append(pltpu.make_async_copy(gate_in.at[0, rows], gate.at[rows], sems.at[2 + number]))
    rest = [
        pltpu.make_async_copy(up_in.at[0], up, sems.at[0]),
        pltpu.make_async_copy(down_in.at[0], down, sems.at[1]),
    ]
    for copy in copies + rest:
        copy.start()
    for copy, (begin, count) in zip(copies, pieces):
        copy.wait()
        gate_t[:, begin : begin + count] = gate[begin : begin + count, :].T
    for copy in rest:
        copy.wait()


def load_weights(w_gate, w_up, w_down):
    _, width, units = w_gate.shape
    weights = [pltpu.with_memory_space_constraint(w, pltpu.HBM) for w in (w_gate, w_up, w_down)]
    shapes = [(width, units), (width, units), (units, width), (units, width)]
    return pl.pallas_call(
        load_kernel,
        in_specs=[pl.BlockSpec(memory_space=pltpu.HBM)] * 3,
        out_specs=[pl.BlockSpec(memory_space=pltpu.VMEM)] * 4,
        out_shape=[pltpu.VMEM(shape, jnp.bfloat16) for shape in shapes],
        scratch_shapes=[pltpu.SemaphoreType.DMA((2 + -(-width // 256),))],
        compiler_params=pltpu.CompilerParams(vmem_limit_bytes=4 * 2**20),
        cost_estimate=pl.CostEstimate(
            flops=0, bytes_accessed=6 * width * units, transcendentals=0
        ),
    )(*weights)


def hidden_grad_kernel(flag_ref, rows_ref, down_ref, out_ref):
    units = down_ref.shape[0]

    @pl.when(flag_ref[0] == 1)
    def _():
        for begin in range(0, units, TILE):
            out_ref[:, begin : begin + TILE] = lax.dot_general(
                rows_ref[...],
                down_ref[begin : begin + TILE, :],
                CONTRACT_LAST,
                preferred_element_type=jnp.float32,
            )

    @pl.when(flag_ref[0] == 0)
    def _():
        out_ref[...] = jnp.zeros_like(out_ref)


def hidden_grad(segment, rows, down_w):
    units, width = down_w.shape
    return pl.pallas_call(
        hidden_grad_kernel,
        in_specs=[pl.BlockSpec(memory_space=pltpu.SMEM)]
        + [pl.BlockSpec(memory_space=pltpu.VMEM)] * 2,
        out_specs=pl.BlockSpec(memory_space=pltpu.VMEM),
        out_shape=jax.ShapeDtypeStruct((rows.shape[0], units), jnp.float32),
        compiler_params=pltpu.CompilerParams(vmem_limit_bytes=16 * 2**20),
        cost_estimate=pl.CostEstimate(
            flops=2 * rows.shape[0] * units * width,
            bytes_accessed=2 * units * width,
            transcendentals=0,
        ),
    )(segment.reshape(1), rows, down_w)


def gradient_kernel(hidden_ref, masked_ref, *rest):
    out_ref = rest[-1]
    piece = out_ref.shape[2]
    product = lax.dot_general(
        hidden_ref[...], masked_ref[...], CONTRACT_FIRST, preferred_element_type=jnp.float32
    )
    for e in range(DOMAINS):
        out_ref[e] = product[:, e * piece : (e + 1) * piece].astype(jnp.bfloat16)


def domain_gradients(hidden, masked, begin, count, grads=None):
    rows, units = hidden.shape
    columns = masked.shape[1]
    piece = columns // DOMAINS
    in_specs = [
        pl.BlockSpec((rows, TILE), lambda i: (0, begin + i)),
        pl.BlockSpec(memory_space=pltpu.VMEM),
    ]
    operands = [hidden, masked]
    if grads is not None:
        in_specs.append(pl.BlockSpec(memory_space=pl.ANY))
        operands.append(grads)
    return pl.pallas_call(
        gradient_kernel,
        grid=(count,),
        in_specs=in_specs,
        out_specs=pl.BlockSpec((DOMAINS, TILE, piece), lambda i: (0, begin + i, 0)),
        out_shape=jax.ShapeDtypeStruct((DOMAINS, units, piece), jnp.bfloat16),
        input_output_aliases={} if grads is None else {2: 0},
        compiler_params=pltpu.CompilerParams(vmem_limit_bytes=16 * 2**20),
        cost_estimate=pl.CostEstimate(
            flops=2 * rows * count * TILE * columns,
            bytes_accessed=2 * count * TILE * (rows + columns),
            transcendentals=0,
        ),
    )(*operands)


def assemble_kernel(count, flag_ref, *refs):
    pieces = refs[: 2 * count]
    hidden_ref, gram_ref, sems = refs[2 * count :]
    rows = pieces[0].shape[0]
    for section in range(2):

        @pl.when(flag_ref[0] == section)
        def _(section=section):
            copies = [
                pltpu.make_async_copy(
                    pieces[section * count + k],
                    hidden_ref.at[pl.ds(k * rows, rows)],
                    sems.at[k],
                )
                for k in range(count)
            ]
            for copy in copies:
                copy.start()
            for copy in copies:
                copy.wait()

    total = rows * count
    step = min(total, 512)
    for begin in range(0, total, step):
        gram_ref[begin : begin + step, :] = lax.dot_general(
            hidden_ref[begin : begin + step, :],
            hidden_ref[...],
            CONTRACT_LAST,
            preferred_element_type=jnp.float32,
        )


def assemble(segment, pieces0, pieces1):
    count = len(pieces0)
    rows, units = pieces0[0].shape
    total = rows * count
    pieces = [pltpu.with_memory_space_constraint(p, pltpu.HBM) for p in pieces0 + pieces1]
    return pl.pallas_call(
        functools.partial(assemble_kernel, count),
        in_specs=[pl.BlockSpec(memory_space=pltpu.SMEM)]
        + [pl.BlockSpec(memory_space=pl.ANY)] * (2 * count),
        out_specs=[pl.BlockSpec(memory_space=pltpu.VMEM)] * 2,
        out_shape=[
            jax.ShapeDtypeStruct((total, units), jnp.bfloat16),
            jax.ShapeDtypeStruct((total, total), jnp.float32),
        ],
        scratch_shapes=[pltpu.SemaphoreType.DMA((count,))],
        compiler_params=pltpu.CompilerParams(
            vmem_limit_bytes=2 * total * units + 4 * total * total + 4 * 2**20
        ),
        cost_estimate=pl.CostEstimate(
            flops=2 * total * total * units,
            bytes_accessed=4 * total * units + 4 * total * total,
            transcendentals=0,
        ),
    )(segment.reshape(1), *pieces)


def norms_kernel(replicas, levels, ids_ref, ids_row_ref, gram_ref, *refs):
    *parts, masked_ref, norms_ref, y_ref, acc = refs
    parts.reverse()
    piece = y_ref.shape[1]
    block = parts[0].shape[0] // replicas
    tok_rows = block * len(parts)
    for t, part in enumerate(parts):
        for k in range(replicas):
            y_ref[k * tok_rows + t * block : k * tok_rows + (t + 1) * block, :] = part[
                k * block : (k + 1) * block, :
            ]
    for e in range(DOMAINS):
        masked_ref[:, e * piece : (e + 1) * piece] = jnp.where(
            ids_ref[...] == e, y_ref[...].astype(jnp.float32), 0.0
        ).astype(jnp.bfloat16)
    acc[...] = jnp.zeros_like(acc)
    lane = lax.broadcasted_iota(jnp.int32, (1, acc.shape[1]), 1)
    for k in range(replicas):
        columns = slice(k * tok_rows, (k + 1) * tok_rows)
        gram_y = lax.dot_general(
            y_ref[...], y_ref[columns, :], CONTRACT_LAST, preferred_element_type=jnp.float32
        )
        pairs = jnp.where(ids_ref[...] == ids_row_ref[:, columns], gram_ref[:, columns] * gram_y, 0.0)
        of_row = jnp.sum(pairs, axis=1, keepdims=True)
        for level in range(levels):
            begin = (k >> level << level) * tok_rows
            end = begin + (tok_rows << level)
            acc[begin:end, :] += jnp.where(lane == level, of_row[begin:end], 0.0)
    for e in range(DOMAINS):
        norms_ref[e : e + 1, :] = jnp.sum(
            jnp.where(ids_ref[...] == e, acc[...], 0.0), axis=0, keepdims=True
        )
    norms_ref[DOMAINS:, :] = jnp.zeros_like(norms_ref[DOMAINS:, :])


def norm_sums(row_ids, gram_hidden, parts, replicas, levels):
    total = gram_hidden.shape[0]
    piece = parts[0].shape[1]
    return pl.pallas_call(
        functools.partial(norms_kernel, replicas, levels),
        in_specs=[pl.BlockSpec(memory_space=pltpu.VMEM)] * (3 + len(parts)),
        out_specs=[pl.BlockSpec(memory_space=pltpu.VMEM)] * 2,
        out_shape=[
            pltpu.VMEM((total, DOMAINS * piece), jnp.bfloat16),
            jax.ShapeDtypeStruct((8, 128), jnp.float32),
        ],
        scratch_shapes=[
            pltpu.VMEM((total, piece), jnp.bfloat16),
            pltpu.VMEM((total, 128), jnp.float32),
        ],
        compiler_params=pltpu.CompilerParams(
            vmem_limit_bytes=8 * total * piece + 4 * total * total + 1024 * total * 4 + 8 * 2**20
        ),
        cost_estimate=pl.CostEstimate(
            flops=2 * total * total * piece + 4 * total * total,
            bytes_accessed=4 * total * piece + 4 * total * total,
            transcendentals=0,
        ),
    )(row_ids, row_ids.reshape(1, total), gram_hidden, *reversed(parts))


def shards(layer_input_activations, cotangent, domain_ids, norm_gain, w_gate, w_up, w_down):
    segment = lax.axis_index("section")
    dp_index = lax.axis_index("dp")
    segments = lax.axis_size("section")
    tensor_size = lax.axis_size("tensor")
    dp_size = lax.axis_size("dp")
    assert segments == 2
    micro, local_rows, width = layer_input_activations.shape
    gain = norm_gain[0][None, :]
    gate_w, up_w, down_w, gate_t = load_weights(w_gate, w_up, w_down)
    units = down_w.shape[0]
    block = micro * local_rows
    tok_rows = block * tensor_size
    first = segment == 0

    x_own = layer_input_activations.reshape(block, width)
    cot_own = cotangent.reshape(block, width)
    rows_in = jnp.concatenate(gather(jnp.where(first, x_own, cot_own), "tensor"), axis=0)

    def layer_parts(rows):
        widened = rows.astype(jnp.float32)
        scale = lax.rsqrt(jnp.mean(widened * widened, axis=-1, keepdims=True) + EPS)
        normed = (widened * scale * gain).astype(jnp.bfloat16)
        gate = jnp.dot(normed, gate_w, preferred_element_type=jnp.float32)
        up = jnp.dot(normed, up_w, preferred_element_type=jnp.float32)
        return widened, scale, gate, up

    _, _, gate0, up0 = layer_parts(rows_in)
    hidden0 = (jax.nn.silu(gate0) * up0).astype(jnp.bfloat16)
    mixed = jnp.dot(hidden0, down_w, preferred_element_type=jnp.float32).astype(jnp.bfloat16)
    cot_rows, hidden0, mixed = lax.optimization_barrier((rows_in, hidden0, mixed))
    d_hidden = hidden_grad(segment, cot_rows, down_w)
    x1_own, pieces0 = scatter_sum(x_own, mixed, 0, block, hidden0)
    x1_own, d_hidden = lax.optimization_barrier((x1_own, d_hidden))
    x1 = jnp.concatenate(gather_in(x1_own, 1, "tensor"), axis=0)

    widened, scale, gate, up = layer_parts(x1)
    sig = jax.nn.sigmoid(gate)
    hidden1 = (gate * sig * up).astype(jnp.bfloat16)
    d_gate = (d_hidden * up * (sig * (1.0 + gate * (1.0 - sig)))).astype(jnp.bfloat16)
    d_up = (d_hidden * gate * sig).astype(jnp.bfloat16)
    d_gate, d_up = lax.optimization_barrier((d_gate, d_up))
    d_normed = jnp.dot(d_gate, gate_t, preferred_element_type=jnp.float32)
    d_normed = d_normed + lax.dot_general(
        d_up, up_w, CONTRACT_LAST, preferred_element_type=jnp.float32
    )
    pulled = d_normed * gain
    along = jnp.sum(pulled * widened, axis=-1, keepdims=True) / width
    term = (pulled * scale - widened * (scale * scale * scale * along)).astype(jnp.bfloat16)
    term, pieces0 = lax.optimization_barrier((term, pieces0))
    dy_own, pieces1 = scatter_sum(cot_own, term, 1, block, hidden1)
    dy_own = jnp.where(first, dy_own, cot_own)

    piece = width // dp_size
    id_rows = -(-micro // 16) * 16
    id_block = jnp.broadcast_to(
        jnp.pad(domain_ids.astype(jnp.bfloat16), ((0, id_rows - micro), (0, 0))), (id_rows, piece)
    )
    messages = []
    for k in range(dp_size):
        part = lax.dynamic_slice_in_dim(dy_own, (dp_index ^ k) * piece, piece, axis=1)
        part = jnp.concatenate([part, id_block], axis=0)
        messages.append(part if k == 0 else swap(part, "dp", k))
    columns = jnp.concatenate([message[:block] for message in messages], axis=0)
    columns, pieces1[1] = lax.optimization_barrier((columns, pieces1[1]))
    parts_y = gather(columns, "tensor")
    hidden_all, gram_hidden = assemble(segment, pieces0, pieces1)
    ids_all = jnp.stack([message[block : block + micro, 0] for message in messages])
    row_ids = jnp.broadcast_to(
        ids_all.astype(jnp.int32)[:, None, :, None], (dp_size, tensor_size, micro, local_rows)
    ).reshape(dp_size * tok_rows, 1)
    levels = dp_size.bit_length()
    masked, norms = norm_sums(row_ids, gram_hidden, parts_y, dp_size, levels)
    rounds = [
        (axis, bit, min(2, bits(axis) - bit))
        for axis in ("tensor", "dp", "section")
        for bit in range(0, bits(axis), 2)
    ]
    tiles = units // TILE
    parts = min(len(rounds), tiles)
    grads = None
    begin = 0
    for part, (axis, bit, count) in enumerate(rounds):
        others = [swap(norms, axis, k << bit) for k in range(1, 1 << count)]
        if part < parts:
            end = tiles * (part + 1) // parts
            grads = domain_gradients(hidden_all, masked, begin, end - begin, grads)
            begin = end
        if count == 2:
            norms = (others[2] + others[1]) + (others[0] + norms)
        else:
            norms = norms + others[0]
        masked, norms = lax.optimization_barrier((masked, norms))
    entries = segments * units * tensor_size * width
    counts = [float((dp_size >> level) * entries) for level in range(levels)]
    return grads[None], norms[:DOMAINS, :levels] / jnp.array(counts, jnp.float32)[None, :]


def solution(mesh):
    return jax.shard_map(
        shards,
        mesh=mesh,
        in_specs=(
            P(None, ("dp", "tensor"), None),
            P(None, ("dp", "tensor"), None),
            P(None, "dp"),
            P("section", None),
            P("section", None, "tensor"),
            P("section", None, "tensor"),
            P("section", "tensor", None),
        ),
        out_specs=(P("section", None, "tensor", "dp"), P()),
        check_vma=False,
    )
```

```python
import functools

import jax
import jax.numpy as jnp
from jax import lax
from jax.experimental import pallas as pl
from jax.experimental.pallas import tpu as pltpu
from jax.sharding import PartitionSpec as P

DOMAINS = 4
TILE = 256
EPS = 1e-05
CONTRACT_LAST = (((1,), (1,)), ((), ()))
CONTRACT_FIRST = (((0,), (0,)), ((), ()))


def swap(block, axis, offset):
    size = lax.axis_size(axis)
    return lax.ppermute(block, axis, [(i, i ^ offset) for i in range(size)])


def swap_in(block, section, axis, offset):
    size = lax.axis_size(axis)
    route = [(section * size + i, section * size + (i ^ offset)) for i in range(size)]
    return lax.ppermute(block, ("section", axis), route)


def across(block, source, offset):
    size = lax.axis_size("tensor")
    route = [
        (source * size + i, (1 - source) * size + (i ^ offset)) for i in range(size)
    ]
    return lax.ppermute(block, ("section", "tensor"), route)


def bits(axis):
    return lax.axis_size(axis).bit_length() - 1


def gather_beside(rows):
    dp_size, tensor_size = lax.axis_size("dp"), lax.axis_size("tensor")

    def route(k):
        beside = (k - 1) % (dp_size - 1) + 1
        pairs = []
        for d in range(dp_size):
            for t in range(tensor_size):
                pairs.append((d * tensor_size + t, (d ^ beside) * tensor_size + t))
                pairs.append(((dp_size + d) * tensor_size + t, (dp_size + d) * tensor_size + (t ^ k)))
        return pairs

    axes = ("section", "dp", "tensor")
    return [rows] + [lax.ppermute(rows, axes, route(k)) for k in range(1, tensor_size)]


def gather(rows, axis):
    return [rows] + [swap(rows, axis, k) for k in range(1, lax.axis_size(axis))]


def scatter_sum(start, terms, source, block, rows):
    arrived = [
        across(terms[k * block : (k + 1) * block], source, k)
        for k in range(lax.axis_size("tensor"))
    ]
    others = []
    if source == 1:
        for k in range(2, lax.axis_size("dp")):
            early, arrived[0] = lax.optimization_barrier((rows, arrived[0]))
            others.append(swap_in(early, source, "dp", k))
    total = start.astype(jnp.float32)
    for value in arrived:
        total = total + value.astype(jnp.float32)
    total = total.astype(jnp.bfloat16)
    late, total = lax.optimization_barrier((rows, total))
    if source == 0:
        short = min(lax.axis_size("dp"), lax.axis_size("tensor"))
        return total, [rows] + [
            swap_in(late[block:] if k < short else late, source, "dp", k)
            for k in range(1, lax.axis_size("dp"))
        ]
    return total, [rows, swap_in(late, source, "dp", 1)] + others


def load_kernel(gate_in, up_in, down_in, gate, up, down, gate_t, sems):
    width = gate.shape[0]
    pieces = [(begin, min(256, width - begin)) for begin in range(0, width, 256)]
    copies = []
    for number, (begin, count) in enumerate(pieces):
        rows = pl.ds(begin, count)
        copies.append(pltpu.make_async_copy(gate_in.at[0, rows], gate.at[rows], sems.at[2 + number]))
    rest = [
        pltpu.make_async_copy(up_in.at[0], up, sems.at[0]),
        pltpu.make_async_copy(down_in.at[0], down, sems.at[1]),
    ]
    for copy in copies + rest:
        copy.start()
    for copy, (begin, count) in zip(copies, pieces):
        copy.wait()
        gate_t[:, begin : begin + count] = gate[begin : begin + count, :].T
    for copy in rest:
        copy.wait()


def load_weights(w_gate, w_up, w_down):
    _, width, units = w_gate.shape
    weights = [pltpu.with_memory_space_constraint(w, pltpu.HBM) for w in (w_gate, w_up, w_down)]
    shapes = [(width, units), (width, units), (units, width), (units, width)]
    return pl.pallas_call(
        load_kernel,
        in_specs=[pl.BlockSpec(memory_space=pltpu.HBM)] * 3,
        out_specs=[pl.BlockSpec(memory_space=pltpu.VMEM)] * 4,
        out_shape=[pltpu.VMEM(shape, jnp.bfloat16) for shape in shapes],
        scratch_shapes=[pltpu.SemaphoreType.DMA((2 + -(-width // 256),))],
        compiler_params=pltpu.CompilerParams(vmem_limit_bytes=4 * 2**20),
        cost_estimate=pl.CostEstimate(
            flops=0, bytes_accessed=6 * width * units, transcendentals=0
        ),
    )(*weights)


def hidden_grad_kernel(flag_ref, rows_ref, down_ref, out_ref):
    units = down_ref.shape[0]

    @pl.when(flag_ref[0] == 1)
    def _():
        for begin in range(0, units, TILE):
            out_ref[:, begin : begin + TILE] = lax.dot_general(
                rows_ref[...],
                down_ref[begin : begin + TILE, :],
                CONTRACT_LAST,
                preferred_element_type=jnp.float32,
            )

    @pl.when(flag_ref[0] == 0)
    def _():
        out_ref[...] = jnp.zeros_like(out_ref)


def hidden_grad(segment, rows, down_w):
    units, width = down_w.shape
    return pl.pallas_call(
        hidden_grad_kernel,
        in_specs=[pl.BlockSpec(memory_space=pltpu.SMEM)]
        + [pl.BlockSpec(memory_space=pltpu.VMEM)] * 2,
        out_specs=pl.BlockSpec(memory_space=pltpu.VMEM),
        out_shape=jax.ShapeDtypeStruct((rows.shape[0], units), jnp.float32),
        compiler_params=pltpu.CompilerParams(vmem_limit_bytes=16 * 2**20),
        cost_estimate=pl.CostEstimate(
            flops=2 * rows.shape[0] * units * width,
            bytes_accessed=2 * units * width,
            transcendentals=0,
        ),
    )(segment.reshape(1), rows, down_w)


def normed_grad_kernel(flag_ref, d_gate_ref, d_up_ref, gate_t_ref, up_ref, out_ref):
    width = out_ref.shape[1]

    @pl.when(flag_ref[0] == 1)
    def _():
        for begin in range(0, width, TILE):
            columns = slice(begin, begin + TILE)
            out_ref[:, columns] = jnp.dot(
                d_gate_ref[...], gate_t_ref[:, columns], preferred_element_type=jnp.float32
            ) + lax.dot_general(
                d_up_ref[...], up_ref[columns, :], CONTRACT_LAST, preferred_element_type=jnp.float32
            )

    @pl.when(flag_ref[0] == 0)
    def _():
        out_ref[...] = jnp.zeros_like(out_ref)


def normed_grad(segment, d_gate, d_up, gate_t, up_w):
    rows, units = d_gate.shape
    width = up_w.shape[0]
    return pl.pallas_call(
        normed_grad_kernel,
        in_specs=[pl.BlockSpec(memory_space=pltpu.SMEM)]
        + [pl.BlockSpec(memory_space=pltpu.VMEM)] * 4,
        out_specs=pl.BlockSpec(memory_space=pltpu.VMEM),
        out_shape=jax.ShapeDtypeStruct((rows, width), jnp.float32),
        compiler_params=pltpu.CompilerParams(vmem_limit_bytes=24 * 2**20),
        cost_estimate=pl.CostEstimate(
            flops=4 * rows * units * width,
            bytes_accessed=4 * units * width,
            transcendentals=0,
        ),
    )(segment.reshape(1), d_gate, d_up, gate_t, up_w)


def gradient_kernel(hidden_ref, masked_ref, *rest):
    out_ref = rest[-1]
    piece = out_ref.shape[2]
    product = lax.dot_general(
        hidden_ref[...], masked_ref[...], CONTRACT_FIRST, preferred_element_type=jnp.float32
    )
    for e in range(DOMAINS):
        out_ref[e] = product[:, e * piece : (e + 1) * piece].astype(jnp.bfloat16)


def domain_gradients(hidden, masked, begin, count, grads=None):
    rows, units = hidden.shape
    columns = masked.shape[1]
    piece = columns // DOMAINS
    in_specs = [
        pl.BlockSpec((rows, TILE), lambda i: (0, begin + i)),
        pl.BlockSpec(memory_space=pltpu.VMEM),
    ]
    operands = [hidden, masked]
    if grads is not None:
        in_specs.append(pl.BlockSpec(memory_space=pl.ANY))
        operands.append(grads)
    return pl.pallas_call(
        gradient_kernel,
        grid=(count,),
        in_specs=in_specs,
        out_specs=pl.BlockSpec((DOMAINS, TILE, piece), lambda i: (0, begin + i, 0)),
        out_shape=jax.ShapeDtypeStruct((DOMAINS, units, piece), jnp.bfloat16),
        input_output_aliases={} if grads is None else {2: 0},
        compiler_params=pltpu.CompilerParams(vmem_limit_bytes=16 * 2**20),
        cost_estimate=pl.CostEstimate(
            flops=2 * rows * count * TILE * columns,
            bytes_accessed=2 * count * TILE * (rows + columns),
            transcendentals=0,
        ),
    )(*operands)


def assemble_kernel(count, flag_ref, *refs):
    heads = len(refs) - 3 - 2 * count
    pieces = (refs[:count][::-1], refs[count : 2 * count])
    firsts = refs[2 * count : 2 * count + heads]
    hidden_ref, gram_ref, sems = refs[2 * count + heads :]
    rows, units = pieces[1][0].shape
    for section in range(2):

        @pl.when(flag_ref[0] == section)
        def _(section=section):
            copies = []
            for k in range(count):
                begin = k * rows
                if section == 0 and 1 <= k <= heads:
                    head = firsts[k - 1]
                    size = head.shape[0]
                    copies.append(
                        pltpu.make_async_copy(
                            head.at[:, pl.ds(0, units)],
                            hidden_ref.at[pl.ds(begin, size)],
                            sems.at[count + k],
                        )
                    )
                    begin += size
                copies.append(
                    pltpu.make_async_copy(
                        pieces[section][k],
                        hidden_ref.at[pl.ds(begin, pieces[section][k].shape[0])],
                        sems.at[k],
                    )
                )
            for copy in copies:
                copy.start()
            for copy in copies:
                copy.wait()

    total = rows * count
    step = min(total, 512)
    for begin in range(0, total, step):
        gram_ref[begin : begin + step, :] = lax.dot_general(
            hidden_ref[begin : begin + step, :],
            hidden_ref[...],
            CONTRACT_LAST,
            preferred_element_type=jnp.float32,
        )


def assemble(segment, pieces0, pieces1, heads):
    count = len(pieces0)
    rows, units = pieces0[0].shape
    total = rows * count
    pieces = [pltpu.with_memory_space_constraint(p, pltpu.HBM) for p in pieces0[::-1] + pieces1 + heads]
    return pl.pallas_call(
        functools.partial(assemble_kernel, count),
        in_specs=[pl.BlockSpec(memory_space=pltpu.SMEM)]
        + [pl.BlockSpec(memory_space=pl.ANY)] * len(pieces),
        out_specs=[pl.BlockSpec(memory_space=pltpu.VMEM)] * 2,
        out_shape=[
            jax.ShapeDtypeStruct((total, units), jnp.bfloat16),
            jax.ShapeDtypeStruct((total, total), jnp.float32),
        ],
        scratch_shapes=[pltpu.SemaphoreType.DMA((2 * count,))],
        compiler_params=pltpu.CompilerParams(
            vmem_limit_bytes=2 * total * units + 4 * total * total + 4 * 2**20
        ),
        cost_estimate=pl.CostEstimate(
            flops=2 * total * total * units,
            bytes_accessed=4 * total * units + 4 * total * total,
            transcendentals=0,
        ),
    )(segment.reshape(1), *pieces)


def norms_kernel(replicas, levels, ids_ref, ids_row_ref, gram_ref, *refs):
    *parts, masked_ref, norms_ref, y_ref, acc = refs
    parts.reverse()
    piece = y_ref.shape[1]
    block = parts[0].shape[0] // replicas
    tok_rows = block * len(parts)
    for t, part in enumerate(parts):
        for k in range(replicas):
            y_ref[k * tok_rows + t * block : k * tok_rows + (t + 1) * block, :] = part[
                k * block : (k + 1) * block, :
            ]
    for e in range(DOMAINS):
        masked_ref[:, e * piece : (e + 1) * piece] = jnp.where(
            ids_ref[...] == e, y_ref[...].astype(jnp.float32), 0.0
        ).astype(jnp.bfloat16)
    acc[...] = jnp.zeros_like(acc)
    lane = lax.broadcasted_iota(jnp.int32, (1, acc.shape[1]), 1)
    for k in range(replicas):
        columns = slice(k * tok_rows, (k + 1) * tok_rows)
        gram_y = lax.dot_general(
            y_ref[...], y_ref[columns, :], CONTRACT_LAST, preferred_element_type=jnp.float32
        )
        pairs = jnp.where(ids_ref[...] == ids_row_ref[:, columns], gram_ref[:, columns] * gram_y, 0.0)
        of_row = jnp.sum(pairs, axis=1, keepdims=True)
        for level in range(levels):
            begin = (k >> level << level) * tok_rows
            end = begin + (tok_rows << level)
            acc[begin:end, :] += jnp.where(lane == level, of_row[begin:end], 0.0)
    for e in range(DOMAINS):
        norms_ref[e : e + 1, :] = jnp.sum(
            jnp.where(ids_ref[...] == e, acc[...], 0.0), axis=0, keepdims=True
        )
    norms_ref[DOMAINS:, :] = jnp.zeros_like(norms_ref[DOMAINS:, :])


def norm_sums(row_ids, gram_hidden, parts, replicas, levels):
    total = gram_hidden.shape[0]
    piece = parts[0].shape[1]
    return pl.pallas_call(
        functools.partial(norms_kernel, replicas, levels),
        in_specs=[pl.BlockSpec(memory_space=pltpu.VMEM)] * (3 + len(parts)),
        out_specs=[pl.BlockSpec(memory_space=pltpu.VMEM)] * 2,
        out_shape=[
            pltpu.VMEM((total, DOMAINS * piece), jnp.bfloat16),
            jax.ShapeDtypeStruct((8, 128), jnp.float32),
        ],
        scratch_shapes=[
            pltpu.VMEM((total, piece), jnp.bfloat16),
            pltpu.VMEM((total, 128), jnp.float32),
        ],
        compiler_params=pltpu.CompilerParams(
            vmem_limit_bytes=8 * total * piece + 4 * total * total + 1024 * total * 4 + 8 * 2**20
        ),
        cost_estimate=pl.CostEstimate(
            flops=2 * total * total * piece + 4 * total * total,
            bytes_accessed=4 * total * piece + 4 * total * total,
            transcendentals=0,
        ),
    )(row_ids, row_ids.reshape(1, total), gram_hidden, *reversed(parts))


def shards(layer_input_activations, cotangent, domain_ids, norm_gain, w_gate, w_up, w_down):
    segment = lax.axis_index("section")
    dp_index = lax.axis_index("dp")
    segments = lax.axis_size("section")
    tensor_size = lax.axis_size("tensor")
    dp_size = lax.axis_size("dp")
    assert segments == 2
    micro, local_rows, width = layer_input_activations.shape
    gain = norm_gain[0][None, :]
    gate_w, up_w, down_w, gate_t = load_weights(w_gate, w_up, w_down)
    units = down_w.shape[0]
    block = micro * local_rows
    tok_rows = block * tensor_size
    first = segment == 0

    x_own = layer_input_activations.reshape(block, width)
    cot_own = cotangent.reshape(block, width)
    rows_in = jnp.concatenate(gather(jnp.where(first, x_own, cot_own), "tensor"), axis=0)

    def layer_parts(rows):
        widened = rows.astype(jnp.float32)
        scale = lax.rsqrt(jnp.mean(widened * widened, axis=-1, keepdims=True) + EPS)
        normed = (widened * scale * gain).astype(jnp.bfloat16)
        gate = jnp.dot(normed, gate_w, preferred_element_type=jnp.float32)
        up = jnp.dot(normed, up_w, preferred_element_type=jnp.float32)
        return widened, scale, gate, up

    _, _, gate0, up0 = layer_parts(rows_in)
    hidden0 = (jax.nn.silu(gate0) * up0).astype(jnp.bfloat16)
    mixed = jnp.dot(hidden0, down_w, preferred_element_type=jnp.float32).astype(jnp.bfloat16)
    cot_rows, hidden0, mixed = lax.optimization_barrier((rows_in, hidden0, mixed))
    d_hidden = hidden_grad(segment, cot_rows, down_w)
    x1_own, pieces0 = scatter_sum(x_own, mixed, 0, block, hidden0)
    x1_own, d_hidden = lax.optimization_barrier((x1_own, d_hidden))
    head = jnp.pad(hidden0[:block], ((0, 0), (0, width - units)))
    blocks = gather_beside(jnp.where(first, head, x1_own))
    x1 = jnp.concatenate(blocks, axis=0)
    heads = blocks[1 : min(dp_size, tensor_size)]

    widened, scale, gate, up = layer_parts(x1)
    sig = jax.nn.sigmoid(gate)
    hidden1 = (gate * sig * up).astype(jnp.bfloat16)
    d_gate = (d_hidden * up * (sig * (1.0 + gate * (1.0 - sig)))).astype(jnp.bfloat16)
    d_up = (d_hidden * gate * sig).astype(jnp.bfloat16)
    d_normed = normed_grad(segment, d_gate, d_up, gate_t, up_w)
    pulled = d_normed * gain
    along = jnp.sum(pulled * widened, axis=-1, keepdims=True) / width
    term = (pulled * scale - widened * (scale * scale * scale * along)).astype(jnp.bfloat16)
    pieces0 = pieces0[::-1]
    term, pieces0 = lax.optimization_barrier((term, pieces0))
    pieces0 = pieces0[::-1]
    dy_own, pieces1 = scatter_sum(cot_own, term, 1, block, hidden1)
    dy_own = jnp.where(first, dy_own, cot_own)

    piece = width // dp_size
    id_rows = -(-micro // 16) * 16
    id_block = jnp.broadcast_to(
        jnp.pad(domain_ids.astype(jnp.bfloat16), ((0, id_rows - micro), (0, 0))), (id_rows, piece)
    )
    messages = []
    for k in range(dp_size):
        part = lax.dynamic_slice_in_dim(dy_own, (dp_index ^ k) * piece, piece, axis=1)
        part = jnp.concatenate([part, id_block], axis=0)
        messages.append(part if k == 0 else swap(part, "dp", k))
    columns = jnp.concatenate([message[:block] for message in messages], axis=0)
    columns, pieces1[1] = lax.optimization_barrier((columns, pieces1[1]))
    parts_y = gather(columns, "tensor")
    hidden_all, gram_hidden = assemble(segment, pieces0, pieces1, heads)
    ids_all = jnp.stack([message[block : block + micro, 0] for message in messages])
    row_ids = jnp.broadcast_to(
        ids_all.astype(jnp.int32)[:, None, :, None], (dp_size, tensor_size, micro, local_rows)
    ).reshape(dp_size * tok_rows, 1)
    levels = dp_size.bit_length()
    masked, norms = norm_sums(row_ids, gram_hidden, parts_y, dp_size, levels)
    rounds = [
        (axis, bit, min(2, bits(axis) - bit))
        for axis in ("tensor", "dp", "section")
        for bit in range(0, bits(axis), 2)
    ]
    tiles = units // TILE
    parts = min(len(rounds), tiles)
    grads = None
    begin = 0
    for part, (axis, bit, count) in enumerate(rounds):
        others = [swap(norms, axis, k << bit) for k in range(1, 1 << count)]
        if part < parts:
            end = tiles * (part + 1) // parts
            grads = domain_gradients(hidden_all, masked, begin, end - begin, grads)
            begin = end
        if count == 2:
            norms = (others[2] + others[1]) + (others[0] + norms)
        else:
            norms = norms + others[0]
        masked, norms = lax.optimization_barrier((masked, norms))
    entries = segments * units * tensor_size * width
    counts = [float((dp_size >> level) * entries) for level in range(levels)]
    return grads[None], norms[:DOMAINS, :levels] / jnp.array(counts, jnp.float32)[None, :]


def solution(mesh):
    return jax.shard_map(
        shards,
        mesh=mesh,
        in_specs=(
            P(None, ("dp", "tensor"), None),
            P(None, ("dp", "tensor"), None),
            P(None, "dp"),
            P("section", None),
            P("section", None, "tensor"),
            P("section", None, "tensor"),
            P("section", "tensor", None),
        ),
        out_specs=(P("section", None, "tensor", "dp"), P()),
        check_vma=False,
    )
```

```python
import functools

import jax
import jax.numpy as jnp
from jax import lax
from jax.experimental import pallas as pl
from jax.experimental.pallas import tpu as pltpu
from jax.sharding import PartitionSpec as P

DOMAINS = 4
TILE = 256
EPS = 1e-05
CONTRACT_LAST = (((1,), (1,)), ((), ()))
CONTRACT_FIRST = (((0,), (0,)), ((), ()))


def swap(block, axis, offset):
    size = lax.axis_size(axis)
    return lax.ppermute(block, axis, [(i, i ^ offset) for i in range(size)])


def swap_in(block, section, axis, offset):
    size = lax.axis_size(axis)
    route = [(section * size + i, section * size + (i ^ offset)) for i in range(size)]
    return lax.ppermute(block, ("section", axis), route)


def across(block, source, offset):
    size = lax.axis_size("tensor")
    route = [
        (source * size + i, (1 - source) * size + (i ^ offset)) for i in range(size)
    ]
    return lax.ppermute(block, ("section", "tensor"), route)


def bits(axis):
    return lax.axis_size(axis).bit_length() - 1


def gather_beside(rows):
    dp_size, tensor_size = lax.axis_size("dp"), lax.axis_size("tensor")

    def route(k):
        beside = (k - 1) % (dp_size - 1) + 1
        pairs = []
        for d in range(dp_size):
            for t in range(tensor_size):
                pairs.append((d * tensor_size + t, (d ^ beside) * tensor_size + t))
                pairs.append(((dp_size + d) * tensor_size + t, (dp_size + d) * tensor_size + (t ^ k)))
        return pairs

    axes = ("section", "dp", "tensor")
    return [rows] + [lax.ppermute(rows, axes, route(k)) for k in range(1, tensor_size)]


def exchange(block, k):
    dp_size, tensor_size = lax.axis_size("dp"), lax.axis_size("tensor")
    pairs = []
    for d in range(dp_size):
        for t in range(tensor_size):
            pairs.append((d * tensor_size + t, d * tensor_size + (t ^ k)))
            pairs.append(((dp_size + d) * tensor_size + t, (dp_size + (d ^ k)) * tensor_size + t))
    return lax.ppermute(block, ("section", "dp", "tensor"), pairs)


def gather(rows, axis):
    return [rows] + [swap(rows, axis, k) for k in range(1, lax.axis_size(axis))]


def scatter_sum(start, terms, source, block, rows):
    arrived = [
        across(terms[k * block : (k + 1) * block], source, k)
        for k in range(lax.axis_size("tensor"))
    ]
    others = []
    if source == 1:
        for k in range(2, lax.axis_size("dp")):
            early, arrived[0] = lax.optimization_barrier((rows, arrived[0]))
            others.append(swap_in(early, source, "dp", k))
    total = start.astype(jnp.float32)
    for value in arrived:
        total = total + value.astype(jnp.float32)
    total = total.astype(jnp.bfloat16)
    late, total = lax.optimization_barrier((rows, total))
    if source == 0:
        short = min(lax.axis_size("dp"), lax.axis_size("tensor"))
        return total, [rows] + [
            swap_in(late[block:] if k < short else late, source, "dp", k)
            for k in range(1, lax.axis_size("dp"))
        ]
    return total, [rows, swap_in(late, source, "dp", 1)] + others


def load_kernel(gate_in, up_in, down_in, gate, up, down, gate_t, sems):
    width = gate.shape[0]
    pieces = [(begin, min(256, width - begin)) for begin in range(0, width, 256)]
    copies = []
    for number, (begin, count) in enumerate(pieces):
        rows = pl.ds(begin, count)
        copies.append(pltpu.make_async_copy(gate_in.at[0, rows], gate.at[rows], sems.at[2 + number]))
    rest = [
        pltpu.make_async_copy(up_in.at[0], up, sems.at[0]),
        pltpu.make_async_copy(down_in.at[0], down, sems.at[1]),
    ]
    for copy in copies + rest:
        copy.start()
    for copy, (begin, count) in zip(copies, pieces):
        copy.wait()
        gate_t[:, begin : begin + count] = gate[begin : begin + count, :].T
    for copy in rest:
        copy.wait()


def load_weights(w_gate, w_up, w_down):
    _, width, units = w_gate.shape
    weights = [pltpu.with_memory_space_constraint(w, pltpu.HBM) for w in (w_gate, w_up, w_down)]
    shapes = [(width, units), (width, units), (units, width), (units, width)]
    return pl.pallas_call(
        load_kernel,
        in_specs=[pl.BlockSpec(memory_space=pltpu.HBM)] * 3,
        out_specs=[pl.BlockSpec(memory_space=pltpu.VMEM)] * 4,
        out_shape=[pltpu.VMEM(shape, jnp.bfloat16) for shape in shapes],
        scratch_shapes=[pltpu.SemaphoreType.DMA((2 + -(-width // 256),))],
        compiler_params=pltpu.CompilerParams(vmem_limit_bytes=4 * 2**20),
        cost_estimate=pl.CostEstimate(
            flops=0, bytes_accessed=6 * width * units, transcendentals=0
        ),
    )(*weights)


def hidden_grad_kernel(flag_ref, rows_ref, down_ref, out_ref):
    units = down_ref.shape[0]

    @pl.when(flag_ref[0] == 1)
    def _():
        for begin in range(0, units, TILE):
            out_ref[:, begin : begin + TILE] = lax.dot_general(
                rows_ref[...],
                down_ref[begin : begin + TILE, :],
                CONTRACT_LAST,
                preferred_element_type=jnp.float32,
            )

    @pl.when(flag_ref[0] == 0)
    def _():
        out_ref[...] = jnp.zeros_like(out_ref)


def hidden_grad(segment, rows, down_w):
    units, width = down_w.shape
    return pl.pallas_call(
        hidden_grad_kernel,
        in_specs=[pl.BlockSpec(memory_space=pltpu.SMEM)]
        + [pl.BlockSpec(memory_space=pltpu.VMEM)] * 2,
        out_specs=pl.BlockSpec(memory_space=pltpu.VMEM),
        out_shape=jax.ShapeDtypeStruct((rows.shape[0], units), jnp.float32),
        compiler_params=pltpu.CompilerParams(vmem_limit_bytes=16 * 2**20),
        cost_estimate=pl.CostEstimate(
            flops=2 * rows.shape[0] * units * width,
            bytes_accessed=2 * units * width,
            transcendentals=0,
        ),
    )(segment.reshape(1), rows, down_w)


def normed_grad_kernel(flag_ref, d_gate_ref, d_up_ref, gate_t_ref, up_ref, out_ref):
    width = out_ref.shape[1]

    @pl.when(flag_ref[0] == 1)
    def _():
        for begin in range(0, width, TILE):
            columns = slice(begin, begin + TILE)
            out_ref[:, columns] = jnp.dot(
                d_gate_ref[...], gate_t_ref[:, columns], preferred_element_type=jnp.float32
            ) + lax.dot_general(
                d_up_ref[...], up_ref[columns, :], CONTRACT_LAST, preferred_element_type=jnp.float32
            )

    @pl.when(flag_ref[0] == 0)
    def _():
        out_ref[...] = jnp.zeros_like(out_ref)


def normed_grad(segment, d_gate, d_up, gate_t, up_w):
    rows, units = d_gate.shape
    width = up_w.shape[0]
    return pl.pallas_call(
        normed_grad_kernel,
        in_specs=[pl.BlockSpec(memory_space=pltpu.SMEM)]
        + [pl.BlockSpec(memory_space=pltpu.VMEM)] * 4,
        out_specs=pl.BlockSpec(memory_space=pltpu.VMEM),
        out_shape=jax.ShapeDtypeStruct((rows, width), jnp.float32),
        compiler_params=pltpu.CompilerParams(vmem_limit_bytes=24 * 2**20),
        cost_estimate=pl.CostEstimate(
            flops=4 * rows * units * width,
            bytes_accessed=4 * units * width,
            transcendentals=0,
        ),
    )(segment.reshape(1), d_gate, d_up, gate_t, up_w)


def gradient_kernel(hidden_ref, masked_ref, *rest):
    out_ref = rest[-1]
    piece = out_ref.shape[2]
    product = lax.dot_general(
        hidden_ref[...], masked_ref[...], CONTRACT_FIRST, preferred_element_type=jnp.float32
    )
    for e in range(DOMAINS):
        out_ref[e] = product[:, e * piece : (e + 1) * piece].astype(jnp.bfloat16)


def domain_gradients(hidden, masked, begin, count, grads=None):
    rows, units = hidden.shape
    columns = masked.shape[1]
    piece = columns // DOMAINS
    in_specs = [
        pl.BlockSpec((rows, TILE), lambda i: (0, begin + i)),
        pl.BlockSpec(memory_space=pltpu.VMEM),
    ]
    operands = [hidden, masked]
    if grads is not None:
        in_specs.append(pl.BlockSpec(memory_space=pl.ANY))
        operands.append(grads)
    return pl.pallas_call(
        gradient_kernel,
        grid=(count,),
        in_specs=in_specs,
        out_specs=pl.BlockSpec((DOMAINS, TILE, piece), lambda i: (0, begin + i, 0)),
        out_shape=jax.ShapeDtypeStruct((DOMAINS, units, piece), jnp.bfloat16),
        input_output_aliases={} if grads is None else {2: 0},
        compiler_params=pltpu.CompilerParams(vmem_limit_bytes=16 * 2**20),
        cost_estimate=pl.CostEstimate(
            flops=2 * rows * count * TILE * columns,
            bytes_accessed=2 * count * TILE * (rows + columns),
            transcendentals=0,
        ),
    )(*operands)


def assemble_kernel(count, flag_ref, *refs):
    heads = len(refs) - 3 - 2 * count
    pieces = (refs[:count][::-1], refs[count : 2 * count])
    firsts = refs[2 * count : 2 * count + heads]
    hidden_ref, gram_ref, sems = refs[2 * count + heads :]
    rows, units = pieces[1][0].shape
    for section in range(2):

        @pl.when(flag_ref[0] == section)
        def _(section=section):
            copies = []
            for k in range(count):
                begin = k * rows
                if section == 0 and 1 <= k <= heads:
                    head = firsts[k - 1]
                    size = head.shape[0]
                    copies.append(
                        pltpu.make_async_copy(
                            head.at[:, pl.ds(0, units)],
                            hidden_ref.at[pl.ds(begin, size)],
                            sems.at[count + k],
                        )
                    )
                    begin += size
                copies.append(
                    pltpu.make_async_copy(
                        pieces[section][k],
                        hidden_ref.at[pl.ds(begin, pieces[section][k].shape[0])],
                        sems.at[k],
                    )
                )
            for copy in copies:
                copy.start()
            for copy in copies:
                copy.wait()

    total = rows * count
    step = min(total, 512)
    for begin in range(0, total, step):
        gram_ref[begin : begin + step, :] = lax.dot_general(
            hidden_ref[begin : begin + step, :],
            hidden_ref[...],
            CONTRACT_LAST,
            preferred_element_type=jnp.float32,
        )


def assemble(segment, pieces0, pieces1, heads):
    count = len(pieces0)
    rows, units = pieces0[0].shape
    total = rows * count
    pieces = [pltpu.with_memory_space_constraint(p, pltpu.HBM) for p in pieces0[::-1] + pieces1 + heads]
    return pl.pallas_call(
        functools.partial(assemble_kernel, count),
        in_specs=[pl.BlockSpec(memory_space=pltpu.SMEM)]
        + [pl.BlockSpec(memory_space=pl.ANY)] * len(pieces),
        out_specs=[pl.BlockSpec(memory_space=pltpu.VMEM)] * 2,
        out_shape=[
            jax.ShapeDtypeStruct((total, units), jnp.bfloat16),
            jax.ShapeDtypeStruct((total, total), jnp.float32),
        ],
        scratch_shapes=[pltpu.SemaphoreType.DMA((2 * count,))],
        compiler_params=pltpu.CompilerParams(
            vmem_limit_bytes=2 * total * units + 4 * total * total + 4 * 2**20
        ),
        cost_estimate=pl.CostEstimate(
            flops=2 * total * total * units,
            bytes_accessed=4 * total * units + 4 * total * total,
            transcendentals=0,
        ),
    )(segment.reshape(1), *pieces)


def norms_kernel(replicas, levels, flag_ref, ids_ref, ids_row_ref, gram_ref, *refs):
    *parts, masked_ref, norms_ref, y_ref, acc = refs
    parts.reverse()
    piece = y_ref.shape[1]
    block = parts[0].shape[0] // replicas
    tok_rows = block * len(parts)

    @pl.when(flag_ref[0] == 0)
    def _():
        for t, part in enumerate(parts):
            for k in range(replicas):
                y_ref[k * tok_rows + t * block : k * tok_rows + (t + 1) * block, :] = part[
                    k * block : (k + 1) * block, :
                ]

    if len(parts) == replicas:

        @pl.when(flag_ref[0] == 1)
        def _():
            for k, part in enumerate(parts):
                y_ref[k * tok_rows : (k + 1) * tok_rows, :] = part[...]

    for e in range(DOMAINS):
        masked_ref[:, e * piece : (e + 1) * piece] = jnp.where(
            ids_ref[...] == e, y_ref[...].astype(jnp.float32), 0.0
        ).astype(jnp.bfloat16)
    acc[...] = jnp.zeros_like(acc)
    lane = lax.broadcasted_iota(jnp.int32, (1, acc.shape[1]), 1)
    for k in range(replicas):
        columns = slice(k * tok_rows, (k + 1) * tok_rows)
        gram_y = lax.dot_general(
            y_ref[...], y_ref[columns, :], CONTRACT_LAST, preferred_element_type=jnp.float32
        )
        pairs = jnp.where(ids_ref[...] == ids_row_ref[:, columns], gram_ref[:, columns] * gram_y, 0.0)
        of_row = jnp.sum(pairs, axis=1, keepdims=True)
        for level in range(levels):
            begin = (k >> level << level) * tok_rows
            end = begin + (tok_rows << level)
            acc[begin:end, :] += jnp.where(lane == level, of_row[begin:end], 0.0)
    for e in range(DOMAINS):
        norms_ref[e : e + 1, :] = jnp.sum(
            jnp.where(ids_ref[...] == e, acc[...], 0.0), axis=0, keepdims=True
        )
    norms_ref[DOMAINS:, :] = jnp.zeros_like(norms_ref[DOMAINS:, :])


def norm_sums(by_dp, row_ids, gram_hidden, parts, replicas, levels):
    total = gram_hidden.shape[0]
    piece = parts[0].shape[1]
    return pl.pallas_call(
        functools.partial(norms_kernel, replicas, levels),
        in_specs=[pl.BlockSpec(memory_space=pltpu.SMEM)]
        + [pl.BlockSpec(memory_space=pltpu.VMEM)] * (3 + len(parts)),
        out_specs=[pl.BlockSpec(memory_space=pltpu.VMEM)] * 2,
        out_shape=[
            pltpu.VMEM((total, DOMAINS * piece), jnp.bfloat16),
            jax.ShapeDtypeStruct((8, 128), jnp.float32),
        ],
        scratch_shapes=[
            pltpu.VMEM((total, piece), jnp.bfloat16),
            pltpu.VMEM((total, 128), jnp.float32),
        ],
        compiler_params=pltpu.CompilerParams(
            vmem_limit_bytes=8 * total * piece + 4 * total * total + 1024 * total * 4 + 8 * 2**20
        ),
        cost_estimate=pl.CostEstimate(
            flops=2 * total * total * piece + 4 * total * total,
            bytes_accessed=4 * total * piece + 4 * total * total,
            transcendentals=0,
        ),
    )(by_dp.reshape(1), row_ids, row_ids.reshape(1, total), gram_hidden, *reversed(parts))


def shards(layer_input_activations, cotangent, domain_ids, norm_gain, w_gate, w_up, w_down):
    segment = lax.axis_index("section")
    dp_index = lax.axis_index("dp")
    segments = lax.axis_size("section")
    tensor_size = lax.axis_size("tensor")
    dp_size = lax.axis_size("dp")
    assert segments == 2
    micro, local_rows, width = layer_input_activations.shape
    gain = norm_gain[0][None, :]
    gate_w, up_w, down_w, gate_t = load_weights(w_gate, w_up, w_down)
    units = down_w.shape[0]
    block = micro * local_rows
    tok_rows = block * tensor_size
    first = segment == 0

    x_own = layer_input_activations.reshape(block, width)
    cot_own = cotangent.reshape(block, width)
    rows_in = jnp.concatenate(gather(jnp.where(first, x_own, cot_own), "tensor"), axis=0)

    def layer_parts(rows):
        widened = rows.astype(jnp.float32)
        scale = lax.rsqrt(jnp.mean(widened * widened, axis=-1, keepdims=True) + EPS)
        normed = (widened * scale * gain).astype(jnp.bfloat16)
        gate = jnp.dot(normed, gate_w, preferred_element_type=jnp.float32)
        up = jnp.dot(normed, up_w, preferred_element_type=jnp.float32)
        return widened, scale, gate, up

    _, _, gate0, up0 = layer_parts(rows_in)
    hidden0 = (jax.nn.silu(gate0) * up0).astype(jnp.bfloat16)
    mixed = jnp.dot(hidden0, down_w, preferred_element_type=jnp.float32).astype(jnp.bfloat16)
    cot_rows, hidden0, mixed = lax.optimization_barrier((rows_in, hidden0, mixed))
    d_hidden = hidden_grad(segment, cot_rows, down_w)
    x1_own, pieces0 = scatter_sum(x_own, mixed, 0, block, hidden0)
    x1_own, d_hidden = lax.optimization_barrier((x1_own, d_hidden))
    head = jnp.pad(hidden0[:block], ((0, 0), (0, width - units)))
    blocks = gather_beside(jnp.where(first, head, x1_own))
    x1 = jnp.concatenate(blocks, axis=0)
    heads = blocks[1 : min(dp_size, tensor_size)]

    widened, scale, gate, up = layer_parts(x1)
    sig = jax.nn.sigmoid(gate)
    hidden1 = (gate * sig * up).astype(jnp.bfloat16)
    d_gate = (d_hidden * up * (sig * (1.0 + gate * (1.0 - sig)))).astype(jnp.bfloat16)
    d_up = (d_hidden * gate * sig).astype(jnp.bfloat16)
    d_normed = normed_grad(segment, d_gate, d_up, gate_t, up_w)
    pulled = d_normed * gain
    along = jnp.sum(pulled * widened, axis=-1, keepdims=True) / width
    term = (pulled * scale - widened * (scale * scale * scale * along)).astype(jnp.bfloat16)
    pieces0 = pieces0[::-1]
    term, pieces0 = lax.optimization_barrier((term, pieces0))
    pieces0 = pieces0[::-1]
    dy_own, pieces1 = scatter_sum(cot_own, term, 1, block, hidden1)
    dy_own = jnp.where(first, dy_own, cot_own)

    piece = width // dp_size
    id_rows = -(-micro // 16) * 16
    id_block = jnp.broadcast_to(
        jnp.pad(domain_ids.astype(jnp.bfloat16), ((0, id_rows - micro), (0, 0))), (id_rows, piece)
    )
    messages = []
    for k in range(dp_size):
        part = lax.dynamic_slice_in_dim(dy_own, (dp_index ^ k) * piece, piece, axis=1)
        part = jnp.concatenate([part, id_block], axis=0)
        messages.append(part if k == 0 else swap(part, "dp", k))
    columns = jnp.concatenate([message[:block] for message in messages], axis=0)
    columns, pieces1[1] = lax.optimization_barrier((columns, pieces1[1]))
    if dp_size == tensor_size:
        by_dp = segment
        parts_y = []
        for k in range(dp_size):
            part = lax.dynamic_slice_in_dim(cot_rows, (dp_index ^ k) * piece, piece, axis=1)
            part = jnp.where(first, columns, part)
            parts_y.append(part if k == 0 else exchange(part, k))
    else:
        by_dp = jnp.zeros_like(segment)
        parts_y = gather(columns, "tensor")
    hidden_all, gram_hidden = assemble(segment, pieces0, pieces1, heads)
    ids_all = jnp.stack([message[block : block + micro, 0] for message in messages])
    row_ids = jnp.broadcast_to(
        ids_all.astype(jnp.int32)[:, None, :, None], (dp_size, tensor_size, micro, local_rows)
    ).reshape(dp_size * tok_rows, 1)
    levels = dp_size.bit_length()
    masked, norms = norm_sums(by_dp, row_ids, gram_hidden, parts_y, dp_size, levels)
    rounds = [
        (axis, bit, min(2, bits(axis) - bit))
        for axis in ("tensor", "dp", "section")
        for bit in range(0, bits(axis), 2)
    ]
    tiles = units // TILE
    parts = min(len(rounds), tiles)
    grads = None
    begin = 0
    for part, (axis, bit, count) in enumerate(rounds):
        others = [swap(norms, axis, k << bit) for k in range(1, 1 << count)]
        if part < parts:
            end = tiles * (part + 1) // parts
            grads = domain_gradients(hidden_all, masked, begin, end - begin, grads)
            begin = end
        if count == 2:
            norms = (others[2] + others[1]) + (others[0] + norms)
        else:
            norms = norms + others[0]
        masked, norms = lax.optimization_barrier((masked, norms))
    entries = segments * units * tensor_size * width
    counts = [float((dp_size >> level) * entries) for level in range(levels)]
    return grads[None], norms[:DOMAINS, :levels] / jnp.array(counts, jnp.float32)[None, :]


def solution(mesh):
    return jax.shard_map(
        shards,
        mesh=mesh,
        in_specs=(
            P(None, ("dp", "tensor"), None),
            P(None, ("dp", "tensor"), None),
            P(None, "dp"),
            P("section", None),
            P("section", None, "tensor"),
            P("section", None, "tensor"),
            P("section", "tensor", None),
        ),
        out_specs=(P("section", None, "tensor", "dp"), P()),
        check_vma=False,
    )
```

```python
import functools

import jax
import jax.numpy as jnp
from jax import lax
from jax.experimental import pallas as pl
from jax.experimental.pallas import tpu as pltpu
from jax.sharding import PartitionSpec as P

DOMAINS = 4
TILE = 256
EPS = 1e-05
CONTRACT_LAST = (((1,), (1,)), ((), ()))
CONTRACT_FIRST = (((0,), (0,)), ((), ()))


def swap(block, axis, offset):
    size = lax.axis_size(axis)
    return lax.ppermute(block, axis, [(i, i ^ offset) for i in range(size)])


def swap_in(block, section, axis, offset):
    size = lax.axis_size(axis)
    route = [(section * size + i, section * size + (i ^ offset)) for i in range(size)]
    return lax.ppermute(block, ("section", axis), route)


def across(block, source, offset):
    size = lax.axis_size("tensor")
    route = [
        (source * size + i, (1 - source) * size + (i ^ offset)) for i in range(size)
    ]
    return lax.ppermute(block, ("section", "tensor"), route)


def bits(axis):
    return lax.axis_size(axis).bit_length() - 1


def gather_beside(rows):
    dp_size, tensor_size = lax.axis_size("dp"), lax.axis_size("tensor")

    def route(k):
        beside = (k - 1) % (dp_size - 1) + 1
        pairs = []
        for d in range(dp_size):
            for t in range(tensor_size):
                pairs.append((d * tensor_size + t, (d ^ beside) * tensor_size + t))
                pairs.append(((dp_size + d) * tensor_size + t, (dp_size + d) * tensor_size + (t ^ k)))
        return pairs

    axes = ("section", "dp", "tensor")
    return [rows] + [lax.ppermute(rows, axes, route(k)) for k in range(1, tensor_size)]


def exchange(block, k):
    dp_size, tensor_size = lax.axis_size("dp"), lax.axis_size("tensor")
    pairs = []
    for d in range(dp_size):
        for t in range(tensor_size):
            pairs.append((d * tensor_size + t, d * tensor_size + (t ^ k)))
            pairs.append(((dp_size + d) * tensor_size + t, (dp_size + (d ^ k)) * tensor_size + t))
    return lax.ppermute(block, ("section", "dp", "tensor"), pairs)


def gather(rows, axis):
    return [rows] + [swap(rows, axis, k) for k in range(1, lax.axis_size(axis))]


def scatter_sum(start, terms, source, block, rows):
    arrived = [
        across(terms[k * block : (k + 1) * block], source, k)
        for k in range(lax.axis_size("tensor"))
    ]
    others = []
    if source == 1:
        for k in range(2, lax.axis_size("dp")):
            early, arrived[0] = lax.optimization_barrier((rows, arrived[0]))
            others.append(swap_in(early, source, "dp", k))
    total = start.astype(jnp.float32)
    for value in arrived:
        total = total + value.astype(jnp.float32)
    total = total.astype(jnp.bfloat16)
    late, total = lax.optimization_barrier((rows, total))
    if source == 0:
        short = min(lax.axis_size("dp"), lax.axis_size("tensor"))
        return total, [rows] + [
            swap_in(late[block:] if k < short else late, source, "dp", k)
            for k in range(1, lax.axis_size("dp"))
        ]
    return total, [rows, swap_in(late, source, "dp", 1)] + others


def load_kernel(gate_in, up_in, down_in, gate, up, down, gate_t, sems):
    width = gate.shape[0]
    pieces = [(begin, min(256, width - begin)) for begin in range(0, width, 256)]
    copies = []
    for number, (begin, count) in enumerate(pieces):
        rows = pl.ds(begin, count)
        copies.append(pltpu.make_async_copy(gate_in.at[0, rows], gate.at[rows], sems.at[2 + number]))
    rest = [
        pltpu.make_async_copy(up_in.at[0], up, sems.at[0]),
        pltpu.make_async_copy(down_in.at[0], down, sems.at[1]),
    ]
    for copy in copies + rest:
        copy.start()
    for copy, (begin, count) in zip(copies, pieces):
        copy.wait()
        gate_t[:, begin : begin + count] = gate[begin : begin + count, :].T
    for copy in rest:
        copy.wait()


def load_weights(w_gate, w_up, w_down):
    _, width, units = w_gate.shape
    weights = [pltpu.with_memory_space_constraint(w, pltpu.HBM) for w in (w_gate, w_up, w_down)]
    shapes = [(width, units), (width, units), (units, width), (units, width)]
    return pl.pallas_call(
        load_kernel,
        in_specs=[pl.BlockSpec(memory_space=pltpu.HBM)] * 3,
        out_specs=[pl.BlockSpec(memory_space=pltpu.VMEM)] * 4,
        out_shape=[pltpu.VMEM(shape, jnp.bfloat16) for shape in shapes],
        scratch_shapes=[pltpu.SemaphoreType.DMA((2 + -(-width // 256),))],
        compiler_params=pltpu.CompilerParams(vmem_limit_bytes=4 * 2**20),
        cost_estimate=pl.CostEstimate(
            flops=0, bytes_accessed=6 * width * units, transcendentals=0
        ),
    )(*weights)


def hidden_grad_kernel(flag_ref, rows_ref, down_ref, out_ref):
    units = down_ref.shape[0]

    @pl.when(flag_ref[0] == 1)
    def _():
        for begin in range(0, units, TILE):
            out_ref[:, begin : begin + TILE] = lax.dot_general(
                rows_ref[...],
                down_ref[begin : begin + TILE, :],
                CONTRACT_LAST,
                preferred_element_type=jnp.float32,
            )

    @pl.when(flag_ref[0] == 0)
    def _():
        out_ref[...] = jnp.zeros_like(out_ref)


def hidden_grad(segment, rows, down_w):
    units, width = down_w.shape
    return pl.pallas_call(
        hidden_grad_kernel,
        in_specs=[pl.BlockSpec(memory_space=pltpu.SMEM)]
        + [pl.BlockSpec(memory_space=pltpu.VMEM)] * 2,
        out_specs=pl.BlockSpec(memory_space=pltpu.VMEM),
        out_shape=jax.ShapeDtypeStruct((rows.shape[0], units), jnp.float32),
        compiler_params=pltpu.CompilerParams(vmem_limit_bytes=16 * 2**20),
        cost_estimate=pl.CostEstimate(
            flops=2 * rows.shape[0] * units * width,
            bytes_accessed=2 * units * width,
            transcendentals=0,
        ),
    )(segment.reshape(1), rows, down_w)


def normed_grad_kernel(flag_ref, d_gate_ref, d_up_ref, gate_t_ref, up_ref, out_ref):
    width = out_ref.shape[1]

    @pl.when(flag_ref[0] == 1)
    def _():
        for begin in range(0, width, TILE):
            columns = slice(begin, begin + TILE)
            out_ref[:, columns] = jnp.dot(
                d_gate_ref[...], gate_t_ref[:, columns], preferred_element_type=jnp.float32
            ) + lax.dot_general(
                d_up_ref[...], up_ref[columns, :], CONTRACT_LAST, preferred_element_type=jnp.float32
            )

    @pl.when(flag_ref[0] == 0)
    def _():
        out_ref[...] = jnp.zeros_like(out_ref)


def normed_grad(segment, d_gate, d_up, gate_t, up_w):
    rows, units = d_gate.shape
    width = up_w.shape[0]
    return pl.pallas_call(
        normed_grad_kernel,
        in_specs=[pl.BlockSpec(memory_space=pltpu.SMEM)]
        + [pl.BlockSpec(memory_space=pltpu.VMEM)] * 4,
        out_specs=pl.BlockSpec(memory_space=pltpu.VMEM),
        out_shape=jax.ShapeDtypeStruct((rows, width), jnp.float32),
        compiler_params=pltpu.CompilerParams(vmem_limit_bytes=24 * 2**20),
        cost_estimate=pl.CostEstimate(
            flops=4 * rows * units * width,
            bytes_accessed=4 * units * width,
            transcendentals=0,
        ),
    )(segment.reshape(1), d_gate, d_up, gate_t, up_w)


def gradient_kernel(hidden_ref, masked_ref, *rest):
    out_ref = rest[-1]
    piece = out_ref.shape[2]
    product = lax.dot_general(
        hidden_ref[...], masked_ref[...], CONTRACT_FIRST, preferred_element_type=jnp.float32
    )
    for e in range(DOMAINS):
        out_ref[e] = product[:, e * piece : (e + 1) * piece].astype(jnp.bfloat16)


def domain_gradients(hidden, masked, begin, count, grads=None):
    rows, units = hidden.shape
    columns = masked.shape[1]
    piece = columns // DOMAINS
    in_specs = [
        pl.BlockSpec((rows, TILE), lambda i: (0, begin + i)),
        pl.BlockSpec(memory_space=pltpu.VMEM),
    ]
    operands = [hidden, masked]
    if grads is not None:
        in_specs.append(pl.BlockSpec(memory_space=pl.ANY))
        operands.append(grads)
    return pl.pallas_call(
        gradient_kernel,
        grid=(count,),
        in_specs=in_specs,
        out_specs=pl.BlockSpec((DOMAINS, TILE, piece), lambda i: (0, begin + i, 0)),
        out_shape=jax.ShapeDtypeStruct((DOMAINS, units, piece), jnp.bfloat16),
        input_output_aliases={} if grads is None else {2: 0},
        compiler_params=pltpu.CompilerParams(vmem_limit_bytes=16 * 2**20),
        cost_estimate=pl.CostEstimate(
            flops=2 * rows * count * TILE * columns,
            bytes_accessed=2 * count * TILE * (rows + columns),
            transcendentals=0,
        ),
    )(*operands)


def assemble_kernel(count, flag_ref, *refs):
    heads = len(refs) - 3 - 2 * count
    pieces = (refs[:count][::-1], refs[count : 2 * count])
    firsts = refs[2 * count : 2 * count + heads]
    hidden_ref, gram_ref, sems = refs[2 * count + heads :]
    rows, units = pieces[1][0].shape
    for section in range(2):

        @pl.when(flag_ref[0] == section)
        def _(section=section):
            copies = []
            for k in range(count):
                begin = k * rows
                if section == 0 and 1 <= k <= heads:
                    head = firsts[k - 1]
                    size = head.shape[0]
                    copies.append(
                        pltpu.make_async_copy(
                            head.at[:, pl.ds(0, units)],
                            hidden_ref.at[pl.ds(begin, size)],
                            sems.at[count + k],
                        )
                    )
                    begin += size
                copies.append(
                    pltpu.make_async_copy(
                        pieces[section][k],
                        hidden_ref.at[pl.ds(begin, pieces[section][k].shape[0])],
                        sems.at[k],
                    )
                )
            for copy in copies:
                copy.start()
            for copy in copies:
                copy.wait()

    total = rows * count
    step = min(total, 512)
    for begin in range(0, total, step):
        gram_ref[begin : begin + step, :] = lax.dot_general(
            hidden_ref[begin : begin + step, :],
            hidden_ref[...],
            CONTRACT_LAST,
            preferred_element_type=jnp.float32,
        )


def assemble(segment, pieces0, pieces1, heads):
    count = len(pieces0)
    rows, units = pieces0[0].shape
    total = rows * count
    pieces = [pltpu.with_memory_space_constraint(p, pltpu.HBM) for p in pieces0[::-1] + pieces1 + heads]
    return pl.pallas_call(
        functools.partial(assemble_kernel, count),
        in_specs=[pl.BlockSpec(memory_space=pltpu.SMEM)]
        + [pl.BlockSpec(memory_space=pl.ANY)] * len(pieces),
        out_specs=[pl.BlockSpec(memory_space=pltpu.VMEM)] * 2,
        out_shape=[
            jax.ShapeDtypeStruct((total, units), jnp.bfloat16),
            jax.ShapeDtypeStruct((total, total), jnp.float32),
        ],
        scratch_shapes=[pltpu.SemaphoreType.DMA((2 * count,))],
        compiler_params=pltpu.CompilerParams(
            vmem_limit_bytes=2 * total * units + 4 * total * total + 4 * 2**20
        ),
        cost_estimate=pl.CostEstimate(
            flops=2 * total * total * units,
            bytes_accessed=4 * total * units + 4 * total * total,
            transcendentals=0,
        ),
    )(segment.reshape(1), *pieces)


def norms_kernel(replicas, levels, flag_ref, ids_ref, ids_row_ref, gram_ref, *refs):
    *parts, masked_ref, norms_ref, y_ref, acc = refs
    parts.reverse()
    piece = y_ref.shape[1]
    block = parts[0].shape[0] // replicas
    tok_rows = block * len(parts)

    @pl.when(flag_ref[0] == 0)
    def _():
        for t, part in enumerate(parts):
            for k in range(replicas):
                y_ref[k * tok_rows + t * block : k * tok_rows + (t + 1) * block, :] = part[
                    k * block : (k + 1) * block, :
                ]

    if len(parts) == replicas:

        @pl.when(flag_ref[0] == 1)
        def _():
            for k, part in enumerate(parts):
                y_ref[k * tok_rows : (k + 1) * tok_rows, :] = part[...]

    for e in range(DOMAINS):
        masked_ref[:, e * piece : (e + 1) * piece] = jnp.where(
            ids_ref[...] == e, y_ref[...].astype(jnp.float32), 0.0
        ).astype(jnp.bfloat16)
    acc[...] = jnp.zeros_like(acc)
    lane = lax.broadcasted_iota(jnp.int32, (1, acc.shape[1]), 1)
    for k in range(replicas):
        columns = slice(k * tok_rows, (k + 1) * tok_rows)
        gram_y = lax.dot_general(
            y_ref[...], y_ref[columns, :], CONTRACT_LAST, preferred_element_type=jnp.float32
        )
        pairs = jnp.where(ids_ref[...] == ids_row_ref[:, columns], gram_ref[:, columns] * gram_y, 0.0)
        of_row = jnp.sum(pairs, axis=1, keepdims=True)
        for level in range(levels):
            begin = (k >> level << level) * tok_rows
            end = begin + (tok_rows << level)
            acc[begin:end, :] += jnp.where(lane == level, of_row[begin:end], 0.0)
    for e in range(DOMAINS):
        norms_ref[e : e + 1, :] = jnp.sum(
            jnp.where(ids_ref[...] == e, acc[...], 0.0), axis=0, keepdims=True
        )
    norms_ref[DOMAINS:, :] = jnp.zeros_like(norms_ref[DOMAINS:, :])


def norm_sums(by_dp, row_ids, gram_hidden, parts, replicas, levels):
    total = gram_hidden.shape[0]
    piece = parts[0].shape[1]
    return pl.pallas_call(
        functools.partial(norms_kernel, replicas, levels),
        in_specs=[pl.BlockSpec(memory_space=pltpu.SMEM)]
        + [pl.BlockSpec(memory_space=pltpu.VMEM)] * (3 + len(parts)),
        out_specs=[pl.BlockSpec(memory_space=pltpu.VMEM)] * 2,
        out_shape=[
            pltpu.VMEM((total, DOMAINS * piece), jnp.bfloat16),
            jax.ShapeDtypeStruct((8, 128), jnp.float32),
        ],
        scratch_shapes=[
            pltpu.VMEM((total, piece), jnp.bfloat16),
            pltpu.VMEM((total, 128), jnp.float32),
        ],
        compiler_params=pltpu.CompilerParams(
            vmem_limit_bytes=8 * total * piece + 4 * total * total + 1024 * total * 4 + 8 * 2**20
        ),
        cost_estimate=pl.CostEstimate(
            flops=2 * total * total * piece + 4 * total * total,
            bytes_accessed=4 * total * piece + 4 * total * total,
            transcendentals=0,
        ),
    )(by_dp.reshape(1), row_ids, row_ids.reshape(1, total), gram_hidden, *reversed(parts))


def shards(layer_input_activations, cotangent, domain_ids, norm_gain, w_gate, w_up, w_down):
    segment = lax.axis_index("section")
    dp_index = lax.axis_index("dp")
    segments = lax.axis_size("section")
    tensor_size = lax.axis_size("tensor")
    dp_size = lax.axis_size("dp")
    assert segments == 2
    micro, local_rows, width = layer_input_activations.shape
    gain = norm_gain[0][None, :]
    gate_w, up_w, down_w, gate_t = load_weights(w_gate, w_up, w_down)
    units = down_w.shape[0]
    block = micro * local_rows
    tok_rows = block * tensor_size
    first = segment == 0

    x_own = layer_input_activations.reshape(block, width)
    cot_own = cotangent.reshape(block, width)
    rows_in = jnp.concatenate(gather(jnp.where(first, x_own, cot_own), "tensor"), axis=0)

    def layer_parts(rows):
        widened = rows.astype(jnp.float32)
        scale = lax.rsqrt(jnp.mean(widened * widened, axis=-1, keepdims=True) + EPS)
        normed = (widened * scale * gain).astype(jnp.bfloat16)
        gate = jnp.dot(normed, gate_w, preferred_element_type=jnp.float32)
        up = jnp.dot(normed, up_w, preferred_element_type=jnp.float32)
        return widened, scale, gate, up

    _, _, gate0, up0 = layer_parts(rows_in)
    hidden0 = (jax.nn.silu(gate0) * up0).astype(jnp.bfloat16)
    mixed = jnp.dot(hidden0, down_w, preferred_element_type=jnp.float32).astype(jnp.bfloat16)
    cot_rows, hidden0, mixed = lax.optimization_barrier((rows_in, hidden0, mixed))
    d_hidden = hidden_grad(segment, cot_rows, down_w)
    x1_own, pieces0 = scatter_sum(x_own, mixed, 0, block, hidden0)
    x1_own, d_hidden = lax.optimization_barrier((x1_own, d_hidden))
    head = jnp.pad(hidden0[:block], ((0, 0), (0, width - units)))
    blocks = gather_beside(jnp.where(first, head, x1_own))
    x1 = jnp.concatenate(blocks, axis=0)
    heads = blocks[1 : min(dp_size, tensor_size)]

    widened, scale, gate, up = layer_parts(x1)
    sig = jax.nn.sigmoid(gate)
    hidden1 = (gate * sig * up).astype(jnp.bfloat16)
    d_gate = (d_hidden * up * (sig * (1.0 + gate * (1.0 - sig)))).astype(jnp.bfloat16)
    d_up = (d_hidden * gate * sig).astype(jnp.bfloat16)
    d_normed = normed_grad(segment, d_gate, d_up, gate_t, up_w)
    pulled = d_normed * gain
    along = jnp.sum(pulled * widened, axis=-1, keepdims=True) / width
    term = (pulled * scale - widened * (scale * scale * scale * along)).astype(jnp.bfloat16)
    pieces0 = pieces0[::-1]
    term, pieces0 = lax.optimization_barrier((term, pieces0))
    pieces0 = pieces0[::-1]
    dy_own, pieces1 = scatter_sum(cot_own, term, 1, block, hidden1)
    dy_own = jnp.where(first, dy_own, cot_own)

    piece = width // dp_size
    id_rows = -(-micro // 16) * 16
    id_block = jnp.broadcast_to(
        jnp.pad(domain_ids.astype(jnp.bfloat16), ((0, id_rows - micro), (0, 0))), (id_rows, piece)
    )
    messages = []
    for k in range(dp_size):
        part = lax.dynamic_slice_in_dim(dy_own, (dp_index ^ k) * piece, piece, axis=1)
        part = jnp.concatenate([part, id_block], axis=0)
        messages.append(part if k == 0 else swap(part, "dp", k))
    columns = jnp.concatenate([message[:block] for message in messages], axis=0)
    columns, pieces1[-1] = lax.optimization_barrier((columns, pieces1[-1]))
    if dp_size == tensor_size:
        by_dp = segment
        parts_y = []
        for k in range(dp_size):
            part = lax.dynamic_slice_in_dim(cot_rows, (dp_index ^ k) * piece, piece, axis=1)
            part = jnp.where(first, columns, part)
            parts_y.append(part if k == 0 else exchange(part, k))
    else:
        by_dp = jnp.zeros_like(segment)
        parts_y = gather(columns, "tensor")
    hidden_all, gram_hidden = assemble(segment, pieces0, pieces1, heads)
    ids_all = jnp.stack([message[block : block + micro, 0] for message in messages])
    row_ids = jnp.broadcast_to(
        ids_all.astype(jnp.int32)[:, None, :, None], (dp_size, tensor_size, micro, local_rows)
    ).reshape(dp_size * tok_rows, 1)
    levels = dp_size.bit_length()
    masked, norms = norm_sums(by_dp, row_ids, gram_hidden, parts_y, dp_size, levels)
    rounds = [
        (axis, bit, min(2, bits(axis) - bit))
        for axis in ("tensor", "dp", "section")
        for bit in range(0, bits(axis), 2)
    ]
    tiles = units // TILE
    parts = min(len(rounds), tiles)
    grads = None
    begin = 0
    for part, (axis, bit, count) in enumerate(rounds):
        others = [swap(norms, axis, k << bit) for k in range(1, 1 << count)]
        if part < parts:
            end = tiles * (part + 1) // parts
            grads = domain_gradients(hidden_all, masked, begin, end - begin, grads)
            begin = end
        if count == 2:
            norms = (others[2] + others[1]) + (others[0] + norms)
        else:
            norms = norms + others[0]
        masked, norms = lax.optimization_barrier((masked, norms))
    entries = segments * units * tensor_size * width
    counts = [float((dp_size >> level) * entries) for level in range(levels)]
    return grads[None], norms[:DOMAINS, :levels] / jnp.array(counts, jnp.float32)[None, :]


def solution(mesh):
    return jax.shard_map(
        shards,
        mesh=mesh,
        in_specs=(
            P(None, ("dp", "tensor"), None),
            P(None, ("dp", "tensor"), None),
            P(None, "dp"),
            P("section", None),
            P("section", None, "tensor"),
            P("section", None, "tensor"),
            P("section", "tensor", None),
        ),
        out_specs=(P("section", None, "tensor", "dp"), P()),
        check_vma=False,
    )
```

```python
import functools

import jax
import jax.numpy as jnp
from jax import lax
from jax.experimental import pallas as pl
from jax.experimental.pallas import tpu as pltpu
from jax.sharding import PartitionSpec as P

DOMAINS = 4
TILE = 256
EPS = 1e-05
CONTRACT_LAST = (((1,), (1,)), ((), ()))
CONTRACT_FIRST = (((0,), (0,)), ((), ()))


def swap(block, axis, offset):
    size = lax.axis_size(axis)
    return lax.ppermute(block, axis, [(i, i ^ offset) for i in range(size)])


def swap_in(block, section, axis, offset):
    size = lax.axis_size(axis)
    route = [(section * size + i, section * size + (i ^ offset)) for i in range(size)]
    return lax.ppermute(block, ("section", axis), route)


def across(block, source, offset):
    size = lax.axis_size("tensor")
    route = [
        (source * size + i, (1 - source) * size + (i ^ offset)) for i in range(size)
    ]
    return lax.ppermute(block, ("section", "tensor"), route)


def bits(axis):
    return lax.axis_size(axis).bit_length() - 1


def gather_beside(rows):
    dp_size, tensor_size = lax.axis_size("dp"), lax.axis_size("tensor")

    def route(k):
        beside = (k - 1) % (dp_size - 1) + 1
        pairs = []
        for d in range(dp_size):
            for t in range(tensor_size):
                pairs.append((d * tensor_size + t, (d ^ beside) * tensor_size + t))
                pairs.append(((dp_size + d) * tensor_size + t, (dp_size + d) * tensor_size + (t ^ k)))
        return pairs

    axes = ("section", "dp", "tensor")
    return [rows] + [lax.ppermute(rows, axes, route(k)) for k in range(1, tensor_size)]


def exchange(block, k):
    dp_size, tensor_size = lax.axis_size("dp"), lax.axis_size("tensor")
    pairs = []
    for d in range(dp_size):
        for t in range(tensor_size):
            pairs.append((d * tensor_size + t, d * tensor_size + (t ^ k)))
            pairs.append(((dp_size + d) * tensor_size + t, (dp_size + (d ^ k)) * tensor_size + t))
    return lax.ppermute(block, ("section", "dp", "tensor"), pairs)


def gather(rows, axis):
    return [rows] + [swap(rows, axis, k) for k in range(1, lax.axis_size(axis))]


def scatter_sum(start, terms, source, block, rows):
    arrived = [
        across(terms[k * block : (k + 1) * block], source, k)
        for k in range(lax.axis_size("tensor"))
    ]
    others = []
    if source == 1:
        for k in range(2, lax.axis_size("dp")):
            early, arrived[0] = lax.optimization_barrier((rows, arrived[0]))
            others.append(swap_in(early, source, "dp", k))
    total = start.astype(jnp.float32)
    for value in arrived:
        total = total + value.astype(jnp.float32)
    total = total.astype(jnp.bfloat16)
    late, total = lax.optimization_barrier((rows, total))
    if source == 0:
        short = min(lax.axis_size("dp"), lax.axis_size("tensor"))
        return total, [rows] + [
            swap_in(late[block:] if k < short else late, source, "dp", k)
            for k in range(1, lax.axis_size("dp"))
        ]
    return total, [rows, swap_in(late, source, "dp", 1)] + others


def load_kernel(gate_in, up_in, down_in, gate, up, down, gate_t, sems):
    width = gate.shape[0]
    pieces = [(begin, min(256, width - begin)) for begin in range(0, width, 256)]
    copies = []
    for number, (begin, count) in enumerate(pieces):
        rows = pl.ds(begin, count)
        copies.append(pltpu.make_async_copy(gate_in.at[0, rows], gate.at[rows], sems.at[2 + number]))
    rest = [
        pltpu.make_async_copy(up_in.at[0], up, sems.at[0]),
        pltpu.make_async_copy(down_in.at[0], down, sems.at[1]),
    ]
    for copy in copies + rest:
        copy.start()
    for copy, (begin, count) in zip(copies, pieces):
        copy.wait()
        gate_t[:, begin : begin + count] = gate[begin : begin + count, :].T
    for copy in rest:
        copy.wait()


def load_weights(w_gate, w_up, w_down):
    _, width, units = w_gate.shape
    weights = [pltpu.with_memory_space_constraint(w, pltpu.HBM) for w in (w_gate, w_up, w_down)]
    shapes = [(width, units), (width, units), (units, width), (units, width)]
    return pl.pallas_call(
        load_kernel,
        in_specs=[pl.BlockSpec(memory_space=pltpu.HBM)] * 3,
        out_specs=[pl.BlockSpec(memory_space=pltpu.VMEM)] * 4,
        out_shape=[pltpu.VMEM(shape, jnp.bfloat16) for shape in shapes],
        scratch_shapes=[pltpu.SemaphoreType.DMA((2 + -(-width // 256),))],
        compiler_params=pltpu.CompilerParams(vmem_limit_bytes=4 * 2**20),
        cost_estimate=pl.CostEstimate(
            flops=0, bytes_accessed=6 * width * units, transcendentals=0
        ),
    )(*weights)


def hidden_grad_kernel(flag_ref, rows_ref, down_ref, out_ref):
    units = down_ref.shape[0]

    @pl.when(flag_ref[0] == 1)
    def _():
        for begin in range(0, units, TILE):
            out_ref[:, begin : begin + TILE] = lax.dot_general(
                rows_ref[...],
                down_ref[begin : begin + TILE, :],
                CONTRACT_LAST,
                preferred_element_type=jnp.float32,
            )

    @pl.when(flag_ref[0] == 0)
    def _():
        out_ref[...] = jnp.zeros_like(out_ref)


def hidden_grad(segment, rows, down_w):
    units, width = down_w.shape
    return pl.pallas_call(
        hidden_grad_kernel,
        in_specs=[pl.BlockSpec(memory_space=pltpu.SMEM)]
        + [pl.BlockSpec(memory_space=pltpu.VMEM)] * 2,
        out_specs=pl.BlockSpec(memory_space=pltpu.VMEM),
        out_shape=jax.ShapeDtypeStruct((rows.shape[0], units), jnp.float32),
        compiler_params=pltpu.CompilerParams(vmem_limit_bytes=16 * 2**20),
        cost_estimate=pl.CostEstimate(
            flops=2 * rows.shape[0] * units * width,
            bytes_accessed=2 * units * width,
            transcendentals=0,
        ),
    )(segment.reshape(1), rows, down_w)


def normed_grad_kernel(flag_ref, d_gate_ref, d_up_ref, gate_t_ref, up_ref, out_ref):
    width = out_ref.shape[1]

    @pl.when(flag_ref[0] == 1)
    def _():
        for begin in range(0, width, TILE):
            columns = slice(begin, begin + TILE)
            out_ref[:, columns] = jnp.dot(
                d_gate_ref[...], gate_t_ref[:, columns], preferred_element_type=jnp.float32
            ) + lax.dot_general(
                d_up_ref[...], up_ref[columns, :], CONTRACT_LAST, preferred_element_type=jnp.float32
            )

    @pl.when(flag_ref[0] == 0)
    def _():
        out_ref[...] = jnp.zeros_like(out_ref)


def normed_grad(segment, d_gate, d_up, gate_t, up_w):
    rows, units = d_gate.shape
    width = up_w.shape[0]
    return pl.pallas_call(
        normed_grad_kernel,
        in_specs=[pl.BlockSpec(memory_space=pltpu.SMEM)]
        + [pl.BlockSpec(memory_space=pltpu.VMEM)] * 4,
        out_specs=pl.BlockSpec(memory_space=pltpu.VMEM),
        out_shape=jax.ShapeDtypeStruct((rows, width), jnp.float32),
        compiler_params=pltpu.CompilerParams(vmem_limit_bytes=24 * 2**20),
        cost_estimate=pl.CostEstimate(
            flops=4 * rows * units * width,
            bytes_accessed=4 * units * width,
            transcendentals=0,
        ),
    )(segment.reshape(1), d_gate, d_up, gate_t, up_w)


def gradient_kernel(hidden_ref, masked_ref, *rest):
    out_ref = rest[-1]
    piece = out_ref.shape[2]
    product = lax.dot_general(
        hidden_ref[...], masked_ref[...], CONTRACT_FIRST, preferred_element_type=jnp.float32
    )
    for e in range(DOMAINS):
        out_ref[e] = product[:, e * piece : (e + 1) * piece].astype(jnp.bfloat16)


def domain_gradients(hidden, masked, begin, count, grads=None):
    rows, units = hidden.shape
    columns = masked.shape[1]
    piece = columns // DOMAINS
    in_specs = [
        pl.BlockSpec((rows, TILE), lambda i: (0, begin + i)),
        pl.BlockSpec(memory_space=pltpu.VMEM),
    ]
    operands = [hidden, masked]
    if grads is not None:
        in_specs.append(pl.BlockSpec(memory_space=pl.ANY))
        operands.append(grads)
    return pl.pallas_call(
        gradient_kernel,
        grid=(count,),
        in_specs=in_specs,
        out_specs=pl.BlockSpec((DOMAINS, TILE, piece), lambda i: (0, begin + i, 0)),
        out_shape=jax.ShapeDtypeStruct((DOMAINS, units, piece), jnp.bfloat16),
        input_output_aliases={} if grads is None else {2: 0},
        compiler_params=pltpu.CompilerParams(vmem_limit_bytes=16 * 2**20),
        cost_estimate=pl.CostEstimate(
            flops=2 * rows * count * TILE * columns,
            bytes_accessed=2 * count * TILE * (rows + columns),
            transcendentals=0,
        ),
    )(*operands)


def assemble_kernel(count, flag_ref, *refs):
    heads = len(refs) - 3 - 2 * count
    pieces = (refs[:count][::-1], refs[count : 2 * count])
    firsts = refs[2 * count : 2 * count + heads]
    hidden_ref, gram_ref, sems = refs[2 * count + heads :]
    rows, units = pieces[1][0].shape
    for section in range(2):

        @pl.when(flag_ref[0] == section)
        def _(section=section):
            copies = []
            for k in range(count):
                begin = k * rows
                if section == 0 and 1 <= k <= heads:
                    head = firsts[k - 1]
                    size = head.shape[0]
                    copies.append(
                        pltpu.make_async_copy(
                            head.at[:, pl.ds(0, units)],
                            hidden_ref.at[pl.ds(begin, size)],
                            sems.at[count + k],
                        )
                    )
                    begin += size
                copies.append(
                    pltpu.make_async_copy(
                        pieces[section][k],
                        hidden_ref.at[pl.ds(begin, pieces[section][k].shape[0])],
                        sems.at[k],
                    )
                )
            for copy in copies:
                copy.start()
            for copy in copies:
                copy.wait()

    total = rows * count
    step = min(total, 512)
    for begin in range(0, total, step):
        gram_ref[begin : begin + step, :] = lax.dot_general(
            hidden_ref[begin : begin + step, :],
            hidden_ref[...],
            CONTRACT_LAST,
            preferred_element_type=jnp.float32,
        )


def assemble(segment, pieces0, pieces1, heads):
    count = len(pieces0)
    rows, units = pieces0[0].shape
    total = rows * count
    pieces = [pltpu.with_memory_space_constraint(p, pltpu.HBM) for p in pieces0[::-1] + pieces1 + heads]
    return pl.pallas_call(
        functools.partial(assemble_kernel, count),
        in_specs=[pl.BlockSpec(memory_space=pltpu.SMEM)]
        + [pl.BlockSpec(memory_space=pl.ANY)] * len(pieces),
        out_specs=[pl.BlockSpec(memory_space=pltpu.VMEM)] * 2,
        out_shape=[
            jax.ShapeDtypeStruct((total, units), jnp.bfloat16),
            jax.ShapeDtypeStruct((total, total), jnp.float32),
        ],
        scratch_shapes=[pltpu.SemaphoreType.DMA((2 * count,))],
        compiler_params=pltpu.CompilerParams(
            vmem_limit_bytes=2 * total * units + 4 * total * total + 4 * 2**20
        ),
        cost_estimate=pl.CostEstimate(
            flops=2 * total * total * units,
            bytes_accessed=4 * total * units + 4 * total * total,
            transcendentals=0,
        ),
    )(segment.reshape(1), *pieces)


def norms_kernel(replicas, levels, flag_ref, ids_ref, ids_row_ref, gram_ref, *refs):
    *parts, masked_ref, norms_ref, y_ref, acc = refs
    piece = y_ref.shape[1]
    block = parts[0].shape[0] // replicas
    tok_rows = block * len(parts)

    @pl.when(flag_ref[0] == 0)
    def _():
        for t, part in enumerate(parts):
            for k in range(replicas):
                y_ref[k * tok_rows + t * block : k * tok_rows + (t + 1) * block, :] = part[
                    k * block : (k + 1) * block, :
                ]

    if len(parts) == replicas:

        @pl.when(flag_ref[0] == 1)
        def _():
            for k, part in enumerate(parts):
                y_ref[k * tok_rows : (k + 1) * tok_rows, :] = part[...]

    for e in range(DOMAINS):
        masked_ref[:, e * piece : (e + 1) * piece] = jnp.where(
            ids_ref[...] == e, y_ref[...].astype(jnp.float32), 0.0
        ).astype(jnp.bfloat16)
    acc[...] = jnp.zeros_like(acc)
    lane = lax.broadcasted_iota(jnp.int32, (1, acc.shape[1]), 1)
    for k in range(replicas):
        columns = slice(k * tok_rows, (k + 1) * tok_rows)
        gram_y = lax.dot_general(
            y_ref[...], y_ref[columns, :], CONTRACT_LAST, preferred_element_type=jnp.float32
        )
        pairs = jnp.where(ids_ref[...] == ids_row_ref[:, columns], gram_ref[:, columns] * gram_y, 0.0)
        of_row = jnp.sum(pairs, axis=1, keepdims=True)
        for level in range(levels):
            begin = (k >> level << level) * tok_rows
            end = begin + (tok_rows << level)
            acc[begin:end, :] += jnp.where(lane == level, of_row[begin:end], 0.0)
    for e in range(DOMAINS):
        norms_ref[e : e + 1, :] = jnp.sum(
            jnp.where(ids_ref[...] == e, acc[...], 0.0), axis=0, keepdims=True
        )
    norms_ref[DOMAINS:, :] = jnp.zeros_like(norms_ref[DOMAINS:, :])


def norm_sums(by_dp, row_ids, gram_hidden, parts, replicas, levels):
    total = gram_hidden.shape[0]
    piece = parts[0].shape[1]
    return pl.pallas_call(
        functools.partial(norms_kernel, replicas, levels),
        in_specs=[pl.BlockSpec(memory_space=pltpu.SMEM)]
        + [pl.BlockSpec(memory_space=pltpu.VMEM)] * (3 + len(parts)),
        out_specs=[pl.BlockSpec(memory_space=pltpu.VMEM)] * 2,
        out_shape=[
            pltpu.VMEM((total, DOMAINS * piece), jnp.bfloat16),
            jax.ShapeDtypeStruct((8, 128), jnp.float32),
        ],
        scratch_shapes=[
            pltpu.VMEM((total, piece), jnp.bfloat16),
            pltpu.VMEM((total, 128), jnp.float32),
        ],
        compiler_params=pltpu.CompilerParams(
            vmem_limit_bytes=8 * total * piece + 4 * total * total + 1024 * total * 4 + 8 * 2**20
        ),
        cost_estimate=pl.CostEstimate(
            flops=2 * total * total * piece + 4 * total * total,
            bytes_accessed=4 * total * piece + 4 * total * total,
            transcendentals=0,
        ),
    )(by_dp.reshape(1), row_ids, row_ids.reshape(1, total), gram_hidden, *parts)


def shards(layer_input_activations, cotangent, domain_ids, norm_gain, w_gate, w_up, w_down):
    segment = lax.axis_index("section")
    dp_index = lax.axis_index("dp")
    segments = lax.axis_size("section")
    tensor_size = lax.axis_size("tensor")
    dp_size = lax.axis_size("dp")
    assert segments == 2
    micro, local_rows, width = layer_input_activations.shape
    gain = norm_gain[0][None, :]
    gate_w, up_w, down_w, gate_t = load_weights(w_gate, w_up, w_down)
    units = down_w.shape[0]
    block = micro * local_rows
    tok_rows = block * tensor_size
    first = segment == 0

    x_own = layer_input_activations.reshape(block, width)
    cot_own = cotangent.reshape(block, width)
    rows_in = jnp.concatenate(gather(jnp.where(first, x_own, cot_own), "tensor"), axis=0)

    def layer_parts(rows):
        widened = rows.astype(jnp.float32)
        scale = lax.rsqrt(jnp.mean(widened * widened, axis=-1, keepdims=True) + EPS)
        normed = (widened * scale * gain).astype(jnp.bfloat16)
        gate = jnp.dot(normed, gate_w, preferred_element_type=jnp.float32)
        up = jnp.dot(normed, up_w, preferred_element_type=jnp.float32)
        return widened, scale, gate, up

    _, _, gate0, up0 = layer_parts(rows_in)
    hidden0 = (jax.nn.silu(gate0) * up0).astype(jnp.bfloat16)
    mixed = jnp.dot(hidden0, down_w, preferred_element_type=jnp.float32).astype(jnp.bfloat16)
    cot_rows, hidden0, mixed = lax.optimization_barrier((rows_in, hidden0, mixed))
    d_hidden = hidden_grad(segment, cot_rows, down_w)
    x1_own, pieces0 = scatter_sum(x_own, mixed, 0, block, hidden0)
    x1_own, d_hidden = lax.optimization_barrier((x1_own, d_hidden))
    head = jnp.pad(hidden0[:block], ((0, 0), (0, width - units)))
    blocks = gather_beside(jnp.where(first, head, x1_own))
    x1 = jnp.concatenate(blocks, axis=0)
    heads = blocks[1 : min(dp_size, tensor_size)]

    widened, scale, gate, up = layer_parts(x1)
    sig = jax.nn.sigmoid(gate)
    hidden1 = (gate * sig * up).astype(jnp.bfloat16)
    d_gate = (d_hidden * up * (sig * (1.0 + gate * (1.0 - sig)))).astype(jnp.bfloat16)
    d_up = (d_hidden * gate * sig).astype(jnp.bfloat16)
    d_normed = normed_grad(segment, d_gate, d_up, gate_t, up_w)
    pulled = d_normed * gain
    along = jnp.sum(pulled * widened, axis=-1, keepdims=True) / width
    term = (pulled * scale - widened * (scale * scale * scale * along)).astype(jnp.bfloat16)
    pieces0 = pieces0[::-1]
    term, pieces0 = lax.optimization_barrier((term, pieces0))
    pieces0 = pieces0[::-1]
    dy_own, pieces1 = scatter_sum(cot_own, term, 1, block, hidden1)
    dy_own = jnp.where(first, dy_own, cot_own)

    piece = width // dp_size
    id_rows = -(-micro // 16) * 16
    id_block = jnp.broadcast_to(
        jnp.pad(domain_ids.astype(jnp.bfloat16), ((0, id_rows - micro), (0, 0))), (id_rows, piece)
    )
    messages = []
    for k in range(dp_size):
        part = lax.dynamic_slice_in_dim(dy_own, (dp_index ^ k) * piece, piece, axis=1)
        part = jnp.concatenate([part, id_block], axis=0)
        messages.append(part if k == 0 else swap(part, "dp", k))
    columns = jnp.concatenate([message[:block] for message in messages], axis=0)
    columns, pieces1[-1] = lax.optimization_barrier((columns, pieces1[-1]))
    if dp_size == tensor_size:
        by_dp = segment
        parts_y = []
        for k in range(dp_size):
            part = lax.dynamic_slice_in_dim(cot_rows, (dp_index ^ k) * piece, piece, axis=1)
            part = jnp.where(first, columns, part)
            parts_y.append(part if k == 0 else exchange(part, k))
    else:
        by_dp = jnp.zeros_like(segment)
        parts_y = gather(columns, "tensor")
    hidden_all, gram_hidden = assemble(segment, pieces0, pieces1, heads)
    ids_all = jnp.stack([message[block : block + micro, 0] for message in messages])
    row_ids = jnp.broadcast_to(
        ids_all.astype(jnp.int32)[:, None, :, None], (dp_size, tensor_size, micro, local_rows)
    ).reshape(dp_size * tok_rows, 1)
    levels = dp_size.bit_length()
    masked, norms = norm_sums(by_dp, row_ids, gram_hidden, parts_y, dp_size, levels)
    rounds = [
        (axis, bit, min(2, bits(axis) - bit))
        for axis in ("tensor", "dp", "section")
        for bit in range(0, bits(axis), 2)
    ]
    tiles = units // TILE
    parts = min(len(rounds), tiles)
    grads = None
    begin = 0
    for part, (axis, bit, count) in enumerate(rounds):
        others = [swap(norms, axis, k << bit) for k in range(1, 1 << count)]
        if part < parts:
            end = tiles * (part + 1) // parts
            grads = domain_gradients(hidden_all, masked, begin, end - begin, grads)
            begin = end
        if count == 2:
            norms = (others[2] + others[1]) + (others[0] + norms)
        else:
            norms = norms + others[0]
        masked, norms = lax.optimization_barrier((masked, norms))
    entries = segments * units * tensor_size * width
    counts = [float((dp_size >> level) * entries) for level in range(levels)]
    return grads[None], norms[:DOMAINS, :levels] / jnp.array(counts, jnp.float32)[None, :]


def solution(mesh):
    return jax.shard_map(
        shards,
        mesh=mesh,
        in_specs=(
            P(None, ("dp", "tensor"), None),
            P(None, ("dp", "tensor"), None),
            P(None, "dp"),
            P("section", None),
            P("section", None, "tensor"),
            P("section", None, "tensor"),
            P("section", "tensor", None),
        ),
        out_specs=(P("section", None, "tensor", "dp"), P()),
        check_vma=False,
    )
```
